32 devices in a mesh: batch: 4 (over y, x), blk: 8 (over z, core).
Axes of the slice: x: 2, y: 2, z: 4, core: 2. Of those that a mesh axis runs over, the one named last changes fastest.
Arguments:
- clean_latents: float32 [4, 4096, 16], P('batch', 'blk'), may hold values from -6 to 6
- noise_sample: float32 [4, 4096, 16], P('batch', 'blk'), may hold values from -6 to 6
- noise_levels: int32 [4, 16], replicated, may hold values from 0 to 31
- clean_flags: int32 [4, 16], replicated, may hold values 0 or 1
- span_frame: int32 [16], replicated, may hold values from 0 to 15, as said below
- patch_master: float32 [16, 1024], P(None, ('batch', 'blk')), may hold values from -1.5 to 1.5
- patch_first: float32 [16, 1024], P(None, ('batch', 'blk')), may hold values from -7.6293945e-06 to 7.6293945e-06
- patch_second: float32 [16, 1024], P(None, ('batch', 'blk')), may hold values from 2.111829e-14 to 8.447316e-14
- level_master: float32 [33, 1024], P(None, ('batch', 'blk')), may hold values from -5 to 5
- level_first: float32 [33, 1024], P(None, ('batch', 'blk')), may hold values from -7.6293945e-06 to 7.6293945e-06
- level_second: float32 [33, 1024], P(None, ('batch', 'blk')), may hold values from 2.111829e-14 to 8.447316e-14
- adaptive_master: float32 [1024, 6144], P(('batch', 'blk')), may hold values from -0.1875 to 0.1875
- adaptive_first: float32 [1024, 6144], P(('batch', 'blk')), may hold values from -7.6293945e-06 to 7.6293945e-06
- adaptive_second: float32 [1024, 6144], P(('batch', 'blk')), may hold values from 2.111829e-14 to 8.447316e-14
- triple_master: float32 [1024, 3072], P(('batch', 'blk')), may hold values from -0.1875 to 0.1875
- triple_first: float32 [1024, 3072], P(('batch', 'blk')), may hold values from -7.6293945e-06 to 7.6293945e-06
- triple_second: float32 [1024, 3072], P(('batch', 'blk')), may hold values from 2.111829e-14 to 8.447316e-14
- project_master: float32 [1024, 1024], P(('batch', 'blk')), may hold values from -1.5 to 1.5
- project_first: float32 [1024, 1024], P(('batch', 'blk')), may hold values from -7.6293945e-06 to 7.6293945e-06
- project_second: float32 [1024, 1024], P(('batch', 'blk')), may hold values from 2.111829e-14 to 8.447316e-14
- expand_master: float32 [1024, 4096], P(('batch', 'blk')), may hold values from -0.1875 to 0.1875
- expand_first: float32 [1024, 4096], P(('batch', 'blk')), may hold values from -7.6293945e-06 to 7.6293945e-06
- expand_second: float32 [1024, 4096], P(('batch', 'blk')), may hold values from 2.111829e-14 to 8.447316e-14
- reduce_master: float32 [4096, 1024], P(('batch', 'blk')), may hold values from -0.09375 to 0.09375
- reduce_first: float32 [4096, 1024], P(('batch', 'blk')), may hold values from -7.6293945e-06 to 7.6293945e-06
- reduce_second: float32 [4096, 1024], P(('batch', 'blk')), may hold values from 2.111829e-14 to 8.447316e-14
- readout_master: float32 [1024, 16], P(('batch', 'blk')), may hold values from -0.1875 to 0.1875
- readout_first: float32 [1024, 16], P(('batch', 'blk')), may hold values from -7.6293945e-06 to 7.6293945e-06
- readout_second: float32 [1024, 16], P(('batch', 'blk')), may hold values from 2.111829e-14 to 8.447316e-14
Outputs:
- loss_sum: float32 [], replicated
- frame_count: float32 [], replicated
- bucket_sums: float32 [32], replicated
- clip_norm: float32 [], replicated
- patch_first_next: float32 [16, 1024], P(None, ('batch', 'blk'))
- patch_second_next: float32 [16, 1024], P(None, ('batch', 'blk'))
- patch_master_next: float32 [16, 1024], P(None, ('batch', 'blk'))
- level_first_next: float32 [33, 1024], P(None, ('batch', 'blk'))
- level_second_next: float32 [33, 1024], P(None, ('batch', 'blk'))
- level_master_next: float32 [33, 1024], P(None, ('batch', 'blk'))
- adaptive_first_next: float32 [1024, 6144], P(('batch', 'blk'))
- adaptive_second_next: float32 [1024, 6144], P(('batch', 'blk'))
- adaptive_master_next: float32 [1024, 6144], P(('batch', 'blk'))
- triple_first_next: float32 [1024, 3072], P(('batch', 'blk'))
- triple_second_next: float32 [1024, 3072], P(('batch', 'blk'))
- triple_master_next: float32 [1024, 3072], P(('batch', 'blk'))
- project_first_next: float32 [1024, 1024], P(('batch', 'blk'))
- project_second_next: float32 [1024, 1024], P(('batch', 'blk'))
- project_master_next: float32 [1024, 1024], P(('batch', 'blk'))
- expand_first_next: float32 [1024, 4096], P(('batch', 'blk'))
- expand_second_next: float32 [1024, 4096], P(('batch', 'blk'))
- expand_master_next: float32 [1024, 4096], P(('batch', 'blk'))
- reduce_first_next: float32 [4096, 1024], P(('batch', 'blk'))
- reduce_second_next: float32 [4096, 1024], P(('batch', 'blk'))
- reduce_master_next: float32 [4096, 1024], P(('batch', 'blk'))
- readout_first_next: float32 [1024, 16], P(('batch', 'blk'))
- readout_second_next: float32 [1024, 16], P(('batch', 'blk'))
- readout_master_next: float32 [1024, 16], P(('batch', 'blk'))
The draws below stay inside these ranges and needn't reach their ends.
Inputs may be any that keep to these rules, and one draw needn't show every extreme that they name: `span_frame`: each of the 16 time indices appears once; the stored frames form groups of 2 in a row, and group i holds, one in each half of it, the time indices i * 1 to (i + 1) * 1 - 1 and their mirror images 16 - 1 - t.
All inputs are finite; a program needn't handle non-finite values.
Results may differ from the reference program's by a relative error of at most 0.008.
The reference program's roundings to bfloat16 on the way (of `weights`, `inputs`, `normed` and `attended`) count: a program that leaves them out, or rounds other values in their place, can miss the bound.
Values may be sent and summed in bfloat16 or wider, within the bound.
No kernel may reach another device: no remote copies, remote signals or barrier semaphores. Data moves between devices by JAX's collectives and lax.ppermute only.
A program may use at most 256 MiB of HBM per device.

```python
import math
import jax
import jax.numpy as jnp
import numpy as np
from jax import lax

D = 1024
HEADS = 16
HEAD_DIM = 64
FF = 4096
PATCH_FEAT = 16
FRAME_TOK = 256
SIDE = 16
NB = 32
STEP = 10
FR_DEV = 2
LEVELS = 33
FRAMES = 16
TOKENS = 4096
CLIPS = 4
NPARAM = 18940928


def draw_span_frame(key, part):
    key = jax.random.fold_in(key, 7)
    half_count = FR_DEV // 2
    group_count = FRAMES // FR_DEV
    groups = jnp.arange(group_count, dtype=jnp.int32)
    lower_key, upper_key, order_key = jax.random.split(key, 3)
    lower_within = jax.vmap(lambda sub_key: jax.random.permutation(sub_key, half_count))(jax.random.split(lower_key, group_count)).astype(jnp.int32)
    upper_within = jax.vmap(lambda sub_key: jax.random.permutation(sub_key, half_count))(jax.random.split(upper_key, group_count)).astype(jnp.int32)
    lower_times = groups[:, None] * half_count + lower_within
    upper_times = (2 * group_count - 1 - groups)[:, None] * half_count + upper_within
    flipped = jax.random.randint(order_key, (group_count, 1), 0, 2)
    leading = jnp.where(flipped == 1, upper_times, lower_times)
    trailing = jnp.where(flipped == 1, lower_times, upper_times)
    return jnp.concatenate([leading, trailing], axis=1).reshape(FRAMES).astype(jnp.int32)


def plant(result, key, least, top_value):
    longest = result.shape.index(max(result.shape))
    spots = []
    for shift in (0, 1):
        where = [jax.random.randint(jax.random.fold_in(key, axis), (), 0, length) for axis, length in enumerate(result.shape)]
        where[longest] = (where[longest] + shift) % result.shape[longest]
        spots.append(tuple(where))
    return result.at[spots[0]].set(least).at[spots[1]].set(top_value)


def steps_of(rng, shape, cuts, least, largest):
    def one(dim, shards_of):
        draws = jax.random.uniform(jax.random.fold_in(jax.random.fold_in(rng, 6), dim), (shards_of,), jnp.float32, least / len(cuts), largest / len(cuts))
        return jnp.repeat(jnp.exp(draws), shape[dim] // shards_of).reshape((-1,) + (1,) * (len(shape) - dim - 1))

    gain = one(*cuts[0])
    for cut in cuts[1:]:
        gain = gain * one(*cut)
    return gain


def cumulative_ranks(amount, slope):
    loads = [(1 << 20) // math.isqrt(grade ** slope) + 1 for grade in range(1, amount + 1)]
    spread = 1 + sum(loads) // (1 << 30)
    return np.cumsum(np.array([max(1, weight // spread) for weight in loads]))


def ranked(key, dims, amount, slope):
    listing = cumulative_ranks(amount, slope)
    pick = jax.random.randint(jax.random.fold_in(key, 1), dims, 0, int(listing[amount - 1]))
    grade = jnp.searchsorted(jnp.asarray(listing, jnp.int32), pick, side="right")
    return jax.random.permutation(jax.random.fold_in(key, 2), amount)[grade].astype(jnp.int32)


def normal_values(key, extent, width, limit, cuts=(), held_as=jnp.bfloat16):
    drawn = width * jax.random.normal(key, extent, jnp.float32)
    if cuts:
        drawn = drawn * steps_of(key, extent, cuts, -0.22, 0.18)
    return jnp.clip(drawn, -limit, limit).astype(held_as)


def setup_inputs(seed: int = 0) -> dict:
    keys = jax.random.split(jax.random.key(seed), 30)
    return {
        "clean_latents": normal_values(keys[0], (CLIPS, TOKENS, PATCH_FEAT), 1.0, 6.0, ((0, 4), (1, 8)), jnp.float32),
        "noise_sample": normal_values(keys[1], (CLIPS, TOKENS, PATCH_FEAT), 1.0, 6.0, ((0, 4), (1, 8)), jnp.float32),
        "noise_levels": plant(ranked(keys[2], (CLIPS, FRAMES), NB, 2), jax.random.fold_in(keys[2], 3), 0, NB - 1).astype(jnp.int32),
        "clean_flags": plant((jax.random.randint(keys[3], (CLIPS, FRAMES), 0, 4) < 1).astype(jnp.int32), jax.random.fold_in(keys[3], 1), 0, 1),
        "span_frame": draw_span_frame(jax.random.fold_in(keys[29], 71), 0),
        "patch_master": normal_values(keys[5], (PATCH_FEAT, D), PATCH_FEAT ** -0.5, 1.5, ((1, 32),), jnp.float32),
        "patch_first": normal_values(keys[6], (PATCH_FEAT, D), (0.00222 * NPARAM ** (-0.5)), 7.62939453125e-06, ((1, 32),), jnp.float32),
        "patch_second": jnp.clip(jnp.exp(math.log(8.447315926179283e-14) - 1.3862944 * jax.random.uniform(keys[7], (PATCH_FEAT, D), jnp.float32) ** steps_of(keys[7], (PATCH_FEAT, D), ((1, 32),), -0.2, 0.2)), 2.1118289815448207e-14, 8.447315926179283e-14),
        "level_master": normal_values(keys[8], (LEVELS, D), 1.0, 5.0, ((1, 32),), jnp.float32),
        "level_first": normal_values(keys[9], (LEVELS, D), (0.00222 * NPARAM ** (-0.5)), 7.62939453125e-06, ((1, 32),), jnp.float32),
        "level_second": jnp.clip(jnp.exp(math.log(8.447315926179283e-14) - 1.3862944 * jax.random.uniform(keys[10], (LEVELS, D), jnp.float32) ** steps_of(keys[10], (LEVELS, D), ((1, 32),), -0.2, 0.2)), 2.1118289815448207e-14, 8.447315926179283e-14),
        "adaptive_master": normal_values(keys[11], (D, 6 * D), D ** -0.5, 0.1875, ((0, 32),), jnp.float32),
        "adaptive_first": normal_values(keys[12], (D, 6 * D), (0.00222 * NPARAM ** (-0.5)), 7.62939453125e-06, ((0, 32),), jnp.float32),
        "adaptive_second": jnp.clip(jnp.exp(math.log(8.447315926179283e-14) - 1.3862944 * jax.random.uniform(keys[13], (D, 6 * D), jnp.float32) ** steps_of(keys[13], (D, 6 * D), ((0, 32),), -0.2, 0.2)), 2.1118289815448207e-14, 8.447315926179283e-14),
        "triple_master": normal_values(keys[14], (D, 3 * D), D ** -0.5, 0.1875, ((0, 32),), jnp.float32),
        "triple_first": normal_values(keys[15], (D, 3 * D), (0.00222 * NPARAM ** (-0.5)), 7.62939453125e-06, ((0, 32),), jnp.float32),
        "triple_second": jnp.clip(jnp.exp(math.log(8.447315926179283e-14) - 1.3862944 * jax.random.uniform(keys[16], (D, 3 * D), jnp.float32) ** steps_of(keys[16], (D, 3 * D), ((0, 32),), -0.2, 0.2)), 2.1118289815448207e-14, 8.447315926179283e-14),
        "project_master": normal_values(keys[17], (D, D), 16 ** -0.5, 1.5, ((0, 32),), jnp.float32),
        "project_first": normal_values(keys[18], (D, D), (0.00222 * NPARAM ** (-0.5)), 7.62939453125e-06, ((0, 32),), jnp.float32),
        "project_second": jnp.clip(jnp.exp(math.log(8.447315926179283e-14) - 1.3862944 * jax.random.uniform(keys[19], (D, D), jnp.float32) ** steps_of(keys[19], (D, D), ((0, 32),), -0.2, 0.2)), 2.1118289815448207e-14, 8.447315926179283e-14),
        "expand_master": normal_values(keys[20], (D, FF), D ** -0.5, 0.1875, ((0, 32),), jnp.float32),
        "expand_first": normal_values(keys[21], (D, FF), (0.00222 * NPARAM ** (-0.5)), 7.62939453125e-06, ((0, 32),), jnp.float32),
        "expand_second": jnp.clip(jnp.exp(math.log(8.447315926179283e-14) - 1.3862944 * jax.random.uniform(keys[22], (D, FF), jnp.float32) ** steps_of(keys[22], (D, FF), ((0, 32),), -0.2, 0.2)), 2.1118289815448207e-14, 8.447315926179283e-14),
        "reduce_master": normal_values(keys[23], (FF, D), FF ** -0.5, 0.09375, ((0, 32),), jnp.float32),
        "reduce_first": normal_values(keys[24], (FF, D), (0.00222 * NPARAM ** (-0.5)), 7.62939453125e-06, ((0, 32),), jnp.float32),
        "reduce_second": jnp.clip(jnp.exp(math.log(8.447315926179283e-14) - 1.3862944 * jax.random.uniform(keys[25], (FF, D), jnp.float32) ** steps_of(keys[25], (FF, D), ((0, 32),), -0.2, 0.2)), 2.1118289815448207e-14, 8.447315926179283e-14),
        "readout_master": normal_values(keys[26], (D, PATCH_FEAT), D ** -0.5, 0.1875, ((0, 32),), jnp.float32),
        "readout_first": normal_values(keys[27], (D, PATCH_FEAT), (0.00222 * NPARAM ** (-0.5)), 7.62939453125e-06, ((0, 32),), jnp.float32),
        "readout_second": jnp.clip(jnp.exp(math.log(8.447315926179283e-14) - 1.3862944 * jax.random.uniform(keys[28], (D, PATCH_FEAT), jnp.float32) ** steps_of(keys[28], (D, PATCH_FEAT), ((0, 32),), -0.2, 0.2)), 2.1118289815448207e-14, 8.447315926179283e-14),
    }


@jax.custom_vjp
def low(v):
    return lax.optimization_barrier(v.astype(jnp.bfloat16)).astype(jnp.float32)

@jax.custom_vjp
def low_back(v):
    return v

def low_keep(v):
    return (low(v), None)

def low_pass(kept, grad):
    return (grad,)

def back_keep(v):
    return (v, None)

def back_low(kept, grad):
    return (low(grad),)
low.defvjp(low_keep, low_pass)
low_back.defvjp(back_keep, back_low)
learn_rates = (0.5, 2.0, 0.05, 0.05, 0.5, 0.05, 0.05, 0.05)
beta_first = 0.9
beta_second = 0.999
decay_rate = 0.01
adam_floor = 1e-08
clip_bound = 0.02

def matmul(left, right):
    return jnp.dot(left, right, precision=lax.Precision.HIGHEST)

def plan(levels, clean_flags):
    alpha_bar = jnp.cos(0.5 * math.pi * (levels.astype(jnp.float32) + 1.0) / (NB + 1.0)) ** 2
    noised = (1 - clean_flags).astype(jnp.float32)
    table_index = jnp.where(clean_flags == 1, 0, levels + 1).astype(jnp.int32)
    return (alpha_bar, noised, table_index)

def noised_input(clean_tok, noise_tok, alpha_bar, noised):
    frame_shape = (alpha_bar.shape[0], -1, clean_tok.shape[-1])
    clean_frames = clean_tok.reshape(frame_shape)
    noise_frames = noise_tok.reshape(frame_shape)
    mixed_tok = jnp.sqrt(alpha_bar)[:, None, None] * clean_frames + jnp.sqrt(1.0 - alpha_bar)[:, None, None] * noise_frames
    return jnp.where(noised[:, None, None] > 0.5, mixed_tok, clean_frames).reshape(clean_tok.shape)

def rotary(frame_ids, token_count):
    in_frame = jnp.arange(token_count, dtype=jnp.int32) % FRAME_TOK
    row_pos = (in_frame // SIDE).astype(jnp.float32)
    col_pos = (in_frame % SIDE).astype(jnp.float32)
    frame_pos = jnp.repeat(frame_ids, FRAME_TOK, total_repeat_length=token_count).astype(jnp.float32)
    time_count = HEAD_DIM // 8
    space_count = 3 * HEAD_DIM // 16
    time_freq = 10000.0 ** (-jnp.arange(time_count, dtype=jnp.float32) / time_count)
    space_freq = 100.0 ** (-jnp.arange(space_count, dtype=jnp.float32) / space_count)
    angles = jnp.concatenate([frame_pos[:, None] * time_freq, row_pos[:, None] * space_freq, col_pos[:, None] * space_freq], axis=1)
    return (jnp.cos(angles), jnp.sin(angles))

def rotate(values, cosine_table, sine_table):
    half_dim = values.shape[-1] // 2
    first_half, second_half = (values[..., :half_dim], values[..., half_dim:])
    cosine_part, sine_part = (cosine_table[:, None, :], sine_table[:, None, :])
    return jnp.concatenate([first_half * cosine_part - second_half * sine_part, second_half * cosine_part + first_half * sine_part], axis=-1)

def layer_norm(hidden):
    centred = hidden - lax.optimization_barrier(jnp.mean(hidden, axis=-1, keepdims=True))
    variance = lax.optimization_barrier(jnp.mean(centred * centred, axis=-1, keepdims=True))
    return centred * lax.rsqrt(variance + 1e-06)

def modulate(hidden, shift, scale):
    normed = layer_norm(hidden).reshape(shift.shape[0], -1, hidden.shape[-1])
    return (normed * (1.0 + scale[:, None]) + shift[:, None]).reshape(hidden.shape)

def per_frame(gate, hidden):
    return (hidden.reshape(gate.shape[0], -1, hidden.shape[-1]) * gate[:, None]).reshape(hidden.shape)

def attention(queries, key_block, values, token_frame):
    row_count = min(512, queries.shape[0])
    block_count = queries.shape[0] // row_count

    def one_block(pieces):
        query_part, query_frame = pieces
        scores = jnp.einsum('qhd,khd->hqk', query_part, key_block, precision=lax.Precision.HIGHEST) * HEAD_DIM ** (-0.5)
        scores = low_back(scores)
        allowed = query_frame[None, :, None] >= token_frame[None, None, :]
        scores = jnp.where(allowed, scores, -1e+30)
        chances = low(jax.nn.softmax(scores, axis=-1))
        return jnp.einsum('hqk,khd->qhd', chances, values, precision=lax.Precision.HIGHEST)
    attended = lax.map(jax.checkpoint(one_block), (queries.reshape(block_count, row_count, HEADS, HEAD_DIM), token_frame.reshape(block_count, row_count)))
    return attended.reshape(queries.shape)

def clip_loss(weights, clean_tok, noise_tok, levels, clean_flags, span_frame):
    patch_weight, table_weight, adapt_weight, triple_weight, project_weight, expand_weight, reduce_weight, readout_weight = weights
    alpha_bar, noised, table_index = plan(levels, clean_flags)
    token_count = clean_tok.shape[0]
    inputs = low(noised_input(clean_tok, noise_tok, alpha_bar, noised))
    cond = low(jax.nn.silu(table_weight[table_index]))
    adapt = low_back(matmul(cond, adapt_weight))
    shift_one, scale_one, gate_one, shift_two, scale_two, gate_two = jnp.split(adapt, 6, axis=1)
    hidden_zero = low_back(matmul(inputs, patch_weight))
    normed = low(modulate(hidden_zero, shift_one, scale_one))
    triple = low_back(matmul(normed, triple_weight)).reshape(token_count, 3, HEADS, HEAD_DIM)
    cosine_table, sine_table = rotary(span_frame, token_count)
    queries = low(rotate(triple[:, 0], cosine_table, sine_table))
    key_block = low(rotate(triple[:, 1], cosine_table, sine_table))
    values = low(triple[:, 2])
    token_frame = jnp.repeat(span_frame, FRAME_TOK, total_repeat_length=token_count)
    attended = low_back(low(attention(queries, key_block, values, token_frame))).reshape(token_count, D)
    branch = low_back(matmul(attended, project_weight))
    hidden_one = hidden_zero + per_frame(gate_one, branch)
    mixed_tok = low(modulate(hidden_one, shift_two, scale_two))
    inner = low_back(matmul(mixed_tok, expand_weight))
    active = low(jax.nn.gelu(inner, approximate=True))
    outer = low_back(matmul(active, reduce_weight))
    hidden_two = hidden_one + per_frame(gate_two, outer)
    final = low(layer_norm(hidden_two))
    predicted = low_back(matmul(final, readout_weight))
    squared = (predicted - noise_tok) ** 2
    return lax.optimization_barrier(jnp.mean(squared.reshape(alpha_bar.shape[0], -1), axis=1)) * noised

def total_loss(weights, clean_latents, noise_sample, noise_levels, clean_flags, span_frame):
    lowered = tuple((low(weight) for weight in weights))
    frame_loss = lax.map(lambda item: clip_loss(lowered, item[0], item[1], item[2], item[3], span_frame), (clean_latents, noise_sample, noise_levels, clean_flags))
    loss_sum = jnp.sum(frame_loss)
    frame_count = jnp.sum((1 - clean_flags).astype(jnp.float32))
    return (loss_sum / jnp.maximum(frame_count, 1.0), (loss_sum, frame_count, frame_loss))

def adamw_update(master, first_moment, second_moment, gradient, factor, step_rate):
    clipped = gradient * factor
    first_new = beta_first * first_moment + (1.0 - beta_first) * clipped
    second_new = beta_second * second_moment + (1.0 - beta_second) * clipped * clipped
    first_hat = first_new / (1.0 - beta_first ** STEP)
    second_hat = second_new / (1.0 - beta_second ** STEP)
    master_new = master - step_rate * (first_hat / (jnp.sqrt(second_hat) + adam_floor) + decay_rate * master)
    return (first_new, second_new, master_new)

def reference(clean_latents, noise_sample, noise_levels, clean_flags, span_frame, patch_master, patch_first, patch_second, level_master, level_first, level_second, adaptive_master, adaptive_first, adaptive_second, triple_master, triple_first, triple_second, project_master, project_first, project_second, expand_master, expand_first, expand_second, reduce_master, reduce_first, reduce_second, readout_master, readout_first, readout_second):
    masters = (patch_master, level_master, adaptive_master, triple_master, project_master, expand_master, reduce_master, readout_master)
    firsts = (patch_first, level_first, adaptive_first, triple_first, project_first, expand_first, reduce_first, readout_first)
    seconds = (patch_second, level_second, adaptive_second, triple_second, project_second, expand_second, reduce_second, readout_second)

    def objective(*weights):
        return total_loss(weights, clean_latents, noise_sample, noise_levels, clean_flags, span_frame)
    loss_value, pull_back, extras = jax.vjp(objective, *masters, has_aux=True)
    gradients = pull_back(jnp.ones_like(loss_value))
    loss_sum, frame_count, frame_loss = extras
    squares = sum((jnp.sum(gradient * gradient) for gradient in gradients))
    clip_norm = jnp.sqrt(squares)
    factor = jnp.minimum(1.0, clip_bound / clip_norm)
    level_hits = (noise_levels[..., None] == jnp.arange(NB, dtype=jnp.int32)).astype(jnp.float32)
    bucket_sums = lax.optimization_barrier(jnp.sum(level_hits * frame_loss[..., None], axis=(0, 1)))
    new = [adamw_update(masters[item], firsts[item], seconds[item], gradients[item], factor, learn_rates[item]) for item in range(8)]
    return (loss_sum, frame_count, bucket_sums, clip_norm, new[0][0], new[0][1], new[0][2], new[1][0], new[1][1], new[1][2], new[2][0], new[2][1], new[2][2], new[3][0], new[3][1], new[3][2], new[4][0], new[4][1], new[4][2], new[5][0], new[5][1], new[5][2], new[6][0], new[6][1], new[6][2], new[7][0], new[7][1], new[7][2])
```

```python
import functools
import math

import jax
import jax.numpy as jnp
from jax import lax
from jax.experimental import pallas as pl
from jax.experimental.pallas import tpu as pltpu
from jax.sharding import Mesh
from jax.sharding import PartitionSpec as P

D = 1024
HEADS = 16
HEAD_DIM = 64
FF = 4096
PATCH_FEAT = 16
FRAME_TOK = 256
SIDE = 16
NB = 32
STEP = 10
LANES = 128
ALL = ("batch", "row", "core")


learn_rates = (0.5, 2.0, 0.05, 0.05, 0.5, 0.05, 0.05, 0.05)
beta_first = 0.9
beta_second = 0.999
decay_rate = 0.01
adam_floor = 1e-08
clip_bound = 0.02
low_type = jnp.bfloat16


def product(left, right):
    return jnp.dot(left, right, preferred_element_type=jnp.float32)


def across(left, right):
    return lax.dot_general(
        left, right, (((0,), (0,)), ((), ())), preferred_element_type=jnp.float32
    )


def against(left, right):
    return lax.dot_general(
        left, right, (((1,), (1,)), ((), ())), preferred_element_type=jnp.float32
    )


def plan(levels, clean_flags):
    alpha_bar = jnp.cos(0.5 * math.pi * (levels.astype(jnp.float32) + 1.0) / (NB + 1.0)) ** 2
    noised = (1 - clean_flags).astype(jnp.float32)
    table_index = jnp.where(clean_flags == 1, 0, levels + 1)
    return (alpha_bar, noised, table_index)


def noised_input(clean_tok, noise_tok, alpha_bar, noised):
    frame_shape = (alpha_bar.shape[0], -1, clean_tok.shape[-1])
    clean_frames = clean_tok.reshape(frame_shape)
    noise_frames = noise_tok.reshape(frame_shape)
    mixed_tok = (
        jnp.sqrt(alpha_bar)[:, None, None] * clean_frames
        + jnp.sqrt(1.0 - alpha_bar)[:, None, None] * noise_frames
    )
    return jnp.where(noised[:, None, None] > 0.5, mixed_tok, clean_frames).reshape(clean_tok.shape)


def layer_norm(hidden):
    centred = hidden - jnp.mean(hidden, axis=-1, keepdims=True)
    variance = jnp.mean(centred * centred, axis=-1, keepdims=True)
    return centred * lax.rsqrt(variance + 1e-06)


def modulate(hidden, shift, scale):
    normed = layer_norm(hidden).reshape(shift.shape[0], -1, hidden.shape[-1])
    return (normed * (1.0 + scale[:, None]) + shift[:, None]).reshape(hidden.shape)


def per_frame(gate, hidden):
    return (hidden.reshape(gate.shape[0], -1, hidden.shape[-1]) * gate[:, None]).reshape(
        hidden.shape
    )


def frame_sum(gate, hidden):
    return jnp.sum(hidden.reshape(gate.shape[0], -1, hidden.shape[-1]), axis=1)


def gelu_tanh(value):
    return jax.nn.gelu(value, approximate=True)


def adamw_update(master, first_moment, second_moment, gradient, factor, step_rate):
    clipped = gradient * factor
    first_new = beta_first * first_moment + (1.0 - beta_first) * clipped
    second_new = beta_second * second_moment + (1.0 - beta_second) * clipped * clipped
    first_hat = first_new / (1.0 - beta_first**STEP)
    second_hat = second_new / (1.0 - beta_second**STEP)
    master_new = master - step_rate * (
        first_hat / (jnp.sqrt(second_hat) + adam_floor) + decay_rate * master
    )
    return (first_new, second_new, master_new)


def lane_places():
    lane = jnp.arange(LANES, dtype=jnp.int32) % HEAD_DIM
    half = HEAD_DIM // 2
    place = lane % half
    time_count = HEAD_DIM // 8
    space_count = 3 * HEAD_DIM // 16
    sign = jnp.where(lane < half, -1.0, 1.0)
    time_freq = 10000.0 ** (-(place.astype(jnp.float32)) / time_count)
    space_place = jnp.where(place < time_count + space_count, place - time_count, place - time_count - space_count)
    space_freq = 100.0 ** (-(space_place.astype(jnp.float32)) / space_count)
    is_time = place < time_count
    is_row = (place >= time_count) & (place < time_count + space_count)
    return sign, time_freq, space_freq, is_time, is_row


def time_tables(frames):
    sign, time_freq, _, is_time, _ = lane_places()
    angle = frames.astype(jnp.float32)[:, None] * time_freq[None]
    return (
        jnp.where(is_time, jnp.cos(angle), 0.0)[:, None],
        jnp.where(is_time, jnp.sin(angle) * sign, 0.0)[:, None],
    )


def space_tables():
    sign, _, space_freq, is_time, is_row = lane_places()
    token = jnp.arange(FRAME_TOK, dtype=jnp.int32)
    row_pos = (token // SIDE).astype(jnp.float32)[:, None]
    col_pos = (token % SIDE).astype(jnp.float32)[:, None]
    angle = jnp.where(is_row[None], row_pos, col_pos) * space_freq[None]
    return (
        jnp.where(is_time, 0.0, jnp.cos(angle)),
        jnp.where(is_time, 0.0, jnp.sin(angle) * sign),
    )


def partner(value):
    half = HEAD_DIM // 2
    width = value.shape[1]
    if width == LANES:
        lane = lax.broadcasted_iota(jnp.int32, value.shape, 1)
        ahead = pltpu.roll(value, width - half, 1)
        behind = pltpu.roll(value, half, 1)
        return jnp.where(lane % HEAD_DIM < half, ahead, behind)
    return jnp.concatenate([value[:, half:], value[:, :half]], axis=1)


def triple_kernel(normed_ref, weight_ref, time_cos, time_sin, space_cos, space_sin, out_ref):
    column = pl.program_id(0)
    width = out_ref.shape[-1]
    acc = product(normed_ref[...], weight_ref[...])
    per_block = acc.shape[1] // LANES
    frames = acc.shape[0] // FRAME_TOK

    def store(piece, values):
        for part in range(LANES // width):
            out_ref[piece * (LANES // width) + part, 0] = values[
                :, part * width : (part + 1) * width
            ].astype(low_type)

    turned = column < 2 * D // acc.shape[1]

    @pl.when(turned)
    def _():
        for piece in range(per_block):
            done = []
            for frame in range(frames):
                value = acc[
                    frame * FRAME_TOK : (frame + 1) * FRAME_TOK,
                    piece * LANES : (piece + 1) * LANES,
                ]
                cosine = time_cos[frame] + space_cos[...]
                sine = time_sin[frame] + space_sin[...]
                done.append(value * cosine + partner(value) * sine)
            store(piece, jnp.concatenate(done, axis=0))

    @pl.when(jnp.logical_not(turned))
    def _():
        for piece in range(per_block):
            store(piece, acc[:, piece * LANES : (piece + 1) * LANES])


def triple_heads(normed, weight, times, spaces, groups):
    tokens = normed.shape[0]
    width = D // groups
    block = 256
    per_block = block // width
    per_part = D // block
    return pl.pallas_call(
        triple_kernel,
        grid=(3 * D // block,),
        in_specs=[
            pl.BlockSpec((tokens, D), lambda j: (0, 0)),
            pl.BlockSpec((D, block), lambda j: (0, j)),
            pl.BlockSpec(times[0].shape, lambda j: (0, 0, 0)),
            pl.BlockSpec(times[1].shape, lambda j: (0, 0, 0)),
            pl.BlockSpec(spaces[0].shape, lambda j: (0, 0)),
            pl.BlockSpec(spaces[1].shape, lambda j: (0, 0)),
        ],
        out_specs=pl.BlockSpec(
            (per_block, 1, tokens, width), lambda j: (j % per_part, j // per_part, 0, 0)
        ),
        out_shape=jax.ShapeDtypeStruct((groups, 3, tokens, width), low_type),
        compiler_params=pltpu.CompilerParams(vmem_limit_bytes=32 * 1024 * 1024),
        name="triple_heads",
    )(normed, weight, *times, *spaces)


def head_stack(value):
    count = value.shape[1] // HEAD_DIM
    if count == 1:
        return value
    lane = lax.broadcasted_iota(jnp.int32, value.shape, 1)
    zero = jnp.zeros_like(value)
    return jnp.concatenate(
        [jnp.where(lane // HEAD_DIM == head, value, zero) for head in range(count)], axis=0
    )


def attend_kernel(
    order_ref, count_ref, query_ref, key_ref, value_ref, out_ref, flat_ref, log_ref, turned_ref
):
    step = pl.program_id(0)
    chunks, per_chunk = key_ref.shape[0], key_ref.shape[1]
    width = key_ref.shape[-1]
    heads = width // HEAD_DIM
    span = heads * FRAME_TOK

    @pl.when(step == 0)
    def _():
        def turn(chunk, carry):
            for part in range(per_chunk):
                turned_ref[chunk, part] = jnp.transpose(value_ref[chunk, part])
            return carry

        lax.fori_loop(0, chunks, turn, 0)

    queries = head_stack(query_ref[...] * jnp.asarray(HEAD_DIM**-0.5, low_type))

    def visit(place, carry):
        top, total, sums = carry
        frame = order_ref[place]
        chunk, part = frame // per_chunk, frame % per_chunk
        scores = against(key_ref[chunk, part], queries)
        new_top = jnp.maximum(top, jnp.max(scores, axis=0, keepdims=True))
        rescale = jnp.exp(top - new_top)
        chances = jnp.exp(scores - new_top)
        total = total * rescale + jnp.sum(chances, axis=0, keepdims=True)
        chances = chances.astype(low_type)
        new_sums = []
        for head in range(heads):
            columns = slice(head * FRAME_TOK, (head + 1) * FRAME_TOK)
            values = turned_ref[chunk, part, head * HEAD_DIM : (head + 1) * HEAD_DIM, :]
            new_sums.append(
                sums[head] * rescale[:, columns] + product(values, chances[:, columns])
            )
        return new_top, total, tuple(new_sums)

    initial = (
        jnp.full((1, span), -1e30, jnp.float32),
        jnp.zeros((1, span), jnp.float32),
        tuple(jnp.zeros((HEAD_DIM, FRAME_TOK), jnp.float32) for _ in range(heads)),
    )
    top, total, sums = lax.fori_loop(0, count_ref[step], visit, initial)
    log_ref[...] = top + jnp.log(total)
    inverse = 1.0 / total
    result = jnp.concatenate(
        [
            sums[head] * inverse[:, head * FRAME_TOK : (head + 1) * FRAME_TOK]
            for head in range(heads)
        ],
        axis=0,
    )
    flat_ref[...] = result
    out_ref[...] = jnp.transpose(result).astype(low_type)


def whole(shape):
    return pl.BlockSpec(shape, lambda *_: (0,) * len(shape))


def attend(order, count, queries, keys, values):
    chunks, per_chunk, _, width = queries.shape
    frames = chunks * per_chunk
    span = width // HEAD_DIM * FRAME_TOK
    return pl.pallas_call(
        attend_kernel,
        grid_spec=pltpu.PrefetchScalarGridSpec(
            num_scalar_prefetch=2,
            grid=(frames,),
            in_specs=[
                pl.BlockSpec(
                    (None, None, FRAME_TOK, width),
                    lambda i, *_: (i // per_chunk, i % per_chunk, 0, 0),
                ),
                whole(keys.shape),
                whole(values.shape),
            ],
            out_specs=[
                pl.BlockSpec(
                    (None, None, FRAME_TOK, width),
                    lambda i, *_: (i // per_chunk, i % per_chunk, 0, 0),
                ),
                pl.BlockSpec((None, width, FRAME_TOK), lambda i, *_: (i, 0, 0)),
                pl.BlockSpec((None, 1, span), lambda i, *_: (i, 0, 0)),
            ],
            scratch_shapes=[
                pltpu.VMEM((keys.shape[0], per_chunk, width, FRAME_TOK), low_type),
            ],
        ),
        out_shape=[
            jax.ShapeDtypeStruct(queries.shape, low_type),
            jax.ShapeDtypeStruct((frames, width, FRAME_TOK), jnp.float32),
            jax.ShapeDtypeStruct((frames, 1, span), jnp.float32),
        ],
        compiler_params=pltpu.CompilerParams(vmem_limit_bytes=48 * 1024 * 1024),
        name="attend",
    )(order, count, queries, keys, values)


def attend_back_kernel(
    order_ref,
    count_ref,
    query_ref,
    key_ref,
    value_ref,
    grad_ref,
    flat_ref,
    log_ref,
    query_cos,
    query_sin,
    key_cos,
    key_sin,
    space_cos,
    space_sin,
    grad_query_ref,
    grad_key_ref,
    grad_value_ref,
    stacked_query,
    stacked_grad,
    row_dot,
    sums_ref,
):
    step = pl.program_id(0)
    frames, width, _ = flat_ref.shape
    per_chunk = query_ref.shape[1]
    heads = width // HEAD_DIM
    scale = HEAD_DIM**-0.5

    @pl.when(step == 0)
    def _():
        def ready(frame, carry):
            chunk, part = frame // per_chunk, frame % per_chunk
            query = query_ref[chunk, part] * jnp.asarray(scale, low_type)
            stacked_query[frame] = head_stack(query)
            grad = grad_ref[chunk, part]
            stacked_grad[frame] = head_stack(grad)
            both = jnp.transpose(grad.astype(jnp.float32)) * flat_ref[frame]
            row_dot[frame] = jnp.concatenate(
                [
                    jnp.sum(both[head * HEAD_DIM : (head + 1) * HEAD_DIM], axis=0, keepdims=True)
                    for head in range(heads)
                ],
                axis=1,
            )
            sums_ref[frame] = jnp.zeros((width, FRAME_TOK), jnp.float32)
            return carry

        lax.fori_loop(0, frames, ready, 0)

    keys = key_ref[...]
    values = value_ref[...]
    turned_keys = jnp.transpose(keys)

    def visit(place, carry):
        grad_keys, grad_values = carry
        frame = order_ref[place]
        queries = stacked_query[frame]
        grads = stacked_grad[frame]
        scores = against(keys, queries)
        chances = jnp.exp(scores - log_ref[frame])
        grad_chances = against(values, grads)
        grad_scores = (chances * (grad_chances - row_dot[frame])).astype(low_type)
        grad_values = grad_values + product(chances.astype(low_type), grads)
        grad_keys = grad_keys + product(grad_scores, queries)
        for head in range(heads):
            rows = slice(head * HEAD_DIM, (head + 1) * HEAD_DIM)
            sums_ref[frame, rows, :] += product(
                turned_keys[rows], grad_scores[:, head * FRAME_TOK : (head + 1) * FRAME_TOK]
            )
        return grad_keys, grad_values

    zero = jnp.zeros((FRAME_TOK, width), jnp.float32)
    grad_keys, grad_values = lax.fori_loop(0, count_ref[step], visit, (zero, zero))
    space_c, space_s = space_cos[:, :width], space_sin[:, :width]
    grad_value_ref[...] = grad_values.astype(low_type)
    grad_key_ref[...] = (
        grad_keys * (key_cos[:, :width] + space_c)
        - partner(grad_keys) * (key_sin[:, :width] + space_s)
    ).astype(low_type)

    @pl.when(step == pl.num_programs(0) - 1)
    def _():
        def finish(frame, carry):
            chunk, part = frame // per_chunk, frame % per_chunk
            value = jnp.transpose(sums_ref[frame]) * scale
            grad_query_ref[chunk, part] = (
                value * (query_cos[frame][:, :width] + space_c)
                - partner(value) * (query_sin[frame][:, :width] + space_s)
            ).astype(low_type)
            return carry

        lax.fori_loop(0, frames, finish, 0)


def attend_back(
    order, count, queries, keys, values, grads, flat, logs, query_times, key_times, spaces
):
    per_chunk, width = queries.shape[1], queries.shape[3]
    frames = flat.shape[0]
    key_frames = keys.shape[0] * per_chunk
    span = width // HEAD_DIM * FRAME_TOK
    key_spec = pl.BlockSpec(
        (None, None, FRAME_TOK, width), lambda i, *_: (i // per_chunk, i % per_chunk, 0, 0)
    )
    key_time = pl.BlockSpec((None, 1, LANES), lambda i, *_: (i, 0, 0))
    return pl.pallas_call(
        attend_back_kernel,
        grid_spec=pltpu.PrefetchScalarGridSpec(
            num_scalar_prefetch=2,
            grid=(key_frames,),
            in_specs=[
                whole(queries.shape),
                key_spec,
                key_spec,
                whole(grads.shape),
                whole(flat.shape),
                whole(logs.shape),
                whole(query_times[0].shape),
                whole(query_times[1].shape),
                key_time,
                key_time,
                whole(spaces[0].shape),
                whole(spaces[1].shape),
            ],
            out_specs=[whole(queries.shape), key_spec, key_spec],
            scratch_shapes=[
                pltpu.VMEM((frames, span, width), low_type),
                pltpu.VMEM((frames, span, width), low_type),
                pltpu.VMEM((frames, 1, span), jnp.float32),
                pltpu.VMEM((frames, width, FRAME_TOK), jnp.float32),
            ],
        ),
        out_shape=[
            jax.ShapeDtypeStruct(queries.shape, low_type),
            jax.ShapeDtypeStruct(keys.shape, low_type),
            jax.ShapeDtypeStruct(keys.shape, low_type),
        ],
        compiler_params=pltpu.CompilerParams(vmem_limit_bytes=56 * 1024 * 1024),
        name="attend_back",
    )(
        order,
        count,
        queries,
        keys,
        values,
        grads,
        flat,
        logs,
        *query_times,
        *key_times,
        *spaces,
    )


def total_sum(value):
    for axis in ("core", "batch", "row"):
        size = lax.axis_size(axis)
        by = 1
        while by < size:
            value = value + lax.ppermute(value, axis, [(i, i ^ by) for i in range(size)])
            by *= 2
    return value


def staged_sum(value):
    batch, row, core = (lax.axis_size(axis) for axis in ALL)
    value = value.reshape((batch, row, core) + value.shape[1:])
    mine = lax.axis_index("core")
    send = lax.dynamic_index_in_dim(value, 1 - mine, 2, keepdims=False).astype(low_type)
    keep = lax.dynamic_index_in_dim(value, mine, 2, keepdims=False)
    swap = [(i, 1 - i) for i in range(core)]
    value = keep + lax.ppermute(send, "core", swap).astype(jnp.float32)
    for axis in ("batch", "row"):
        parts = lax.all_to_all(value.astype(low_type), axis, 0, 0, tiled=True)
        value = jnp.sum(parts.astype(jnp.float32), axis=0)
    return value


def per_device(
    clean_latents,
    noise_sample,
    noise_levels,
    clean_flags,
    span_frame,
    patch_master,
    patch_first,
    patch_second,
    level_master,
    level_first,
    level_second,
    adaptive_master,
    adaptive_first,
    adaptive_second,
    triple_master,
    triple_first,
    triple_second,
    project_master,
    project_first,
    project_second,
    expand_master,
    expand_first,
    expand_second,
    reduce_master,
    reduce_first,
    reduce_second,
    readout_master,
    readout_first,
    readout_second,
):
    masters = (
        patch_master,
        level_master,
        adaptive_master,
        triple_master,
        project_master,
        expand_master,
        reduce_master,
        readout_master,
    )
    firsts = (
        patch_first,
        level_first,
        adaptive_first,
        triple_first,
        project_first,
        expand_first,
        reduce_first,
        readout_first,
    )
    seconds = (
        patch_second,
        level_second,
        adaptive_second,
        triple_second,
        project_second,
        expand_second,
        reduce_second,
        readout_second,
    )
    batch_count, row_count, core_count = (lax.axis_size(axis) for axis in ALL)
    batch_index, row_index, core_index = (lax.axis_index(axis) for axis in ALL)
    devices = batch_count * row_count * core_count
    rows = D // devices
    token_count = clean_latents.shape[1]
    frame_local = token_count // FRAME_TOK

    moved = batch_count == row_count and HEADS % (batch_count * core_count) == 0
    if moved:
        clip_index, chunk_index = row_index, batch_index * core_count + core_index
        head_axes, head_groups = ("batch", "core"), batch_count * core_count
    else:
        clip_index, chunk_index = batch_index, row_index * core_count + core_index
        head_axes, head_groups = ("row",), row_count

    both = jnp.concatenate([clean_latents[0], noise_sample[0]], axis=1)
    if moved:
        turn = [
            (
                (a * row_count + b) * core_count + c,
                (b * row_count + a) * core_count + c,
            )
            for a in range(batch_count)
            for b in range(row_count)
            for c in range(core_count)
        ]
        both = lax.ppermute(both, ALL, turn)
    clean_tok, noise_tok = both[:, :PATCH_FEAT], both[:, PATCH_FEAT:]

    first_weights = jnp.concatenate(
        [
            triple_master.astype(low_type),
            jnp.transpose(patch_master).astype(low_type),
            readout_master.astype(low_type),
            jnp.zeros((rows, LANES - 2 * PATCH_FEAT), low_type),
        ],
        axis=1,
    )
    first_weights = lax.all_gather(first_weights, ALL, axis=0, tiled=True)
    second_weights = jnp.concatenate(
        [project_master.astype(low_type)]
        + [expand_master[:, k * D : (k + 1) * D].astype(low_type) for k in range(FF // D)]
        + [reduce_master.astype(low_type)],
        axis=0,
    )
    second_weights = lax.all_gather(second_weights, ALL, axis=0)

    levels_all = noise_levels.reshape(-1)
    flags_all = clean_flags.reshape(-1)
    _, _, index_all = plan(levels_all, flags_all)
    if moved:
        order_all = lambda v: (
            v.reshape((row_count, batch_count, core_count, frame_local) + v.shape[1:])
            .swapaxes(0, 1)
            .reshape(v.shape)
        )
    else:
        order_all = lambda v: v
    index_all = order_all(index_all)
    hot_all = (index_all[:, None] == jnp.arange(NB + 1, dtype=jnp.int32)[None, :]).astype(
        jnp.float32
    )
    pre_own = jnp.dot(
        hot_all,
        level_master.astype(low_type).astype(jnp.float32),
        precision=lax.Precision.HIGHEST,
    )
    cond_value, silu_back = jax.vjp(jax.nn.silu, pre_own)
    cond_own = cond_value.astype(low_type)
    adaptive_low = adaptive_master.astype(low_type)
    adapt_parts = lax.all_to_all(
        product(cond_own, adaptive_low).reshape(devices, frame_local, 6 * D), ALL, 0, 0, tiled=True
    )
    adapt = jnp.sum(adapt_parts, axis=0)
    shift_one, scale_one, gate_one, shift_two, scale_two, gate_two = jnp.split(adapt, 6, axis=1)

    my_levels = lax.dynamic_slice_in_dim(
        lax.dynamic_index_in_dim(noise_levels, clip_index, 0, keepdims=False),
        chunk_index * frame_local,
        frame_local,
    )
    my_flags = lax.dynamic_slice_in_dim(
        lax.dynamic_index_in_dim(clean_flags, clip_index, 0, keepdims=False),
        chunk_index * frame_local,
        frame_local,
    )
    my_frames = lax.dynamic_slice_in_dim(span_frame, chunk_index * frame_local, frame_local)
    if moved:
        query_frames = key_frames = span_frame
    else:
        by_chunk = span_frame.reshape(row_count, core_count, frame_local)
        query_frames = lax.dynamic_index_in_dim(by_chunk, core_index, 1, keepdims=False).reshape(-1)
        key_frames = by_chunk.swapaxes(0, 1).reshape(-1)
    query_total, key_total = query_frames.shape[0], key_frames.shape[0]
    earlier = jnp.sum(key_frames[None, :] < key_frames[:, None], axis=1)
    key_order = jnp.sum(
        jnp.where(earlier[:, None] == jnp.arange(key_total)[None, :], jnp.arange(key_total)[:, None], 0),
        axis=0,
    ).astype(jnp.int32)
    key_count = jnp.sum(key_frames[None, :] <= query_frames[:, None], axis=1).astype(jnp.int32)
    later = jnp.sum(query_frames[None, :] > query_frames[:, None], axis=1)
    query_order = jnp.sum(
        jnp.where(later[:, None] == jnp.arange(query_total)[None, :], jnp.arange(query_total)[:, None], 0),
        axis=0,
    ).astype(jnp.int32)
    query_count = jnp.sum(query_frames[None, :] >= key_frames[:, None], axis=1).astype(jnp.int32)
    my_times, query_times, key_times = (
        time_tables(my_frames),
        time_tables(query_frames),
        time_tables(key_frames),
    )
    spaces = space_tables()

    alpha_bar, noised, _ = plan(my_levels, my_flags)
    inputs = noised_input(clean_tok, noise_tok, alpha_bar, noised).astype(low_type)
    patch_turned = first_weights[:, 3 * D : 3 * D + PATCH_FEAT]
    readout_weight = first_weights[:, 3 * D + PATCH_FEAT : 3 * D + 2 * PATCH_FEAT]
    triple_weight = first_weights
    hidden_zero = against(inputs, patch_turned)
    normed, first_back = jax.vjp(modulate, hidden_zero, shift_one, scale_one)
    normed_low = normed.astype(low_type)

    heads = triple_heads(normed_low, triple_weight, my_times, spaces, head_groups)
    heads = lax.all_to_all(heads, head_axes, 0, 0, tiled=True)
    width = D // head_groups
    heads = heads.reshape(head_groups, 3, frame_local, FRAME_TOK, width)
    queries, keys, values = heads[:, 0], heads[:, 1], heads[:, 2]
    if not moved:
        keys = lax.all_gather(keys, "core", axis=0, tiled=True)
        values = lax.all_gather(values, "core", axis=0, tiled=True)
    attended, flat, logs = attend(key_order, key_count, queries, keys, values)
    attended = attended.reshape(head_groups, token_count, width)
    attended = lax.all_to_all(attended, head_axes, 0, 0, tiled=True)
    attended_low = attended.swapaxes(0, 1).reshape(token_count, D)

    project_weight = second_weights[:, :rows].reshape(D, D)
    expand_weights = [
        second_weights[:, (1 + k) * rows : (2 + k) * rows].reshape(D, D) for k in range(FF // D)
    ]
    reduce_weight = second_weights[:, (1 + FF // D) * rows :].reshape(FF, D)
    expand_weight = jnp.concatenate(expand_weights, axis=1)

    branch = product(attended_low, project_weight)
    hidden_one = hidden_zero + per_frame(gate_one, branch)
    mixed_tok, second_back = jax.vjp(modulate, hidden_one, shift_two, scale_two)
    mixed_low = mixed_tok.astype(low_type)
    inner = product(mixed_low, expand_weight)
    active, gelu_back = jax.vjp(gelu_tanh, inner)
    active_low = active.astype(low_type)
    outer = product(active_low, reduce_weight)
    hidden_two = hidden_one + per_frame(gate_two, outer)
    final, final_back = jax.vjp(layer_norm, hidden_two)
    final_low = final.astype(low_type)
    predicted = product(final_low, readout_weight)
    residue = predicted - noise_tok
    frame_loss = jnp.mean(jnp.square(residue).reshape(frame_local, -1), axis=1) * noised
    frame_count = jnp.sum((1 - clean_flags).astype(jnp.float32))
    loss_scale = noised * (2.0 / (FRAME_TOK * PATCH_FEAT)) / jnp.maximum(frame_count, 1.0)
    grad_pred = (
        (residue.reshape(frame_local, -1, residue.shape[-1]) * loss_scale[:, None, None])
        .reshape(residue.shape)
        .astype(low_type)
    )
    grad_readout = across(final_low, grad_pred)
    (grad_hidden_two,) = final_back(against(grad_pred, readout_weight))
    grad_outer = per_frame(gate_two, grad_hidden_two).astype(low_type)
    grad_gate_two = frame_sum(gate_two, grad_hidden_two * outer)
    grad_reduce = across(active_low, grad_outer)
    (grad_inner,) = gelu_back(against(grad_outer, reduce_weight))
    grad_inner_low = grad_inner.astype(low_type)
    grad_expand = across(mixed_low, grad_inner_low)
    hidden_part, grad_shift_two, grad_scale_two = second_back(
        against(grad_inner_low, expand_weight)
    )
    grad_hidden_one = grad_hidden_two + hidden_part
    grad_branch = per_frame(gate_one, grad_hidden_one).astype(low_type)
    grad_gate_one = frame_sum(gate_one, grad_hidden_one * branch)
    grad_project = across(attended_low, grad_branch)
    second_grads = jnp.concatenate(
        [grad_project.reshape(devices, rows, D)]
        + [
            grad_expand[:, k * D : (k + 1) * D].reshape(devices, rows, D) for k in range(FF // D)
        ]
        + [grad_reduce.reshape(devices, FF // devices, D)],
        axis=1,
    )
    second_own = lax.psum_scatter(second_grads, ALL, scatter_dimension=0)

    grad_attended = (
        against(grad_branch, project_weight)
        .astype(low_type)
        .reshape(token_count, head_groups, width)
        .swapaxes(0, 1)
    )
    grad_attended = lax.all_to_all(grad_attended, head_axes, 0, 0, tiled=True)
    grad_attended = grad_attended.reshape(queries.shape)
    grad_queries, grad_keys, grad_values = attend_back(
        query_order,
        query_count,
        queries,
        keys,
        values,
        grad_attended,
        flat,
        logs,
        query_times,
        key_times,
        spaces,
    )
    if not moved:
        grad_keys, grad_values = (
            lax.psum_scatter(
                item.astype(jnp.float32), "core", scatter_dimension=0, tiled=True
            ).astype(low_type)
            for item in (grad_keys, grad_values)
        )
    grad_heads = jnp.stack([grad_queries, grad_keys, grad_values], axis=1)
    grad_heads = lax.all_to_all(
        grad_heads.reshape(head_groups, 3, token_count, width), head_axes, 0, 0, tiled=True
    )
    grad_triple_tok = jnp.transpose(grad_heads, (2, 1, 0, 3)).reshape(token_count, 3 * D)
    grad_triple = across(normed_low, grad_triple_tok)
    hidden_part, grad_shift_one, grad_scale_one = first_back(
        against(grad_triple_tok, triple_weight[:, : 3 * D])
    )
    grad_hidden_zero = (grad_hidden_one + hidden_part).astype(low_type)
    grad_patch = across(grad_hidden_zero, inputs)
    first_grads = jnp.concatenate(
        [
            grad_triple,
            grad_patch,
            grad_readout,
            jnp.zeros((D, LANES - 2 * PATCH_FEAT), jnp.float32),
        ],
        axis=1,
    )
    first_own = staged_sum(first_grads.reshape(devices, rows, first_grads.shape[1]))

    grad_adapt_tok = jnp.concatenate(
        [
            grad_shift_one,
            grad_scale_one,
            grad_gate_one,
            grad_shift_two,
            grad_scale_two,
            grad_gate_two,
        ],
        axis=1,
    ).astype(low_type)
    adapt_tok_all = lax.all_gather(grad_adapt_tok, ALL, axis=0, tiled=True)
    adapt_own = across(cond_own, adapt_tok_all)
    (grad_pre,) = silu_back(against(adapt_tok_all, adaptive_low))
    table_own = lax.dot_general(
        hot_all,
        grad_pre,
        (((0,), (0,)), ((), ())),
        precision=lax.Precision.HIGHEST,
        preferred_element_type=jnp.float32,
    )
    expand_own = jnp.concatenate(
        [second_own[(1 + k) * rows : (2 + k) * rows] for k in range(FF // D)], axis=1
    )
    reduced = (
        jnp.transpose(first_own[:, 3 * D : 3 * D + PATCH_FEAT]),
        table_own,
        adapt_own,
        first_own[:, : 3 * D],
        second_own[:rows],
        expand_own,
        second_own[(1 + FF // D) * rows :],
        first_own[:, 3 * D + PATCH_FEAT : 3 * D + 2 * PATCH_FEAT],
    )
    squares = sum((jnp.sum(gradient * gradient) for gradient in reduced))
    level_hits = (my_levels[:, None] == jnp.arange(NB, dtype=jnp.int32)[None, :]).astype(
        jnp.float32
    )
    bucket_local = jnp.sum(level_hits * frame_loss[:, None], axis=0)
    sums = jnp.zeros((8, LANES), jnp.float32)
    sums = sums.at[0, :NB].set(bucket_local)
    sums = sums.at[1, 0].set(squares)
    sums = sums.at[2, 0].set(jnp.sum(frame_loss))
    sums = total_sum(sums)
    clip_norm = jnp.sqrt(sums[1, 0])
    factor = jnp.minimum(1.0, clip_bound / clip_norm)
    new = [
        adamw_update(
            masters[item], firsts[item], seconds[item], reduced[item], factor, learn_rates[item]
        )
        for item in range(8)
    ]
    return (sums[2, 0], frame_count, sums[0, :NB], clip_norm) + tuple(
        item for triple in new for item in triple
    )


def solution(mesh):
    in_specs = (
        P("batch", ("row", "core"), None),
        P("batch", ("row", "core"), None),
        P(),
        P(),
        P(),
        P(None, ALL),
        P(None, ALL),
        P(None, ALL),
        P(None, ALL),
        P(None, ALL),
        P(None, ALL),
        P(ALL, None),
        P(ALL, None),
        P(ALL, None),
        P(ALL, None),
        P(ALL, None),
        P(ALL, None),
        P(ALL, None),
        P(ALL, None),
        P(ALL, None),
        P(ALL, None),
        P(ALL, None),
        P(ALL, None),
        P(ALL, None),
        P(ALL, None),
        P(ALL, None),
        P(ALL, None),
        P(ALL, None),
        P(ALL, None),
    )
    out_specs = (
        P(),
        P(),
        P(),
        P(),
        P(None, ALL),
        P(None, ALL),
        P(None, ALL),
        P(None, ALL),
        P(None, ALL),
        P(None, ALL),
        P(ALL, None),
        P(ALL, None),
        P(ALL, None),
        P(ALL, None),
        P(ALL, None),
        P(ALL, None),
        P(ALL, None),
        P(ALL, None),
        P(ALL, None),
        P(ALL, None),
        P(ALL, None),
        P(ALL, None),
        P(ALL, None),
        P(ALL, None),
        P(ALL, None),
        P(ALL, None),
        P(ALL, None),
        P(ALL, None),
    )
    batch_size, blk_size = mesh.shape["batch"], mesh.shape["blk"]
    inner = Mesh(mesh.devices.reshape(batch_size, blk_size // 2, 2), ALL)
    return jax.shard_map(
        per_device, mesh=inner, in_specs=in_specs, out_specs=out_specs, check_vma=False
    )
```

```python
import functools
import math

import jax
import jax.numpy as jnp
from jax import lax
from jax.experimental import pallas as pl
from jax.experimental.pallas import tpu as pltpu
from jax.sharding import Mesh
from jax.sharding import PartitionSpec as P

D = 1024
HEADS = 16
HEAD_DIM = 64
FF = 4096
PATCH_FEAT = 16
FRAME_TOK = 256
SIDE = 16
NB = 32
STEP = 10
LANES = 128
ALL = ("batch", "row", "core")


learn_rates = (0.5, 2.0, 0.05, 0.05, 0.5, 0.05, 0.05, 0.05)
beta_first = 0.9
beta_second = 0.999
decay_rate = 0.01
adam_floor = 1e-08
clip_bound = 0.02
low_type = jnp.bfloat16


def product(left, right):
    return jnp.dot(left, right, preferred_element_type=jnp.float32)


def across(left, right):
    return lax.dot_general(
        left, right, (((0,), (0,)), ((), ())), preferred_element_type=jnp.float32
    )


def against(left, right):
    return lax.dot_general(
        left, right, (((1,), (1,)), ((), ())), preferred_element_type=jnp.float32
    )


def plan(levels, clean_flags):
    alpha_bar = jnp.cos(0.5 * math.pi * (levels.astype(jnp.float32) + 1.0) / (NB + 1.0)) ** 2
    noised = (1 - clean_flags).astype(jnp.float32)
    table_index = jnp.where(clean_flags == 1, 0, levels + 1)
    return (alpha_bar, noised, table_index)


def noised_input(clean_tok, noise_tok, alpha_bar, noised):
    frame_shape = (alpha_bar.shape[0], -1, clean_tok.shape[-1])
    clean_frames = clean_tok.reshape(frame_shape)
    noise_frames = noise_tok.reshape(frame_shape)
    mixed_tok = (
        jnp.sqrt(alpha_bar)[:, None, None] * clean_frames
        + jnp.sqrt(1.0 - alpha_bar)[:, None, None] * noise_frames
    )
    return jnp.where(noised[:, None, None] > 0.5, mixed_tok, clean_frames).reshape(clean_tok.shape)


def layer_norm(hidden):
    centred = hidden - jnp.mean(hidden, axis=-1, keepdims=True)
    variance = jnp.mean(centred * centred, axis=-1, keepdims=True)
    return centred * lax.rsqrt(variance + 1e-06)


def modulate(hidden, shift, scale):
    normed = layer_norm(hidden).reshape(shift.shape[0], -1, hidden.shape[-1])
    return (normed * (1.0 + scale[:, None]) + shift[:, None]).reshape(hidden.shape)


def adamw_update(master, first_moment, second_moment, gradient, factor, step_rate):
    clipped = gradient * factor
    first_new = beta_first * first_moment + (1.0 - beta_first) * clipped
    second_new = beta_second * second_moment + (1.0 - beta_second) * clipped * clipped
    first_hat = first_new / (1.0 - beta_first**STEP)
    second_hat = second_new / (1.0 - beta_second**STEP)
    master_new = master - step_rate * (
        first_hat / (jnp.sqrt(second_hat) + adam_floor) + decay_rate * master
    )
    return (first_new, second_new, master_new)


def lane_places():
    lane = jnp.arange(LANES, dtype=jnp.int32) % HEAD_DIM
    half = HEAD_DIM // 2
    place = lane % half
    time_count = HEAD_DIM // 8
    space_count = 3 * HEAD_DIM // 16
    sign = jnp.where(lane < half, -1.0, 1.0)
    time_freq = 10000.0 ** (-(place.astype(jnp.float32)) / time_count)
    space_place = jnp.where(place < time_count + space_count, place - time_count, place - time_count - space_count)
    space_freq = 100.0 ** (-(space_place.astype(jnp.float32)) / space_count)
    is_time = place < time_count
    is_row = (place >= time_count) & (place < time_count + space_count)
    return sign, time_freq, space_freq, is_time, is_row


def time_tables(frames):
    sign, time_freq, _, is_time, _ = lane_places()
    angle = frames.astype(jnp.float32)[:, None] * time_freq[None]
    return (
        jnp.where(is_time, jnp.cos(angle), 0.0)[:, None],
        jnp.where(is_time, jnp.sin(angle) * sign, 0.0)[:, None],
    )


def space_tables():
    sign, _, space_freq, is_time, is_row = lane_places()
    token = jnp.arange(FRAME_TOK, dtype=jnp.int32)
    row_pos = (token // SIDE).astype(jnp.float32)[:, None]
    col_pos = (token % SIDE).astype(jnp.float32)[:, None]
    angle = jnp.where(is_row[None], row_pos, col_pos) * space_freq[None]
    return (
        jnp.where(is_time, 0.0, jnp.cos(angle)),
        jnp.where(is_time, 0.0, jnp.sin(angle) * sign),
    )


def partner(value):
    half = HEAD_DIM // 2
    width = value.shape[1]
    if width == LANES:
        lane = lax.broadcasted_iota(jnp.int32, value.shape, 1)
        ahead = pltpu.roll(value, width - half, 1)
        behind = pltpu.roll(value, half, 1)
        return jnp.where(lane % HEAD_DIM < half, ahead, behind)
    return jnp.concatenate([value[:, half:], value[:, :half]], axis=1)


def triple_kernel(normed_ref, weight_ref, time_cos, time_sin, space_cos, space_sin, out_ref):
    column = pl.program_id(0)
    width = out_ref.shape[-1]
    acc = product(normed_ref[...], weight_ref[...])
    per_block = acc.shape[1] // LANES
    frames = acc.shape[0] // FRAME_TOK

    def store(piece, values):
        for part in range(LANES // width):
            place = piece * (LANES // width) + part
            done = values[:, part * width : (part + 1) * width].astype(low_type)
            if len(out_ref.shape) == 3:
                out_ref[place] = done
            else:
                out_ref[place, 0] = done

    turned = column < 2 * D // acc.shape[1]

    @pl.when(turned)
    def _():
        for piece in range(per_block):
            done = []
            for frame in range(frames):
                value = acc[
                    frame * FRAME_TOK : (frame + 1) * FRAME_TOK,
                    piece * LANES : (piece + 1) * LANES,
                ]
                cosine = time_cos[frame] + space_cos[...]
                sine = time_sin[frame] + space_sin[...]
                done.append(value * cosine + partner(value) * sine)
            store(piece, jnp.concatenate(done, axis=0))

    @pl.when(jnp.logical_not(turned))
    def _():
        for piece in range(per_block):
            store(piece, acc[:, piece * LANES : (piece + 1) * LANES])


def triple_heads(normed, weight, times, spaces, groups):
    tokens = normed.shape[0]
    width = D // groups
    block = 256
    per_block = block // width
    per_part = D // block
    if width == LANES:
        out_specs = pl.BlockSpec(
            (per_block, tokens, width), lambda j: (j % per_part, 0, j // per_part)
        )
        out_shape = jax.ShapeDtypeStruct((groups, tokens, 3 * width), low_type)
    else:
        out_specs = pl.BlockSpec(
            (per_block, 1, tokens, width), lambda j: (j % per_part, j // per_part, 0, 0)
        )
        out_shape = jax.ShapeDtypeStruct((groups, 3, tokens, width), low_type)
    return pl.pallas_call(
        triple_kernel,
        grid=(3 * D // block,),
        in_specs=[
            pl.BlockSpec((tokens, D), lambda j: (0, 0)),
            pl.BlockSpec((D, block), lambda j: (0, j)),
            pl.BlockSpec(times[0].shape, lambda j: (0, 0, 0)),
            pl.BlockSpec(times[1].shape, lambda j: (0, 0, 0)),
            pl.BlockSpec(spaces[0].shape, lambda j: (0, 0)),
            pl.BlockSpec(spaces[1].shape, lambda j: (0, 0)),
        ],
        out_specs=out_specs,
        out_shape=out_shape,
        compiler_params=pltpu.CompilerParams(vmem_limit_bytes=32 * 1024 * 1024),
        cost_estimate=about(10),
        name="triple_heads",
    )(normed, weight, *times, *spaces)


def head_stack(value):
    count = value.shape[1] // HEAD_DIM
    if count == 1:
        return value
    lane = lax.broadcasted_iota(jnp.int32, value.shape, 1)
    zero = jnp.zeros_like(value)
    return jnp.concatenate(
        [jnp.where(lane // HEAD_DIM == head, value, zero) for head in range(count)], axis=0
    )


UNROLL = 4


def unrolled(count, body, carry):
    def several(base, now):
        for offset in range(UNROLL):
            now = body(base * UNROLL + offset, now)
        return now

    whole_part = count // UNROLL
    carry = lax.fori_loop(0, whole_part, several, carry)
    return lax.fori_loop(whole_part * UNROLL, count, body, carry)


def attend_kernel(
    order_ref,
    count_ref,
    query_ref,
    key_ref,
    value_ref,
    out_ref,
    flat_ref,
    log_ref,
    turned_ref,
    scores_ref,
):
    step = pl.program_id(0)
    chunks, per_chunk = key_ref.shape[0], key_ref.shape[1]
    width = key_ref.shape[-1]
    heads = width // HEAD_DIM
    span = heads * FRAME_TOK

    @pl.when(step == 0)
    def _():
        def turn(chunk, carry):
            for part in range(per_chunk):
                turned_ref[chunk, part] = jnp.transpose(value_ref[chunk, part])
            return carry

        lax.fori_loop(0, chunks, turn, 0)

    queries = jnp.transpose(head_stack(query_ref[...] * jnp.asarray(HEAD_DIM**-0.5, low_type)))
    count = count_ref[step]

    def by_eight(value):
        return value.reshape(FRAME_TOK // 8, 8, span)

    def score(place, top):
        frame = order_ref[place]
        scores = product(key_ref[frame // per_chunk, frame % per_chunk], queries)
        scores_ref[place] = scores
        return jnp.maximum(top, jnp.max(by_eight(scores), axis=0))

    top = unrolled(count, score, jnp.full((8, span), -1e30, jnp.float32))
    top = jnp.max(top, axis=0, keepdims=True)

    def weigh(place, carry):
        total, sums = carry
        frame = order_ref[place]
        chances = jnp.exp(scores_ref[place] - top)
        total = total + jnp.sum(by_eight(chances), axis=0)
        chances = chances.astype(low_type)
        new_sums = []
        for head in range(heads):
            values = turned_ref[
                frame // per_chunk,
                frame % per_chunk,
                head * HEAD_DIM : (head + 1) * HEAD_DIM,
                :,
            ]
            columns = slice(head * FRAME_TOK, (head + 1) * FRAME_TOK)
            new_sums.append(sums[head] + product(values, chances[:, columns]))
        return total, tuple(new_sums)

    initial = (
        jnp.zeros((8, span), jnp.float32),
        tuple(jnp.zeros((HEAD_DIM, FRAME_TOK), jnp.float32) for _ in range(heads)),
    )
    total, sums = unrolled(count, weigh, initial)
    total = jnp.sum(total, axis=0, keepdims=True)
    log_ref[...] = top + jnp.log(total)
    inverse = 1.0 / total
    result = jnp.concatenate(
        [
            sums[head] * inverse[:, head * FRAME_TOK : (head + 1) * FRAME_TOK]
            for head in range(heads)
        ],
        axis=0,
    )
    flat_ref[...] = result
    out_ref[...] = jnp.transpose(result).astype(low_type)


def about(microseconds):
    return pl.CostEstimate(
        flops=microseconds * 1_100_000_000, bytes_accessed=1 << 20, transcendentals=0
    )


def whole(shape):
    return pl.BlockSpec(shape, lambda *_: (0,) * len(shape))


def lanes_of(items, width):
    joint = items[0].shape[-1] != width
    return [place if joint else 0 for place in range(3)]


def attend(order, count, items, width):
    chunks, per_chunk = items[0].shape[:2]
    key_chunks = items[1].shape[0]
    frames = chunks * per_chunk
    span = width // HEAD_DIM * FRAME_TOK
    lane = lanes_of(items, width)
    return pl.pallas_call(
        attend_kernel,
        grid_spec=pltpu.PrefetchScalarGridSpec(
            num_scalar_prefetch=2,
            grid=(frames,),
            in_specs=[
                pl.BlockSpec(
                    (None, None, FRAME_TOK, width),
                    lambda i, *_: (i // per_chunk, i % per_chunk, 0, lane[0]),
                ),
                pl.BlockSpec(
                    (key_chunks, per_chunk, FRAME_TOK, width), lambda i, *_: (0, 0, 0, lane[1])
                ),
                pl.BlockSpec(
                    (key_chunks, per_chunk, FRAME_TOK, width), lambda i, *_: (0, 0, 0, lane[2])
                ),
            ],
            out_specs=[
                pl.BlockSpec(
                    (None, None, FRAME_TOK, width),
                    lambda i, *_: (i // per_chunk, i % per_chunk, 0, 0),
                ),
                pl.BlockSpec((None, width, FRAME_TOK), lambda i, *_: (i, 0, 0)),
                pl.BlockSpec((None, 1, span), lambda i, *_: (i, 0, 0)),
            ],
            scratch_shapes=[
                pltpu.VMEM((key_chunks, per_chunk, width, FRAME_TOK), low_type),
                pltpu.VMEM((key_chunks * per_chunk, FRAME_TOK, span), jnp.float32),
            ],
        ),
        out_shape=[
            jax.ShapeDtypeStruct((chunks, per_chunk, FRAME_TOK, width), low_type),
            jax.ShapeDtypeStruct((frames, width, FRAME_TOK), jnp.float32),
            jax.ShapeDtypeStruct((frames, 1, span), jnp.float32),
        ],
        compiler_params=pltpu.CompilerParams(vmem_limit_bytes=48 * 1024 * 1024),
        cost_estimate=about(45),
        name="attend",
    )(order, count, *items)


def attend_back_kernel(
    order_ref,
    count_ref,
    query_ref,
    key_ref,
    value_ref,
    grad_ref,
    flat_ref,
    log_ref,
    query_cos,
    query_sin,
    key_cos,
    key_sin,
    space_cos,
    space_sin,
    *rest,
):
    outs, (stacked_query, stacked_grad, row_dot, sums_ref) = rest[:-4], rest[-4:]
    step = pl.program_id(0)
    frames, width, _ = flat_ref.shape
    per_chunk = query_ref.shape[1]
    heads = width // HEAD_DIM
    scale = HEAD_DIM**-0.5

    @pl.when(step == 0)
    def _():
        def ready(frame, carry):
            chunk, part = frame // per_chunk, frame % per_chunk
            query = query_ref[chunk, part] * jnp.asarray(scale, low_type)
            stacked_query[frame] = head_stack(query)
            grad = grad_ref[chunk, part]
            stacked_grad[frame] = head_stack(grad)
            both = jnp.transpose(grad.astype(jnp.float32)) * flat_ref[frame]
            row_dot[frame] = jnp.concatenate(
                [
                    jnp.sum(both[head * HEAD_DIM : (head + 1) * HEAD_DIM], axis=0, keepdims=True)
                    for head in range(heads)
                ],
                axis=1,
            )
            sums_ref[frame] = jnp.zeros((width, FRAME_TOK), jnp.float32)
            return carry

        lax.fori_loop(0, frames, ready, 0)

    keys = key_ref[...]
    values = value_ref[...]
    turned_keys = jnp.transpose(keys)

    def several(base, count, carry):
        grad_keys, grad_values = carry
        frames_now = [order_ref[base + i] for i in range(count)]
        updates = []
        scores = [against(keys, stacked_query[frame]) for frame in frames_now]
        grad_chances = [against(values, stacked_grad[frame]) for frame in frames_now]
        for frame, score, grad_chance in zip(frames_now, scores, grad_chances):
            chances = jnp.exp(score - log_ref[frame])
            grad_scores = (chances * (grad_chance - row_dot[frame])).astype(low_type)
            grad_values = grad_values + product(chances.astype(low_type), stacked_grad[frame])
            grad_keys = grad_keys + product(grad_scores, stacked_query[frame])
            for head in range(heads):
                rows = slice(head * HEAD_DIM, (head + 1) * HEAD_DIM)
                updates.append(
                    product(
                        turned_keys[rows],
                        grad_scores[:, head * FRAME_TOK : (head + 1) * FRAME_TOK],
                    )
                )
        for i, frame in enumerate(frames_now):
            for head in range(heads):
                rows = slice(head * HEAD_DIM, (head + 1) * HEAD_DIM)
                sums_ref[frame, rows, :] += updates[i * heads + head]
        return grad_keys, grad_values

    zero = jnp.zeros((FRAME_TOK, width), jnp.float32)
    total = count_ref[step]
    carry = lax.fori_loop(
        0, total // UNROLL, lambda i, c: several(i * UNROLL, UNROLL, c), (zero, zero)
    )
    grad_keys, grad_values = lax.fori_loop(
        total // UNROLL * UNROLL, total, lambda i, c: several(i, 1, c), carry
    )
    space_c, space_s = space_cos[:, :width], space_sin[:, :width]

    def store(part, frame, value):
        place = (frame // per_chunk, frame % per_chunk)
        if len(outs) == 1:
            outs[0][place + (slice(None), slice(part * width, (part + 1) * width))] = value
        else:
            outs[part][place] = value

    store(2, step, grad_values.astype(low_type))
    store(
        1,
        step,
        (
            grad_keys * (key_cos[:, :width] + space_c)
            - partner(grad_keys) * (key_sin[:, :width] + space_s)
        ).astype(low_type),
    )

    @pl.when(step == pl.num_programs(0) - 1)
    def _():
        def finish(frame, carry):
            value = jnp.transpose(sums_ref[frame]) * scale
            store(
                0,
                frame,
                (
                    value * (query_cos[frame][:, :width] + space_c)
                    - partner(value) * (query_sin[frame][:, :width] + space_s)
                ).astype(low_type),
            )
            return carry

        lax.fori_loop(0, frames, finish, 0)


def attend_back(order, count, items, grads, flat, logs, query_times, key_times, spaces):
    per_chunk, width = grads.shape[1], grads.shape[3]
    frames = flat.shape[0]
    key_frames = items[1].shape[0] * per_chunk
    span = width // HEAD_DIM * FRAME_TOK
    lane = lanes_of(items, width)

    def key_spec(place):
        return pl.BlockSpec(
            (None, None, FRAME_TOK, width), lambda i, *_: (i // per_chunk, i % per_chunk, 0, place)
        )

    key_time = pl.BlockSpec((None, 1, LANES), lambda i, *_: (i, 0, 0))
    if lane[1]:
        shapes = [items[0].shape]
    else:
        shapes = [item.shape for item in items]
    return pl.pallas_call(
        attend_back_kernel,
        grid_spec=pltpu.PrefetchScalarGridSpec(
            num_scalar_prefetch=2,
            grid=(key_frames,),
            in_specs=[
                whole(grads.shape),
                key_spec(lane[1]),
                key_spec(lane[2]),
                whole(grads.shape),
                whole(flat.shape),
                whole(logs.shape),
                whole(query_times[0].shape),
                whole(query_times[1].shape),
                key_time,
                key_time,
                whole(spaces[0].shape),
                whole(spaces[1].shape),
            ],
            out_specs=[whole(shape) for shape in shapes],
            scratch_shapes=[
                pltpu.VMEM((frames, span, width), low_type),
                pltpu.VMEM((frames, span, width), low_type),
                pltpu.VMEM((frames, 1, span), jnp.float32),
                pltpu.VMEM((frames, width, FRAME_TOK), jnp.float32),
            ],
        ),
        out_shape=[jax.ShapeDtypeStruct(shape, low_type) for shape in shapes],
        compiler_params=pltpu.CompilerParams(vmem_limit_bytes=56 * 1024 * 1024),
        cost_estimate=about(65),
        name="attend_back",
    )(order, count, *items, grads, flat, logs, *query_times, *key_times, *spaces)


def norm_parts(hidden):
    centred = hidden - jnp.mean(hidden, axis=-1, keepdims=True)
    variance = jnp.mean(centred * centred, axis=-1, keepdims=True)
    inverse = lax.rsqrt(variance + 1e-06)
    return centred * inverse, inverse


def norm_back(normed, inverse, grad):
    along = jnp.mean(grad * normed, axis=-1, keepdims=True)
    return inverse * (grad - jnp.mean(grad, axis=-1, keepdims=True) - normed * along)


def row_sum(value):
    return jnp.sum(value, axis=0, keepdims=True)


def flat_weight(ref):
    return ref[...].reshape(-1, ref.shape[-1])


def project_kernel(
    heads_ref, weight_ref, hidden_ref, mods_ref, attended_ref, branch_ref, next_ref, mixed_ref
):
    attended = jnp.concatenate([heads_ref[group] for group in range(heads_ref.shape[0])], axis=1)
    attended_ref[...] = attended
    branch = product(attended, flat_weight(weight_ref))
    branch_ref[...] = branch
    hidden = hidden_ref[...] + mods_ref[2:3] * branch
    next_ref[...] = hidden
    normed, _ = norm_parts(hidden)
    mixed_ref[...] = (normed * (1.0 + mods_ref[4:5]) + mods_ref[3:4]).astype(low_type)


def project_norm(heads, weights, hidden, mods):
    groups, tokens, width = heads.shape
    devices, height, _ = weights.shape
    rows = D // devices
    by_frame = pl.BlockSpec((FRAME_TOK, D), lambda i: (i, 0))
    wide = jax.ShapeDtypeStruct((tokens, D), jnp.float32)
    low = jax.ShapeDtypeStruct((tokens, D), low_type)
    return pl.pallas_call(
        project_kernel,
        grid=(tokens // FRAME_TOK,),
        in_specs=[
            pl.BlockSpec((groups, FRAME_TOK, width), lambda i: (0, i, 0)),
            pl.BlockSpec((devices, rows, D), lambda i: (0, FF // D, 0)),
            by_frame,
            pl.BlockSpec((None, 6, D), lambda i: (i, 0, 0)),
        ],
        out_specs=[by_frame] * 4,
        out_shape=[low, wide, wide, low],
        compiler_params=pltpu.CompilerParams(vmem_limit_bytes=40 * 1024 * 1024),
        cost_estimate=about(4),
        name="project_norm",
    )(heads, weights, hidden, mods)


GELU_OUT = math.sqrt(2.0 / math.pi)
GELU_CUBE = 0.044715


def forward_kernel(
    scale_ref,
    mixed_ref,
    expand_ref,
    reduce_ref,
    hidden_ref,
    mods_ref,
    readout_ref,
    noise_ref,
    inner_ref,
    active_ref,
    grad_hidden_ref,
    grad_outer_ref,
    grad_readout_ref,
    grad_gate_ref,
    loss_ref,
    outer_ref,
):
    step = pl.program_id(0)
    frames = mods_ref.shape[0]
    inner = product(mixed_ref[...], flat_weight(expand_ref))
    inner_ref[...] = inner
    bend = jnp.tanh(GELU_OUT * (inner + GELU_CUBE * (inner * inner * inner)))
    active = (0.5 * inner * (1.0 + bend)).astype(low_type)
    active_ref[...] = active
    part = product(active, flat_weight(reduce_ref))

    @pl.when(step == 0)
    def _():
        outer_ref[...] = part

    @pl.when(step > 0)
    def _():
        outer_ref[...] += part

    @pl.when(step == pl.num_programs(0) - 1)
    def _():
        readout = readout_ref[...][:, PATCH_FEAT : 2 * PATCH_FEAT]
        grad_readout = jnp.zeros((D, PATCH_FEAT), jnp.float32)
        for frame in range(frames):
            tokens = slice(frame * FRAME_TOK, (frame + 1) * FRAME_TOK)
            outer = outer_ref[tokens]
            gate = mods_ref[frame, 5:6]
            final, inverse = norm_parts(hidden_ref[tokens] + gate * outer)
            final_low = final.astype(low_type)
            residue = product(final_low, readout) - noise_ref[tokens]
            loss_ref[frame] = jnp.zeros((1, LANES), jnp.float32) + jnp.sum(residue * residue)
            grad_pred = (residue * scale_ref[frame]).astype(low_type)
            grad_readout += across(final_low, grad_pred)
            grad_hidden = norm_back(final, inverse, against(grad_pred, readout))
            grad_hidden_ref[tokens] = grad_hidden
            grad_outer_ref[tokens] = (gate * grad_hidden).astype(low_type)
            grad_gate_ref[frame] = row_sum(grad_hidden * outer)
        grad_readout_ref[...] = grad_readout


def feed_forward(loss_scale, mixed, weights, hidden, mods, first_weights, noise):
    tokens = mixed.shape[0]
    devices, height, _ = weights.shape
    rows = D // devices
    frames = mods.shape[0]
    pieces = FF // D
    wide = jax.ShapeDtypeStruct((tokens, D), jnp.float32)
    by_piece = pl.BlockSpec((tokens, D), lambda k, *_: (0, k))
    return pl.pallas_call(
        forward_kernel,
        grid_spec=pltpu.PrefetchScalarGridSpec(
            num_scalar_prefetch=1,
            grid=(pieces,),
            in_specs=[
                whole((tokens, D)),
                pl.BlockSpec((devices, rows, D), lambda k, *_: (0, pieces + 1 + k, 0)),
                pl.BlockSpec((devices // pieces, pieces * rows, D), lambda k, *_: (k, 0, 0)),
                whole((tokens, D)),
                whole(mods.shape),
                pl.BlockSpec((D, LANES), lambda k, *_: (0, 3 * D // LANES)),
                whole((tokens, PATCH_FEAT)),
            ],
            out_specs=[
                by_piece,
                by_piece,
                whole((tokens, D)),
                whole((tokens, D)),
                whole((D, PATCH_FEAT)),
                whole((frames, 1, D)),
                whole((frames, 1, LANES)),
            ],
            scratch_shapes=[pltpu.VMEM((tokens, D), jnp.float32)],
        ),
        out_shape=[
            jax.ShapeDtypeStruct((tokens, FF), jnp.float32),
            jax.ShapeDtypeStruct((tokens, FF), low_type),
            wide,
            jax.ShapeDtypeStruct((tokens, D), low_type),
            jax.ShapeDtypeStruct((D, PATCH_FEAT), jnp.float32),
            jax.ShapeDtypeStruct((frames, 1, D), jnp.float32),
            jax.ShapeDtypeStruct((frames, 1, LANES), jnp.float32),
        ],
        compiler_params=pltpu.CompilerParams(vmem_limit_bytes=56 * 1024 * 1024),
        cost_estimate=about(20),
        name="feed_forward",
    )(loss_scale, mixed, weights, weights, hidden, mods, first_weights, noise)


def backward_kernel(
    grad_outer_ref,
    reduce_ref,
    expand_ref,
    inner_ref,
    hidden_ref,
    grad_hidden_ref,
    branch_ref,
    mods_ref,
    project_ref,
    grad_inner_ref,
    grad_one_ref,
    grad_branch_ref,
    heads_ref,
    grad_mods_ref,
    grad_mixed_ref,
):
    step = pl.program_id(0)
    frames = mods_ref.shape[0]
    groups, _, width = heads_ref.shape
    inner = inner_ref[...]
    square = inner * inner
    bend = jnp.tanh(GELU_OUT * (inner + GELU_CUBE * (square * inner)))
    slope = 0.5 * (1.0 + bend) + 0.5 * inner * (1.0 - bend * bend) * (
        GELU_OUT * (1.0 + 3.0 * GELU_CUBE * square)
    )
    grad_active = against(grad_outer_ref[...], flat_weight(reduce_ref))
    grad_inner = (grad_active * slope).astype(low_type)
    grad_inner_ref[...] = grad_inner
    part = against(grad_inner, flat_weight(expand_ref))

    @pl.when(step == 0)
    def _():
        grad_mixed_ref[...] = part

    @pl.when(step > 0)
    def _():
        grad_mixed_ref[...] += part

    @pl.when(step == pl.num_programs(0) - 1)
    def _():
        project = flat_weight(project_ref)
        for frame in range(frames):
            tokens = slice(frame * FRAME_TOK, (frame + 1) * FRAME_TOK)
            normed, inverse = norm_parts(hidden_ref[tokens])
            grad_mixed = grad_mixed_ref[tokens]
            grad_mods_ref[frame, 1:2] = row_sum(grad_mixed)
            grad_mods_ref[frame, 2:3] = row_sum(grad_mixed * normed)
            grad_one = grad_hidden_ref[tokens] + norm_back(
                normed, inverse, grad_mixed * (1.0 + mods_ref[frame, 4:5])
            )
            grad_one_ref[tokens] = grad_one
            grad_mods_ref[frame, 0:1] = row_sum(grad_one * branch_ref[tokens])
            grad_branch = (mods_ref[frame, 2:3] * grad_one).astype(low_type)
            grad_branch_ref[tokens] = grad_branch
            grad_attended = against(grad_branch, project).astype(low_type)
            for group in range(groups):
                heads_ref[group, tokens] = grad_attended[:, group * width : (group + 1) * width]


def feed_backward(grad_outer, weights, inner, hidden, grad_hidden, branch, mods, groups):
    tokens = hidden.shape[0]
    devices, height, _ = weights.shape
    rows = D // devices
    frames = mods.shape[0]
    pieces = FF // D
    by_piece = pl.BlockSpec((tokens, D), lambda k: (0, k))
    return pl.pallas_call(
        backward_kernel,
        grid=(pieces,),
        in_specs=[
            whole((tokens, D)),
            pl.BlockSpec((devices // pieces, pieces * rows, D), lambda k: (k, 0, 0)),
            pl.BlockSpec((devices, rows, D), lambda k: (0, pieces + 1 + k, 0)),
            by_piece,
            whole((tokens, D)),
            whole((tokens, D)),
            whole((tokens, D)),
            whole(mods.shape),
            pl.BlockSpec((devices, rows, D), lambda k: (0, pieces, 0)),
        ],
        out_specs=[
            by_piece,
            whole((tokens, D)),
            whole((tokens, D)),
            whole((groups, tokens, D // groups)),
            whole((frames, 3, D)),
        ],
        out_shape=[
            jax.ShapeDtypeStruct((tokens, FF), low_type),
            jax.ShapeDtypeStruct((tokens, D), jnp.float32),
            jax.ShapeDtypeStruct((tokens, D), low_type),
            jax.ShapeDtypeStruct((groups, tokens, D // groups), low_type),
            jax.ShapeDtypeStruct((frames, 3, D), jnp.float32),
        ],
        scratch_shapes=[pltpu.VMEM((tokens, D), jnp.float32)],
        compiler_params=pltpu.CompilerParams(vmem_limit_bytes=58 * 1024 * 1024),
        cost_estimate=about(22),
        name="feed_backward",
    )(grad_outer, weights, weights, inner, hidden, grad_hidden, branch, mods, weights)


def grads_kernel(
    active_ref, grad_outer_ref, attended_ref, grad_branch_ref, mixed_ref, grad_inner_ref, out_ref
):
    cores, lines, height, _ = out_ref.shape
    pieces = FF // D
    rows = height // (2 * pieces + 1)

    def store(start, count, value):
        value = value.astype(low_type)
        for line in range(lines):
            for core in range(cores):
                at = (line * cores + core) * count
                out_ref[core, line, start : start + count] = value[at : at + count]

    store(0, pieces * rows, across(active_ref[...], grad_outer_ref[...]))
    store(pieces * rows, rows, across(attended_ref[...], grad_branch_ref[...]))
    for piece in range(pieces):
        store(
            (pieces + 1 + piece) * rows,
            rows,
            across(mixed_ref[...], grad_inner_ref[:, piece * D : (piece + 1) * D]),
        )


def weight_grads(sizes, active, grad_outer, attended, grad_branch, mixed, grad_inner):
    batch, row, core = sizes
    tokens = mixed.shape[0]
    rows = D // (batch * row * core)
    height = rows * (2 * (FF // D) + 1)
    part = pl.BlockSpec((tokens, D // batch), lambda i: (0, i))
    return pl.pallas_call(
        grads_kernel,
        grid=(batch,),
        in_specs=[
            pl.BlockSpec((tokens, FF // batch), lambda i: (0, i)),
            whole((tokens, D)),
            part,
            whole((tokens, D)),
            part,
            whole((tokens, FF)),
        ],
        out_specs=pl.BlockSpec((None, core, row, height, D), lambda i: (i, 0, 0, 0, 0)),
        out_shape=jax.ShapeDtypeStruct((batch, core, row, height, D), low_type),
        compiler_params=pltpu.CompilerParams(vmem_limit_bytes=56 * 1024 * 1024),
        cost_estimate=about(28),
        name="weight_grads",
    )(active, grad_outer, attended, grad_branch, mixed, grad_inner)


def place_bits():
    bits = []
    for axis in ("core", "row", "batch"):
        by = 1
        while by < lax.axis_size(axis):
            bits.append((axis, by))
            by *= 2
    return bits


def swapped(value, axis, by):
    return lax.ppermute(value, axis, [(i, i ^ by) for i in range(lax.axis_size(axis))])


def gather_near(value):
    for axis, by in place_bits():
        value = jnp.concatenate([value, swapped(value, axis, by)], axis=0)
    return value


def halved_sum(value):
    bits = place_bits()
    value = value.reshape((2,) * len(bits) + value.shape[1:])
    for count, (axis, by) in enumerate(bits):
        mine = (lax.axis_index(axis) // by) % 2
        at = len(bits) - 1 - count
        send = lax.dynamic_index_in_dim(value, 1 - mine, at, keepdims=False)
        keep = lax.dynamic_index_in_dim(value, mine, at, keepdims=False)
        value = keep + swapped(send, axis, by)
    return value


def total_sum(value):
    for axis, by in place_bits():
        value = value + swapped(value, axis, by)
    return value


def exchange_sum(value, axes):
    count = value.shape[0]
    mine = lax.axis_index(axes)
    total = lax.dynamic_index_in_dim(value, mine, 0, keepdims=False)
    value = value.astype(low_type)
    parts = [
        lax.ppermute(
            lax.dynamic_index_in_dim(value, mine ^ offset, 0, keepdims=False),
            axes,
            [(i, i ^ offset) for i in range(count)],
        )
        for offset in range(1, count)
    ]
    for part in parts:
        total = total + part.astype(jnp.float32)
    return total


def per_device(
    clean_latents,
    noise_sample,
    noise_levels,
    clean_flags,
    span_frame,
    patch_master,
    patch_first,
    patch_second,
    level_master,
    level_first,
    level_second,
    adaptive_master,
    adaptive_first,
    adaptive_second,
    triple_master,
    triple_first,
    triple_second,
    project_master,
    project_first,
    project_second,
    expand_master,
    expand_first,
    expand_second,
    reduce_master,
    reduce_first,
    reduce_second,
    readout_master,
    readout_first,
    readout_second,
):
    masters = (
        patch_master,
        level_master,
        adaptive_master,
        triple_master,
        project_master,
        expand_master,
        reduce_master,
        readout_master,
    )
    firsts = (
        patch_first,
        level_first,
        adaptive_first,
        triple_first,
        project_first,
        expand_first,
        reduce_first,
        readout_first,
    )
    seconds = (
        patch_second,
        level_second,
        adaptive_second,
        triple_second,
        project_second,
        expand_second,
        reduce_second,
        readout_second,
    )
    batch_count, row_count, core_count = (lax.axis_size(axis) for axis in ALL)
    batch_index, row_index, core_index = (lax.axis_index(axis) for axis in ALL)
    devices = batch_count * row_count * core_count
    rows = D // devices
    token_count = clean_latents.shape[1]
    frame_local = token_count // FRAME_TOK

    moved = batch_count == row_count and HEADS % (batch_count * core_count) == 0
    if moved:
        clip_index, chunk_index = row_index, batch_index * core_count + core_index
        head_axes, head_groups = ("batch", "core"), batch_count * core_count
        rest_axes = ("row",)
    else:
        clip_index, chunk_index = batch_index, row_index * core_count + core_index
        head_axes, head_groups = ("row",), row_count
        rest_axes = ("batch", "core")
    owner_index = (batch_index * row_count + row_index) * core_count + core_index

    both = jnp.concatenate([clean_latents[0], noise_sample[0]], axis=1)
    if moved:
        turn = [
            (
                (a * row_count + b) * core_count + c,
                (b * row_count + a) * core_count + c,
            )
            for a in range(batch_count)
            for b in range(row_count)
            for c in range(core_count)
        ]
        both = lax.ppermute(both, ALL, turn)
    clean_tok, noise_tok = both[:, :PATCH_FEAT], both[:, PATCH_FEAT:]

    first_weights = jnp.concatenate(
        [
            triple_master.astype(low_type),
            jnp.transpose(patch_master).astype(low_type),
            readout_master.astype(low_type),
            jnp.zeros((rows, LANES - 2 * PATCH_FEAT), low_type),
        ],
        axis=1,
    )
    first_weights = lax.all_gather(first_weights, ALL, axis=0, tiled=True)
    second_weights = jnp.concatenate(
        [reduce_master.astype(low_type), project_master.astype(low_type)]
        + [expand_master[:, k * D : (k + 1) * D].astype(low_type) for k in range(FF // D)],
        axis=0,
    )
    second_weights = lax.all_gather(second_weights, ALL, axis=0)

    levels_all = noise_levels.reshape(-1)
    flags_all = clean_flags.reshape(-1)
    _, _, index_all = plan(levels_all, flags_all)
    if moved:
        order_all = lambda v: (
            v.reshape((row_count, batch_count, core_count, frame_local) + v.shape[1:])
            .swapaxes(0, 1)
            .reshape(v.shape)
        )
    else:
        order_all = lambda v: v
    index_all = order_all(index_all)
    place = jnp.arange(devices, dtype=jnp.int32)
    index_near = jnp.sum(
        jnp.where(
            ((owner_index ^ place)[:, None] == place[None, :])[..., None],
            index_all.reshape(1, devices, frame_local),
            0,
        ),
        axis=1,
    ).reshape(-1)
    table_low = level_master.astype(low_type).astype(jnp.float32)

    def table_rows(index):
        hot = (index[:, None] == jnp.arange(NB + 1, dtype=jnp.int32)[None, :]).astype(jnp.float32)
        return hot, jnp.dot(hot, table_low, precision=lax.Precision.HIGHEST)

    _, pre_own = table_rows(index_all)
    hot_near, pre_near = table_rows(index_near)
    cond_near, silu_back = jax.vjp(jax.nn.silu, pre_near)
    cond_near = cond_near.astype(low_type)
    cond_own = jax.nn.silu(pre_own).astype(low_type)
    adaptive_low = adaptive_master.astype(low_type)
    adapt_parts = lax.all_to_all(
        product(cond_own, adaptive_low).reshape(devices, frame_local, 6 * D), ALL, 0, 0, tiled=True
    )
    adapt = jnp.sum(adapt_parts, axis=0)
    shift_one, scale_one = adapt[:, :D], adapt[:, D : 2 * D]
    mods = adapt.reshape(frame_local, 6, D)

    my_levels = lax.dynamic_slice_in_dim(
        lax.dynamic_index_in_dim(noise_levels, clip_index, 0, keepdims=False),
        chunk_index * frame_local,
        frame_local,
    )
    my_flags = lax.dynamic_slice_in_dim(
        lax.dynamic_index_in_dim(clean_flags, clip_index, 0, keepdims=False),
        chunk_index * frame_local,
        frame_local,
    )
    my_frames = lax.dynamic_slice_in_dim(span_frame, chunk_index * frame_local, frame_local)
    if moved:
        query_frames = key_frames = span_frame
    else:
        by_chunk = span_frame.reshape(row_count, core_count, frame_local)
        query_frames = lax.dynamic_index_in_dim(by_chunk, core_index, 1, keepdims=False).reshape(-1)
        key_frames = by_chunk.swapaxes(0, 1).reshape(-1)
    query_total, key_total = query_frames.shape[0], key_frames.shape[0]
    earlier = jnp.sum(key_frames[None, :] < key_frames[:, None], axis=1)
    key_order = jnp.sum(
        jnp.where(earlier[:, None] == jnp.arange(key_total)[None, :], jnp.arange(key_total)[:, None], 0),
        axis=0,
    ).astype(jnp.int32)
    key_count = jnp.sum(key_frames[None, :] <= query_frames[:, None], axis=1).astype(jnp.int32)
    later = jnp.sum(query_frames[None, :] > query_frames[:, None], axis=1)
    query_order = jnp.sum(
        jnp.where(later[:, None] == jnp.arange(query_total)[None, :], jnp.arange(query_total)[:, None], 0),
        axis=0,
    ).astype(jnp.int32)
    query_count = jnp.sum(query_frames[None, :] >= key_frames[:, None], axis=1).astype(jnp.int32)
    my_times, query_times, key_times = (
        time_tables(my_frames),
        time_tables(query_frames),
        time_tables(key_frames),
    )
    spaces = space_tables()

    alpha_bar, noised, _ = plan(my_levels, my_flags)
    inputs = noised_input(clean_tok, noise_tok, alpha_bar, noised).astype(low_type)
    patch_turned = first_weights[:, 3 * D : 3 * D + PATCH_FEAT]
    triple_weight = first_weights
    hidden_zero = against(inputs, patch_turned)
    normed, first_back = jax.vjp(modulate, hidden_zero, shift_one, scale_one)
    normed_low = normed.astype(low_type)

    width = D // head_groups
    heads = triple_heads(normed_low, triple_weight, my_times, spaces, head_groups)
    heads = lax.all_to_all(heads, head_axes, 0, 0, tiled=True)
    if moved:
        heads = heads.reshape(head_groups, frame_local, FRAME_TOK, 3 * width)
        items = (heads, heads, heads)
    else:
        heads = heads.reshape(head_groups, 3, frame_local, FRAME_TOK, width)
        items = (heads[:, 0],) + tuple(
            lax.all_gather(heads[:, part], "core", axis=0, tiled=True) for part in (1, 2)
        )
    attended, flat, logs = attend(key_order, key_count, items, width)
    attended = attended.reshape(head_groups, token_count, width)
    attended = lax.all_to_all(attended, head_axes, 0, 0, tiled=True)
    attended, normed_low = lax.optimization_barrier((attended, normed_low))
    normed_clip = lax.all_gather(normed_low, head_axes, axis=0, tiled=True)
    attended_low, branch, hidden_one, mixed_low = project_norm(
        attended, second_weights, hidden_zero, mods
    )
    frame_count = jnp.sum((1 - clean_flags).astype(jnp.float32))
    loss_scale = noised * (2.0 / (FRAME_TOK * PATCH_FEAT)) / jnp.maximum(frame_count, 1.0)
    (
        inner,
        active_low,
        grad_hidden_two,
        grad_outer,
        grad_readout,
        grad_gate_two,
        squared,
    ) = feed_forward(
        loss_scale, mixed_low, second_weights, hidden_one, mods, first_weights, noise_tok
    )
    frame_loss = squared[:, 0, 0] * (1.0 / (FRAME_TOK * PATCH_FEAT)) * noised
    grad_inner_low, grad_hidden_one, grad_branch, grad_attended, grad_mods = feed_backward(
        grad_outer,
        second_weights,
        inner,
        hidden_one,
        grad_hidden_two,
        branch,
        mods,
        head_groups,
    )
    grad_attended = lax.all_to_all(grad_attended, head_axes, 0, 0, tiled=True)
    grad_attended = grad_attended.reshape(head_groups, frame_local, FRAME_TOK, width)
    early_adapt = jnp.concatenate(
        [grad_mods.reshape(frame_local, 3 * D), grad_gate_two.reshape(frame_local, D)], axis=1
    ).astype(low_type)
    early_adapt = gather_near(early_adapt)

    second_grads = weight_grads(
        (batch_count, row_count, core_count),
        active_low,
        grad_outer,
        attended_low,
        grad_branch,
        mixed_low,
        grad_inner_low,
    )
    second_own = lax.psum_scatter(
        second_grads.reshape((-1,) + second_grads.shape[2:]),
        ("batch", "core"),
        scatter_dimension=0,
    )
    second_own = lax.psum_scatter(second_own, "row", scatter_dimension=0).astype(jnp.float32)

    grads = attend_back(
        query_order,
        query_count,
        items,
        grad_attended,
        flat,
        logs,
        query_times,
        key_times,
        spaces,
    )
    if moved:
        grad_heads = grads[0].reshape(head_groups, token_count, 3 * width)
    else:
        grad_heads = [grads[0]] + [
            lax.psum_scatter(
                item.astype(jnp.float32), "core", scatter_dimension=0, tiled=True
            ).astype(low_type)
            for item in grads[1:]
        ]
        grad_heads = jnp.concatenate(grad_heads, axis=-1).reshape(
            head_groups, token_count, 3 * width
        )
    grad_triple = across(
        normed_clip.reshape(-1, D), grad_heads.reshape(head_groups * token_count, 3 * width)
    )
    grad_heads = lax.all_to_all(grad_heads, head_axes, 0, 0, tiled=True)
    grad_triple_tok = (
        grad_heads.reshape(head_groups, token_count, 3, width)
        .transpose(1, 2, 0, 3)
        .reshape(token_count, 3 * D)
    )
    hidden_part, grad_shift_one, grad_scale_one = first_back(
        against(grad_triple_tok, triple_weight[:, : 3 * D])
    )
    late_adapt = gather_near(
        jnp.concatenate([grad_shift_one, grad_scale_one], axis=1).astype(low_type)
    )
    grad_hidden_zero = (grad_hidden_one + hidden_part).astype(low_type)
    grad_patch = across(grad_hidden_zero, inputs)
    small_own = halved_sum(
        jnp.concatenate([grad_patch, grad_readout], axis=1).reshape(devices, -1, LANES)
    ).reshape(rows, 2 * PATCH_FEAT)

    grad_triple = grad_triple.reshape(batch_count, row_count, core_count, rows, 3 * width)
    if moved:
        grad_triple = grad_triple.transpose(1, 0, 2, 3, 4)
    else:
        grad_triple = grad_triple.transpose(0, 2, 1, 3, 4)
    rest_count = devices // head_groups
    triple_own = exchange_sum(
        grad_triple.reshape(rest_count, head_groups, rows, 3 * width), rest_axes
    )
    triple_own = lax.all_to_all(triple_own, head_axes, 0, 0, tiled=True)
    triple_own = (
        triple_own.reshape(head_groups, rows, 3, width).transpose(1, 2, 0, 3).reshape(rows, 3 * D)
    )
    early_columns = 2 * D
    adapt_own = jnp.concatenate(
        [across(cond_near, late_adapt), across(cond_near, early_adapt)], axis=1
    )
    grad_cond = against(late_adapt, adaptive_low[:, :early_columns]) + against(
        early_adapt, adaptive_low[:, early_columns:]
    )
    (grad_pre,) = silu_back(grad_cond)
    table_own = lax.dot_general(
        hot_near,
        grad_pre,
        (((0,), (0,)), ((), ())),
        precision=lax.Precision.HIGHEST,
        preferred_element_type=jnp.float32,
    )
    expand_own = jnp.concatenate(
        [
            second_own[(FF // D + 1 + k) * rows : (FF // D + 2 + k) * rows]
            for k in range(FF // D)
        ],
        axis=1,
    )
    reduced = (
        jnp.transpose(small_own[:, :PATCH_FEAT]),
        table_own,
        adapt_own,
        triple_own,
        second_own[FF // D * rows : (FF // D + 1) * rows],
        expand_own,
        second_own[: FF // D * rows],
        small_own[:, PATCH_FEAT:],
    )
    squares = sum((jnp.sum(gradient * gradient) for gradient in reduced))
    level_hits = (my_levels[:, None] == jnp.arange(NB, dtype=jnp.int32)[None, :]).astype(
        jnp.float32
    )
    bucket_local = jnp.sum(level_hits * frame_loss[:, None], axis=0)
    sums = jnp.zeros((8, LANES), jnp.float32)
    sums = sums.at[0, :NB].set(bucket_local)
    sums = sums.at[1, 0].set(squares)
    sums = sums.at[2, 0].set(jnp.sum(frame_loss))
    sums = total_sum(sums)
    clip_norm = jnp.sqrt(sums[1, 0])
    factor = jnp.minimum(1.0, clip_bound / clip_norm)
    new = [
        adamw_update(
            masters[item], firsts[item], seconds[item], reduced[item], factor, learn_rates[item]
        )
        for item in range(8)
    ]
    return (sums[2, 0], frame_count, sums[0, :NB], clip_norm) + tuple(
        item for triple in new for item in triple
    )


def solution(mesh):
    in_specs = (
        P("batch", ("row", "core"), None),
        P("batch", ("row", "core"), None),
        P(),
        P(),
        P(),
        P(None, ALL),
        P(None, ALL),
        P(None, ALL),
        P(None, ALL),
        P(None, ALL),
        P(None, ALL),
        P(ALL, None),
        P(ALL, None),
        P(ALL, None),
        P(ALL, None),
        P(ALL, None),
        P(ALL, None),
        P(ALL, None),
        P(ALL, None),
        P(ALL, None),
        P(ALL, None),
        P(ALL, None),
        P(ALL, None),
        P(ALL, None),
        P(ALL, None),
        P(ALL, None),
        P(ALL, None),
        P(ALL, None),
        P(ALL, None),
    )
    out_specs = (
        P(),
        P(),
        P(),
        P(),
        P(None, ALL),
        P(None, ALL),
        P(None, ALL),
        P(None, ALL),
        P(None, ALL),
        P(None, ALL),
        P(ALL, None),
        P(ALL, None),
        P(ALL, None),
        P(ALL, None),
        P(ALL, None),
        P(ALL, None),
        P(ALL, None),
        P(ALL, None),
        P(ALL, None),
        P(ALL, None),
        P(ALL, None),
        P(ALL, None),
        P(ALL, None),
        P(ALL, None),
        P(ALL, None),
        P(ALL, None),
        P(ALL, None),
        P(ALL, None),
    )
    batch_size, blk_size = mesh.shape["batch"], mesh.shape["blk"]
    inner = Mesh(mesh.devices.reshape(batch_size, blk_size // 2, 2), ALL)
    return jax.shard_map(
        per_device, mesh=inner, in_specs=in_specs, out_specs=out_specs, check_vma=False
    )
```

```python
import functools
import math

import jax
import jax.numpy as jnp
from jax import lax
from jax.experimental import pallas as pl
from jax.experimental.pallas import tpu as pltpu
from jax.sharding import Mesh
from jax.sharding import PartitionSpec as P

D = 1024
HEADS = 16
HEAD_DIM = 64
FF = 4096
PATCH_FEAT = 16
FRAME_TOK = 256
SIDE = 16
NB = 32
STEP = 10
LANES = 128
ALL = ("batch", "row", "core")


learn_rates = (0.5, 2.0, 0.05, 0.05, 0.5, 0.05, 0.05, 0.05)
beta_first = 0.9
beta_second = 0.999
decay_rate = 0.01
adam_floor = 1e-08
clip_bound = 0.02
low_type = jnp.bfloat16


def product(left, right):
    return jnp.dot(left, right, preferred_element_type=jnp.float32)


def across(left, right):
    return lax.dot_general(
        left, right, (((0,), (0,)), ((), ())), preferred_element_type=jnp.float32
    )


def against(left, right):
    return lax.dot_general(
        left, right, (((1,), (1,)), ((), ())), preferred_element_type=jnp.float32
    )


def plan(levels, clean_flags):
    alpha_bar = jnp.cos(0.5 * math.pi * (levels.astype(jnp.float32) + 1.0) / (NB + 1.0)) ** 2
    noised = (1 - clean_flags).astype(jnp.float32)
    table_index = jnp.where(clean_flags == 1, 0, levels + 1)
    return (alpha_bar, noised, table_index)


def noised_input(clean_tok, noise_tok, alpha_bar, noised):
    frame_shape = (alpha_bar.shape[0], -1, clean_tok.shape[-1])
    clean_frames = clean_tok.reshape(frame_shape)
    noise_frames = noise_tok.reshape(frame_shape)
    mixed_tok = (
        jnp.sqrt(alpha_bar)[:, None, None] * clean_frames
        + jnp.sqrt(1.0 - alpha_bar)[:, None, None] * noise_frames
    )
    return jnp.where(noised[:, None, None] > 0.5, mixed_tok, clean_frames).reshape(clean_tok.shape)


def adamw_update(master, first_moment, second_moment, gradient, factor, step_rate):
    clipped = gradient * factor
    first_new = beta_first * first_moment + (1.0 - beta_first) * clipped
    second_new = beta_second * second_moment + (1.0 - beta_second) * clipped * clipped
    first_hat = first_new / (1.0 - beta_first**STEP)
    second_hat = second_new / (1.0 - beta_second**STEP)
    master_new = master - step_rate * (
        first_hat / (jnp.sqrt(second_hat) + adam_floor) + decay_rate * master
    )
    return (first_new, second_new, master_new)


def lane_places():
    lane = jnp.arange(LANES, dtype=jnp.int32) % HEAD_DIM
    half = HEAD_DIM // 2
    place = lane % half
    time_count = HEAD_DIM // 8
    space_count = 3 * HEAD_DIM // 16
    sign = jnp.where(lane < half, -1.0, 1.0)
    time_freq = 10000.0 ** (-(place.astype(jnp.float32)) / time_count)
    space_place = jnp.where(place < time_count + space_count, place - time_count, place - time_count - space_count)
    space_freq = 100.0 ** (-(space_place.astype(jnp.float32)) / space_count)
    is_time = place < time_count
    is_row = (place >= time_count) & (place < time_count + space_count)
    return sign, time_freq, space_freq, is_time, is_row


def time_tables(frames):
    sign, time_freq, _, is_time, _ = lane_places()
    angle = frames.astype(jnp.float32)[:, None] * time_freq[None]
    return (
        jnp.where(is_time, jnp.cos(angle), 0.0)[:, None],
        jnp.where(is_time, jnp.sin(angle) * sign, 0.0)[:, None],
    )


def space_tables():
    sign, _, space_freq, is_time, is_row = lane_places()
    token = jnp.arange(FRAME_TOK, dtype=jnp.int32)
    row_pos = (token // SIDE).astype(jnp.float32)[:, None]
    col_pos = (token % SIDE).astype(jnp.float32)[:, None]
    angle = jnp.where(is_row[None], row_pos, col_pos) * space_freq[None]
    return (
        jnp.where(is_time, 0.0, jnp.cos(angle)),
        jnp.where(is_time, 0.0, jnp.sin(angle) * sign),
    )


def partner(value):
    half = HEAD_DIM // 2
    width = value.shape[1]
    if width == LANES:
        lane = lax.broadcasted_iota(jnp.int32, value.shape, 1)
        ahead = pltpu.roll(value, width - half, 1)
        behind = pltpu.roll(value, half, 1)
        return jnp.where(lane % HEAD_DIM < half, ahead, behind)
    return jnp.concatenate([value[:, half:], value[:, :half]], axis=1)


def norm_parts(hidden):
    centred = hidden - jnp.mean(hidden, axis=-1, keepdims=True)
    variance = jnp.mean(centred * centred, axis=-1, keepdims=True)
    inverse = lax.rsqrt(variance + 1e-06)
    return centred * inverse, inverse


def norm_back(normed, inverse, grad):
    along = jnp.mean(grad * normed, axis=-1, keepdims=True)
    return inverse * (grad - jnp.mean(grad, axis=-1, keepdims=True) - normed * along)


def row_sum(value):
    return jnp.sum(value, axis=0, keepdims=True)


def triple_kernel(
    inputs_ref,
    extra_ref,
    mods_ref,
    weight_ref,
    time_cos,
    time_sin,
    space_cos,
    space_sin,
    hidden_ref,
    normed_ref,
    out_ref,
):
    column = pl.program_id(0)
    width = out_ref.shape[-1]
    frames = mods_ref.shape[0]

    @pl.when(column == 0)
    def _():
        patch = extra_ref[...][:, :PATCH_FEAT]
        for frame in range(frames):
            tokens = slice(frame * FRAME_TOK, (frame + 1) * FRAME_TOK)
            hidden = against(inputs_ref[tokens], patch)
            hidden_ref[tokens] = hidden
            normed, _ = norm_parts(hidden)
            normed_ref[tokens] = (
                normed * (1.0 + mods_ref[frame, 1:2]) + mods_ref[frame, 0:1]
            ).astype(low_type)

    acc = product(normed_ref[...], weight_ref[...])
    per_block = acc.shape[1] // LANES

    def store(piece, values):
        for part in range(LANES // width):
            at = piece * (LANES // width) + part
            done = values[:, part * width : (part + 1) * width].astype(low_type)
            if len(out_ref.shape) == 3:
                out_ref[at] = done
            else:
                out_ref[at, 0] = done

    turned = column < 2 * D // acc.shape[1]

    @pl.when(turned)
    def _():
        for piece in range(per_block):
            done = []
            for frame in range(frames):
                value = acc[
                    frame * FRAME_TOK : (frame + 1) * FRAME_TOK,
                    piece * LANES : (piece + 1) * LANES,
                ]
                cosine = time_cos[frame] + space_cos[...]
                sine = time_sin[frame] + space_sin[...]
                done.append(value * cosine + partner(value) * sine)
            store(piece, jnp.concatenate(done, axis=0))

    @pl.when(jnp.logical_not(turned))
    def _():
        for piece in range(per_block):
            store(piece, acc[:, piece * LANES : (piece + 1) * LANES])


BLOCK = 256


def heads_layout(groups, tokens):
    width = D // groups
    per_block = BLOCK // width
    per_part = D // BLOCK
    if width == LANES:
        return (groups, tokens, 3 * width), pl.BlockSpec(
            (per_block, tokens, width), lambda j: (j % per_part, 0, j // per_part)
        )
    return (groups, 3, tokens, width), pl.BlockSpec(
        (per_block, 1, tokens, width), lambda j: (j % per_part, j // per_part, 0, 0)
    )


def triple_heads(inputs, mods, weight, times, spaces, groups):
    tokens = inputs.shape[0]
    shape, spec = heads_layout(groups, tokens)
    return pl.pallas_call(
        triple_kernel,
        grid=(3 * D // BLOCK,),
        in_specs=[
            whole(inputs.shape),
            pl.BlockSpec((D, LANES), lambda j: (0, 3 * D // LANES)),
            whole(mods.shape),
            pl.BlockSpec((D, BLOCK), lambda j: (0, j)),
            whole(times[0].shape),
            whole(times[1].shape),
            whole(spaces[0].shape),
            whole(spaces[1].shape),
        ],
        out_specs=[whole((tokens, D)), whole((tokens, D)), spec],
        out_shape=[
            jax.ShapeDtypeStruct((tokens, D), jnp.float32),
            jax.ShapeDtypeStruct((tokens, D), low_type),
            jax.ShapeDtypeStruct(shape, low_type),
        ],
        compiler_params=pltpu.CompilerParams(vmem_limit_bytes=40 * 1024 * 1024),
        cost_estimate=about(12),
        name="triple_heads",
    )(inputs, weight, mods, weight, *times, *spaces)


def triple_back_kernel(
    grads_ref,
    weight_ref,
    hidden_ref,
    grad_one_ref,
    mods_ref,
    inputs_ref,
    grad_mods_ref,
    grad_patch_ref,
    sum_ref,
):
    step = pl.program_id(0)
    frames = mods_ref.shape[0]
    pieces = range(grads_ref.shape[0])
    if len(grads_ref.shape) == 3:
        grads = jnp.concatenate([grads_ref[piece] for piece in pieces], axis=1)
    else:
        grads = jnp.concatenate([grads_ref[piece, 0] for piece in pieces], axis=1)
    part = against(grads, weight_ref[...])

    @pl.when(step == 0)
    def _():
        sum_ref[...] = part

    @pl.when(step > 0)
    def _():
        sum_ref[...] += part

    @pl.when(step == pl.num_programs(0) - 1)
    def _():
        grad_patch = jnp.zeros((D, PATCH_FEAT), jnp.float32)
        for frame in range(frames):
            tokens = slice(frame * FRAME_TOK, (frame + 1) * FRAME_TOK)
            normed, inverse = norm_parts(hidden_ref[tokens])
            grad_normed = sum_ref[tokens]
            grad_mods_ref[frame, 0:1] = row_sum(grad_normed)
            grad_mods_ref[frame, 1:2] = row_sum(grad_normed * normed)
            grad_hidden = grad_one_ref[tokens] + norm_back(
                normed, inverse, grad_normed * (1.0 + mods_ref[frame, 1:2])
            )
            grad_patch += across(grad_hidden.astype(low_type), inputs_ref[tokens])
        grad_patch_ref[...] = grad_patch


def triple_back(grads, weight, hidden, grad_one, mods, inputs, groups):
    tokens = inputs.shape[0]
    frames = mods.shape[0]
    return pl.pallas_call(
        triple_back_kernel,
        grid=(3 * D // BLOCK,),
        in_specs=[
            heads_layout(groups, tokens)[1],
            pl.BlockSpec((D, BLOCK), lambda j: (0, j)),
            whole(hidden.shape),
            whole(hidden.shape),
            whole(mods.shape),
            whole(inputs.shape),
        ],
        out_specs=[whole((frames, 2, D)), whole((D, PATCH_FEAT))],
        out_shape=[
            jax.ShapeDtypeStruct((frames, 2, D), jnp.float32),
            jax.ShapeDtypeStruct((D, PATCH_FEAT), jnp.float32),
        ],
        scratch_shapes=[pltpu.VMEM((tokens, D), jnp.float32)],
        compiler_params=pltpu.CompilerParams(vmem_limit_bytes=40 * 1024 * 1024),
        cost_estimate=about(12),
        name="triple_back",
    )(grads, weight, hidden, grad_one, mods, inputs)


def head_stack(value):
    count = value.shape[1] // HEAD_DIM
    if count == 1:
        return value
    lane = lax.broadcasted_iota(jnp.int32, value.shape, 1)
    zero = jnp.zeros_like(value)
    return jnp.concatenate(
        [jnp.where(lane // HEAD_DIM == head, value, zero) for head in range(count)], axis=0
    )


UNROLL = 4


def unrolled(count, body, carry):
    def several(base, now):
        for offset in range(UNROLL):
            now = body(base * UNROLL + offset, now)
        return now

    whole_part = count // UNROLL
    carry = lax.fori_loop(0, whole_part, several, carry)
    return lax.fori_loop(whole_part * UNROLL, count, body, carry)


def attend_kernel(
    order_ref,
    count_ref,
    query_ref,
    key_ref,
    value_ref,
    out_ref,
    flat_ref,
    log_ref,
    turned_ref,
    scores_ref,
):
    step = pl.program_id(0)
    chunks, per_chunk = key_ref.shape[0], key_ref.shape[1]
    width = key_ref.shape[-1]
    heads = width // HEAD_DIM
    span = heads * FRAME_TOK

    @pl.when(step == 0)
    def _():
        def turn(chunk, carry):
            for part in range(per_chunk):
                turned_ref[chunk, part] = jnp.transpose(value_ref[chunk, part])
            return carry

        lax.fori_loop(0, chunks, turn, 0)

    queries = jnp.transpose(head_stack(query_ref[...] * jnp.asarray(HEAD_DIM**-0.5, low_type)))
    count = count_ref[step]

    def by_eight(value):
        return value.reshape(FRAME_TOK // 8, 8, span)

    def score(place, top):
        frame = order_ref[place]
        scores = product(key_ref[frame // per_chunk, frame % per_chunk], queries)
        scores_ref[place] = scores
        return jnp.maximum(top, jnp.max(by_eight(scores), axis=0))

    top = unrolled(count, score, jnp.full((8, span), -1e30, jnp.float32))
    top = jnp.max(top, axis=0, keepdims=True)

    def weigh(place, carry):
        total, sums = carry
        frame = order_ref[place]
        chances = jnp.exp(scores_ref[place] - top)
        total = total + jnp.sum(by_eight(chances), axis=0)
        chances = chances.astype(low_type)
        new_sums = []
        for head in range(heads):
            values = turned_ref[
                frame // per_chunk,
                frame % per_chunk,
                head * HEAD_DIM : (head + 1) * HEAD_DIM,
                :,
            ]
            columns = slice(head * FRAME_TOK, (head + 1) * FRAME_TOK)
            new_sums.append(sums[head] + product(values, chances[:, columns]))
        return total, tuple(new_sums)

    initial = (
        jnp.zeros((8, span), jnp.float32),
        tuple(jnp.zeros((HEAD_DIM, FRAME_TOK), jnp.float32) for _ in range(heads)),
    )
    total, sums = unrolled(count, weigh, initial)
    total = jnp.sum(total, axis=0, keepdims=True)
    log_ref[...] = top + jnp.log(total)
    inverse = 1.0 / total
    result = jnp.concatenate(
        [
            sums[head] * inverse[:, head * FRAME_TOK : (head + 1) * FRAME_TOK]
            for head in range(heads)
        ],
        axis=0,
    )
    flat_ref[...] = result
    out_ref[...] = jnp.transpose(result).astype(low_type)


def about(microseconds):
    return pl.CostEstimate(
        flops=microseconds * 1_100_000_000, bytes_accessed=1 << 20, transcendentals=0
    )


def whole(shape):
    return pl.BlockSpec(shape, lambda *_: (0,) * len(shape))


def lanes_of(items, width):
    joint = items[0].shape[-1] != width
    return [place if joint else 0 for place in range(3)]


def attend(order, count, items, width):
    chunks, per_chunk = items[0].shape[:2]
    key_chunks = items[1].shape[0]
    frames = chunks * per_chunk
    span = width // HEAD_DIM * FRAME_TOK
    lane = lanes_of(items, width)
    return pl.pallas_call(
        attend_kernel,
        grid_spec=pltpu.PrefetchScalarGridSpec(
            num_scalar_prefetch=2,
            grid=(frames,),
            in_specs=[
                pl.BlockSpec(
                    (None, None, FRAME_TOK, width),
                    lambda i, *_: (i // per_chunk, i % per_chunk, 0, lane[0]),
                ),
                pl.BlockSpec(
                    (key_chunks, per_chunk, FRAME_TOK, width), lambda i, *_: (0, 0, 0, lane[1])
                ),
                pl.BlockSpec(
                    (key_chunks, per_chunk, FRAME_TOK, width), lambda i, *_: (0, 0, 0, lane[2])
                ),
            ],
            out_specs=[
                pl.BlockSpec(
                    (None, None, FRAME_TOK, width),
                    lambda i, *_: (i // per_chunk, i % per_chunk, 0, 0),
                ),
                pl.BlockSpec((None, width, FRAME_TOK), lambda i, *_: (i, 0, 0)),
                pl.BlockSpec((None, 1, span), lambda i, *_: (i, 0, 0)),
            ],
            scratch_shapes=[
                pltpu.VMEM((key_chunks, per_chunk, width, FRAME_TOK), low_type),
                pltpu.VMEM((key_chunks * per_chunk, FRAME_TOK, span), jnp.float32),
            ],
        ),
        out_shape=[
            jax.ShapeDtypeStruct((chunks, per_chunk, FRAME_TOK, width), low_type),
            jax.ShapeDtypeStruct((frames, width, FRAME_TOK), jnp.float32),
            jax.ShapeDtypeStruct((frames, 1, span), jnp.float32),
        ],
        compiler_params=pltpu.CompilerParams(vmem_limit_bytes=48 * 1024 * 1024),
        cost_estimate=about(45),
        name="attend",
    )(order, count, *items)


def attend_back_kernel(
    order_ref,
    count_ref,
    query_ref,
    key_ref,
    value_ref,
    grad_ref,
    flat_ref,
    log_ref,
    query_cos,
    query_sin,
    key_cos,
    key_sin,
    space_cos,
    space_sin,
    *rest,
):
    outs, (stacked_query, stacked_grad, row_dot, sums_ref) = rest[:-4], rest[-4:]
    step = pl.program_id(0)
    frames, width, _ = flat_ref.shape
    per_chunk = query_ref.shape[1]
    heads = width // HEAD_DIM
    scale = HEAD_DIM**-0.5

    @pl.when(step == 0)
    def _():
        def ready(frame, carry):
            chunk, part = frame // per_chunk, frame % per_chunk
            query = query_ref[chunk, part] * jnp.asarray(scale, low_type)
            stacked_query[frame] = head_stack(query)
            grad = grad_ref[chunk, part]
            stacked_grad[frame] = head_stack(grad)
            both = jnp.transpose(grad.astype(jnp.float32)) * flat_ref[frame]
            row_dot[frame] = jnp.concatenate(
                [
                    jnp.sum(both[head * HEAD_DIM : (head + 1) * HEAD_DIM], axis=0, keepdims=True)
                    for head in range(heads)
                ],
                axis=1,
            )
            sums_ref[frame] = jnp.zeros((width, FRAME_TOK), jnp.float32)
            return carry

        lax.fori_loop(0, frames, ready, 0)

    keys = key_ref[...]
    values = value_ref[...]
    turned_keys = jnp.transpose(keys)

    def several(base, count, carry):
        grad_keys, grad_values = carry
        frames_now = [order_ref[base + i] for i in range(count)]
        updates = []
        scores = [against(keys, stacked_query[frame]) for frame in frames_now]
        grad_chances = [against(values, stacked_grad[frame]) for frame in frames_now]
        for frame, score, grad_chance in zip(frames_now, scores, grad_chances):
            chances = jnp.exp(score - log_ref[frame])
            grad_scores = (chances * (grad_chance - row_dot[frame])).astype(low_type)
            grad_values = grad_values + product(chances.astype(low_type), stacked_grad[frame])
            grad_keys = grad_keys + product(grad_scores, stacked_query[frame])
            for head in range(heads):
                rows = slice(head * HEAD_DIM, (head + 1) * HEAD_DIM)
                updates.append(
                    product(
                        turned_keys[rows],
                        grad_scores[:, head * FRAME_TOK : (head + 1) * FRAME_TOK],
                    )
                )
        for i, frame in enumerate(frames_now):
            for head in range(heads):
                rows = slice(head * HEAD_DIM, (head + 1) * HEAD_DIM)
                sums_ref[frame, rows, :] += updates[i * heads + head]
        return grad_keys, grad_values

    zero = jnp.zeros((FRAME_TOK, width), jnp.float32)
    total = count_ref[step]
    carry = lax.fori_loop(
        0, total // UNROLL, lambda i, c: several(i * UNROLL, UNROLL, c), (zero, zero)
    )
    grad_keys, grad_values = lax.fori_loop(
        total // UNROLL * UNROLL, total, lambda i, c: several(i, 1, c), carry
    )
    space_c, space_s = space_cos[:, :width], space_sin[:, :width]

    def store(part, frame, value):
        place = (frame // per_chunk, frame % per_chunk)
        if len(outs) == 1:
            outs[0][place + (slice(None), slice(part * width, (part + 1) * width))] = value
        else:
            outs[part][place] = value

    store(2, step, grad_values.astype(low_type))
    store(
        1,
        step,
        (
            grad_keys * (key_cos[:, :width] + space_c)
            - partner(grad_keys) * (key_sin[:, :width] + space_s)
        ).astype(low_type),
    )

    @pl.when(step == pl.num_programs(0) - 1)
    def _():
        def finish(frame, carry):
            value = jnp.transpose(sums_ref[frame]) * scale
            store(
                0,
                frame,
                (
                    value * (query_cos[frame][:, :width] + space_c)
                    - partner(value) * (query_sin[frame][:, :width] + space_s)
                ).astype(low_type),
            )
            return carry

        lax.fori_loop(0, frames, finish, 0)


def attend_back(order, count, items, grads, flat, logs, query_times, key_times, spaces):
    per_chunk, width = grads.shape[1], grads.shape[3]
    frames = flat.shape[0]
    key_frames = items[1].shape[0] * per_chunk
    span = width // HEAD_DIM * FRAME_TOK
    lane = lanes_of(items, width)

    def key_spec(place):
        return pl.BlockSpec(
            (None, None, FRAME_TOK, width), lambda i, *_: (i // per_chunk, i % per_chunk, 0, place)
        )

    key_time = pl.BlockSpec((None, 1, LANES), lambda i, *_: (i, 0, 0))
    if lane[1]:
        shapes = [items[0].shape]
    else:
        shapes = [item.shape for item in items]
    return pl.pallas_call(
        attend_back_kernel,
        grid_spec=pltpu.PrefetchScalarGridSpec(
            num_scalar_prefetch=2,
            grid=(key_frames,),
            in_specs=[
                whole(grads.shape),
                key_spec(lane[1]),
                key_spec(lane[2]),
                whole(grads.shape),
                whole(flat.shape),
                whole(logs.shape),
                whole(query_times[0].shape),
                whole(query_times[1].shape),
                key_time,
                key_time,
                whole(spaces[0].shape),
                whole(spaces[1].shape),
            ],
            out_specs=[whole(shape) for shape in shapes],
            scratch_shapes=[
                pltpu.VMEM((frames, span, width), low_type),
                pltpu.VMEM((frames, span, width), low_type),
                pltpu.VMEM((frames, 1, span), jnp.float32),
                pltpu.VMEM((frames, width, FRAME_TOK), jnp.float32),
            ],
        ),
        out_shape=[jax.ShapeDtypeStruct(shape, low_type) for shape in shapes],
        compiler_params=pltpu.CompilerParams(vmem_limit_bytes=56 * 1024 * 1024),
        cost_estimate=about(65),
        name="attend_back",
    )(order, count, *items, grads, flat, logs, *query_times, *key_times, *spaces)


def flat_weight(ref):
    return ref[...].reshape(-1, ref.shape[-1])


def project_kernel(
    heads_ref, weight_ref, hidden_ref, mods_ref, attended_ref, branch_ref, next_ref, mixed_ref
):
    attended = jnp.concatenate([heads_ref[group] for group in range(heads_ref.shape[0])], axis=1)
    attended_ref[...] = attended
    branch = product(attended, flat_weight(weight_ref))
    branch_ref[...] = branch
    hidden = hidden_ref[...] + mods_ref[2:3] * branch
    next_ref[...] = hidden
    normed, _ = norm_parts(hidden)
    mixed_ref[...] = (normed * (1.0 + mods_ref[4:5]) + mods_ref[3:4]).astype(low_type)


def project_norm(heads, weights, hidden, mods):
    groups, tokens, width = heads.shape
    devices, height, _ = weights.shape
    rows = D // devices
    by_frame = pl.BlockSpec((FRAME_TOK, D), lambda i: (i, 0))
    wide = jax.ShapeDtypeStruct((tokens, D), jnp.float32)
    low = jax.ShapeDtypeStruct((tokens, D), low_type)
    return pl.pallas_call(
        project_kernel,
        grid=(tokens // FRAME_TOK,),
        in_specs=[
            pl.BlockSpec((groups, FRAME_TOK, width), lambda i: (0, i, 0)),
            pl.BlockSpec((devices, rows, D), lambda i: (0, FF // D, 0)),
            by_frame,
            pl.BlockSpec((None, 6, D), lambda i: (i, 0, 0)),
        ],
        out_specs=[by_frame] * 4,
        out_shape=[low, wide, wide, low],
        compiler_params=pltpu.CompilerParams(vmem_limit_bytes=40 * 1024 * 1024),
        cost_estimate=about(4),
        name="project_norm",
    )(heads, weights, hidden, mods)


GELU_OUT = math.sqrt(2.0 / math.pi)
GELU_CUBE = 0.044715


def forward_kernel(
    scale_ref,
    mixed_ref,
    expand_ref,
    reduce_ref,
    hidden_ref,
    mods_ref,
    readout_ref,
    noise_ref,
    inner_ref,
    active_ref,
    grad_hidden_ref,
    grad_outer_ref,
    grad_readout_ref,
    grad_gate_ref,
    loss_ref,
    outer_ref,
):
    step = pl.program_id(0)
    frames = mods_ref.shape[0]
    inner = product(mixed_ref[...], flat_weight(expand_ref))
    inner_ref[...] = inner
    bend = jnp.tanh(GELU_OUT * (inner + GELU_CUBE * (inner * inner * inner)))
    active = (0.5 * inner * (1.0 + bend)).astype(low_type)
    active_ref[...] = active
    part = product(active, flat_weight(reduce_ref))

    @pl.when(step == 0)
    def _():
        outer_ref[...] = part

    @pl.when(step > 0)
    def _():
        outer_ref[...] += part

    @pl.when(step == pl.num_programs(0) - 1)
    def _():
        readout = readout_ref[...][:, PATCH_FEAT : 2 * PATCH_FEAT]
        grad_readout = jnp.zeros((D, PATCH_FEAT), jnp.float32)
        for frame in range(frames):
            tokens = slice(frame * FRAME_TOK, (frame + 1) * FRAME_TOK)
            outer = outer_ref[tokens]
            gate = mods_ref[frame, 5:6]
            final, inverse = norm_parts(hidden_ref[tokens] + gate * outer)
            final_low = final.astype(low_type)
            residue = product(final_low, readout) - noise_ref[tokens]
            loss_ref[frame] = jnp.zeros((1, LANES), jnp.float32) + jnp.sum(residue * residue)
            grad_pred = (residue * scale_ref[frame]).astype(low_type)
            grad_readout += across(final_low, grad_pred)
            grad_hidden = norm_back(final, inverse, against(grad_pred, readout))
            grad_hidden_ref[tokens] = grad_hidden
            grad_outer_ref[tokens] = (gate * grad_hidden).astype(low_type)
            grad_gate_ref[frame] = row_sum(grad_hidden * outer)
        grad_readout_ref[...] = grad_readout


def feed_forward(loss_scale, mixed, weights, hidden, mods, first_weights, noise):
    tokens = mixed.shape[0]
    devices, height, _ = weights.shape
    rows = D // devices
    frames = mods.shape[0]
    pieces = FF // D
    wide = jax.ShapeDtypeStruct((tokens, D), jnp.float32)
    by_piece = pl.BlockSpec((tokens, D), lambda k, *_: (0, k))
    return pl.pallas_call(
        forward_kernel,
        grid_spec=pltpu.PrefetchScalarGridSpec(
            num_scalar_prefetch=1,
            grid=(pieces,),
            in_specs=[
                whole((tokens, D)),
                pl.BlockSpec((devices, rows, D), lambda k, *_: (0, pieces + 1 + k, 0)),
                pl.BlockSpec((devices // pieces, pieces * rows, D), lambda k, *_: (k, 0, 0)),
                whole((tokens, D)),
                whole(mods.shape),
                pl.BlockSpec((D, LANES), lambda k, *_: (0, 3 * D // LANES)),
                whole((tokens, PATCH_FEAT)),
            ],
            out_specs=[
                by_piece,
                by_piece,
                whole((tokens, D)),
                whole((tokens, D)),
                whole((D, PATCH_FEAT)),
                whole((frames, 1, D)),
                whole((frames, 1, LANES)),
            ],
            scratch_shapes=[pltpu.VMEM((tokens, D), jnp.float32)],
        ),
        out_shape=[
            jax.ShapeDtypeStruct((tokens, FF), jnp.float32),
            jax.ShapeDtypeStruct((tokens, FF), low_type),
            wide,
            jax.ShapeDtypeStruct((tokens, D), low_type),
            jax.ShapeDtypeStruct((D, PATCH_FEAT), jnp.float32),
            jax.ShapeDtypeStruct((frames, 1, D), jnp.float32),
            jax.ShapeDtypeStruct((frames, 1, LANES), jnp.float32),
        ],
        compiler_params=pltpu.CompilerParams(vmem_limit_bytes=56 * 1024 * 1024),
        cost_estimate=about(20),
        name="feed_forward",
    )(loss_scale, mixed, weights, weights, hidden, mods, first_weights, noise)


def backward_kernel(
    grad_outer_ref,
    reduce_ref,
    expand_ref,
    inner_ref,
    hidden_ref,
    grad_hidden_ref,
    branch_ref,
    mods_ref,
    project_ref,
    grad_inner_ref,
    grad_one_ref,
    grad_branch_ref,
    heads_ref,
    grad_mods_ref,
    grad_mixed_ref,
):
    step = pl.program_id(0)
    frames = mods_ref.shape[0]
    groups, _, width = heads_ref.shape
    inner = inner_ref[...]
    square = inner * inner
    bend = jnp.tanh(GELU_OUT * (inner + GELU_CUBE * (square * inner)))
    slope = 0.5 * (1.0 + bend) + 0.5 * inner * (1.0 - bend * bend) * (
        GELU_OUT * (1.0 + 3.0 * GELU_CUBE * square)
    )
    grad_active = against(grad_outer_ref[...], flat_weight(reduce_ref))
    grad_inner = (grad_active * slope).astype(low_type)
    grad_inner_ref[...] = grad_inner
    part = against(grad_inner, flat_weight(expand_ref))

    @pl.when(step == 0)
    def _():
        grad_mixed_ref[...] = part

    @pl.when(step > 0)
    def _():
        grad_mixed_ref[...] += part

    @pl.when(step == pl.num_programs(0) - 1)
    def _():
        project = flat_weight(project_ref)
        for frame in range(frames):
            tokens = slice(frame * FRAME_TOK, (frame + 1) * FRAME_TOK)
            normed, inverse = norm_parts(hidden_ref[tokens])
            grad_mixed = grad_mixed_ref[tokens]
            grad_mods_ref[frame, 1:2] = row_sum(grad_mixed)
            grad_mods_ref[frame, 2:3] = row_sum(grad_mixed * normed)
            grad_one = grad_hidden_ref[tokens] + norm_back(
                normed, inverse, grad_mixed * (1.0 + mods_ref[frame, 4:5])
            )
            grad_one_ref[tokens] = grad_one
            grad_mods_ref[frame, 0:1] = row_sum(grad_one * branch_ref[tokens])
            grad_branch = (mods_ref[frame, 2:3] * grad_one).astype(low_type)
            grad_branch_ref[tokens] = grad_branch
            grad_attended = against(grad_branch, project).astype(low_type)
            for group in range(groups):
                heads_ref[group, tokens] = grad_attended[:, group * width : (group + 1) * width]


def feed_backward(grad_outer, weights, inner, hidden, grad_hidden, branch, mods, groups):
    tokens = hidden.shape[0]
    devices, height, _ = weights.shape
    rows = D // devices
    frames = mods.shape[0]
    pieces = FF // D
    by_piece = pl.BlockSpec((tokens, D), lambda k: (0, k))
    return pl.pallas_call(
        backward_kernel,
        grid=(pieces,),
        in_specs=[
            whole((tokens, D)),
            pl.BlockSpec((devices // pieces, pieces * rows, D), lambda k: (k, 0, 0)),
            pl.BlockSpec((devices, rows, D), lambda k: (0, pieces + 1 + k, 0)),
            by_piece,
            whole((tokens, D)),
            whole((tokens, D)),
            whole((tokens, D)),
            whole(mods.shape),
            pl.BlockSpec((devices, rows, D), lambda k: (0, pieces, 0)),
        ],
        out_specs=[
            by_piece,
            whole((tokens, D)),
            whole((tokens, D)),
            whole((groups, tokens, D // groups)),
            whole((frames, 3, D)),
        ],
        out_shape=[
            jax.ShapeDtypeStruct((tokens, FF), low_type),
            jax.ShapeDtypeStruct((tokens, D), jnp.float32),
            jax.ShapeDtypeStruct((tokens, D), low_type),
            jax.ShapeDtypeStruct((groups, tokens, D // groups), low_type),
            jax.ShapeDtypeStruct((frames, 3, D), jnp.float32),
        ],
        scratch_shapes=[pltpu.VMEM((tokens, D), jnp.float32)],
        compiler_params=pltpu.CompilerParams(vmem_limit_bytes=58 * 1024 * 1024),
        cost_estimate=about(22),
        name="feed_backward",
    )(grad_outer, weights, weights, inner, hidden, grad_hidden, branch, mods, weights)


def grads_kernel(
    active_ref, grad_outer_ref, attended_ref, grad_branch_ref, mixed_ref, grad_inner_ref, out_ref
):
    cores, lines, height, _ = out_ref.shape
    pieces = FF // D
    rows = height // (2 * pieces + 1)

    def store(start, count, value):
        value = value.astype(low_type)
        for line in range(lines):
            for core in range(cores):
                at = (line * cores + core) * count
                out_ref[core, line, start : start + count] = value[at : at + count]

    store(0, pieces * rows, across(active_ref[...], grad_outer_ref[...]))
    store(pieces * rows, rows, across(attended_ref[...], grad_branch_ref[...]))
    for piece in range(pieces):
        store(
            (pieces + 1 + piece) * rows,
            rows,
            across(mixed_ref[...], grad_inner_ref[:, piece * D : (piece + 1) * D]),
        )


def weight_grads(sizes, active, grad_outer, attended, grad_branch, mixed, grad_inner):
    batch, row, core = sizes
    tokens = mixed.shape[0]
    rows = D // (batch * row * core)
    height = rows * (2 * (FF // D) + 1)
    part = pl.BlockSpec((tokens, D // batch), lambda i: (0, i))
    return pl.pallas_call(
        grads_kernel,
        grid=(batch,),
        in_specs=[
            pl.BlockSpec((tokens, FF // batch), lambda i: (0, i)),
            whole((tokens, D)),
            part,
            whole((tokens, D)),
            part,
            whole((tokens, FF)),
        ],
        out_specs=pl.BlockSpec((None, core, row, height, D), lambda i: (i, 0, 0, 0, 0)),
        out_shape=jax.ShapeDtypeStruct((batch, core, row, height, D), low_type),
        compiler_params=pltpu.CompilerParams(vmem_limit_bytes=56 * 1024 * 1024),
        cost_estimate=about(28),
        name="weight_grads",
    )(active, grad_outer, attended, grad_branch, mixed, grad_inner)


def swapped(value, axis, offset):
    return lax.ppermute(value, axis, [(i, i ^ offset) for i in range(lax.axis_size(axis))])


def gather_near(value, axes=("core", "batch", "row")):
    for axis in axes:
        others = [swapped(value, axis, offset) for offset in range(1, lax.axis_size(axis))]
        value = jnp.concatenate([value] + others, axis=0)
    return value


def near_owner(index):
    batch, row, core = (lax.axis_size(axis) for axis in ALL)
    places = (
        (index // core % batch) ^ lax.axis_index("batch"),
        (index // (core * batch)) ^ lax.axis_index("row"),
        (index % core) ^ lax.axis_index("core"),
    )
    return (places[0] * row + places[1]) * core + places[2]


def exchange_sum(value, axes, at=0, sent=jnp.float32):
    count = value.shape[at]
    mine = lax.axis_index(axes)
    total = lax.dynamic_index_in_dim(value, mine, at, keepdims=False)
    parts = [
        lax.ppermute(
            lax.dynamic_index_in_dim(value, mine ^ offset, at, keepdims=False).astype(sent),
            axes,
            [(i, i ^ offset) for i in range(count)],
        )
        for offset in range(1, count)
    ]
    for part in parts:
        total = total + part.astype(jnp.float32)
    return total


def total_sum(value):
    for axis in ("core", "batch", "row"):
        parts = [value] + [
            swapped(value, axis, offset) for offset in range(1, lax.axis_size(axis))
        ]
        while len(parts) > 1:
            parts = [parts[i] + parts[i + 1] for i in range(0, len(parts), 2)]
        value = parts[0]
    return value


def per_device(
    clean_latents,
    noise_sample,
    noise_levels,
    clean_flags,
    span_frame,
    patch_master,
    patch_first,
    patch_second,
    level_master,
    level_first,
    level_second,
    adaptive_master,
    adaptive_first,
    adaptive_second,
    triple_master,
    triple_first,
    triple_second,
    project_master,
    project_first,
    project_second,
    expand_master,
    expand_first,
    expand_second,
    reduce_master,
    reduce_first,
    reduce_second,
    readout_master,
    readout_first,
    readout_second,
):
    masters = (
        patch_master,
        level_master,
        adaptive_master,
        triple_master,
        project_master,
        expand_master,
        reduce_master,
        readout_master,
    )
    firsts = (
        patch_first,
        level_first,
        adaptive_first,
        triple_first,
        project_first,
        expand_first,
        reduce_first,
        readout_first,
    )
    seconds = (
        patch_second,
        level_second,
        adaptive_second,
        triple_second,
        project_second,
        expand_second,
        reduce_second,
        readout_second,
    )
    batch_count, row_count, core_count = (lax.axis_size(axis) for axis in ALL)
    batch_index, row_index, core_index = (lax.axis_index(axis) for axis in ALL)
    devices = batch_count * row_count * core_count
    rows = D // devices
    token_count = clean_latents.shape[1]
    frame_local = token_count // FRAME_TOK

    moved = batch_count == row_count and HEADS % (batch_count * core_count) == 0
    if moved:
        clip_index, chunk_index = row_index, batch_index * core_count + core_index
        head_axes, head_groups = ("batch", "core"), batch_count * core_count
        rest_axes = ("row",)
    else:
        clip_index, chunk_index = batch_index, row_index * core_count + core_index
        head_axes, head_groups = ("row",), row_count
        rest_axes = ("batch", "core")

    both = jnp.concatenate([clean_latents[0], noise_sample[0]], axis=1)
    if moved:
        turn = [
            (
                (a * row_count + b) * core_count + c,
                (b * row_count + a) * core_count + c,
            )
            for a in range(batch_count)
            for b in range(row_count)
            for c in range(core_count)
        ]
        both = lax.ppermute(both, ALL, turn)
    clean_tok, noise_tok = both[:, :PATCH_FEAT], both[:, PATCH_FEAT:]

    first_weights = jnp.concatenate(
        [
            triple_master.astype(low_type),
            jnp.transpose(patch_master).astype(low_type),
            readout_master.astype(low_type),
            jnp.zeros((rows, LANES - 2 * PATCH_FEAT), low_type),
        ],
        axis=1,
    )
    first_weights = lax.all_gather(first_weights, ALL, axis=0, tiled=True)
    second_weights = jnp.concatenate(
        [reduce_master.astype(low_type), project_master.astype(low_type)]
        + [expand_master[:, k * D : (k + 1) * D].astype(low_type) for k in range(FF // D)],
        axis=0,
    )
    second_weights = lax.all_gather(second_weights, ALL, axis=0)

    levels_all = noise_levels.reshape(-1)
    flags_all = clean_flags.reshape(-1)
    _, _, index_all = plan(levels_all, flags_all)
    if moved:
        order_all = lambda v: (
            v.reshape((row_count, batch_count, core_count, frame_local) + v.shape[1:])
            .swapaxes(0, 1)
            .reshape(v.shape)
        )
    else:
        order_all = lambda v: v
    index_all = order_all(index_all)
    every = jnp.arange(devices, dtype=jnp.int32)
    index_near = jnp.sum(
        jnp.where(
            (near_owner(every)[:, None] == every[None, :])[..., None],
            index_all.reshape(1, devices, frame_local),
            0,
        ),
        axis=1,
    ).reshape(-1)
    table_low = level_master.astype(low_type).astype(jnp.float32)

    def table_rows(index):
        hot = (index[:, None] == jnp.arange(NB + 1, dtype=jnp.int32)[None, :]).astype(jnp.float32)
        return hot, jnp.dot(hot, table_low, precision=lax.Precision.HIGHEST)

    _, pre_own = table_rows(index_all)
    hot_near, pre_near = table_rows(index_near)
    cond_near, silu_back = jax.vjp(jax.nn.silu, pre_near)
    cond_near = cond_near.astype(low_type)
    cond_own = jax.nn.silu(pre_own).astype(low_type)
    adaptive_low = adaptive_master.astype(low_type)
    adapt = product(cond_own, adaptive_low).reshape(devices, frame_local, 6 * D)
    mods = jnp.sum(lax.all_to_all(adapt, ALL, 0, 0, tiled=True), axis=0)
    mods = mods.reshape(frame_local, 6, D)

    my_levels = lax.dynamic_slice_in_dim(
        lax.dynamic_index_in_dim(noise_levels, clip_index, 0, keepdims=False),
        chunk_index * frame_local,
        frame_local,
    )
    my_flags = lax.dynamic_slice_in_dim(
        lax.dynamic_index_in_dim(clean_flags, clip_index, 0, keepdims=False),
        chunk_index * frame_local,
        frame_local,
    )
    my_frames = lax.dynamic_slice_in_dim(span_frame, chunk_index * frame_local, frame_local)
    if moved:
        query_frames = key_frames = span_frame
    else:
        by_chunk = span_frame.reshape(row_count, core_count, frame_local)
        query_frames = lax.dynamic_index_in_dim(by_chunk, core_index, 1, keepdims=False).reshape(-1)
        key_frames = by_chunk.swapaxes(0, 1).reshape(-1)
    query_total, key_total = query_frames.shape[0], key_frames.shape[0]
    earlier = jnp.sum(key_frames[None, :] < key_frames[:, None], axis=1)
    key_order = jnp.sum(
        jnp.where(earlier[:, None] == jnp.arange(key_total)[None, :], jnp.arange(key_total)[:, None], 0),
        axis=0,
    ).astype(jnp.int32)
    key_count = jnp.sum(key_frames[None, :] <= query_frames[:, None], axis=1).astype(jnp.int32)
    later = jnp.sum(query_frames[None, :] > query_frames[:, None], axis=1)
    query_order = jnp.sum(
        jnp.where(later[:, None] == jnp.arange(query_total)[None, :], jnp.arange(query_total)[:, None], 0),
        axis=0,
    ).astype(jnp.int32)
    query_count = jnp.sum(query_frames[None, :] >= key_frames[:, None], axis=1).astype(jnp.int32)
    my_times, query_times, key_times = (
        time_tables(my_frames),
        time_tables(query_frames),
        time_tables(key_frames),
    )
    spaces = space_tables()

    alpha_bar, noised, _ = plan(my_levels, my_flags)
    inputs = noised_input(clean_tok, noise_tok, alpha_bar, noised).astype(low_type)
    width = D // head_groups
    hidden_zero, normed_low, heads = triple_heads(
        inputs, mods, first_weights, my_times, spaces, head_groups
    )
    heads = lax.all_to_all(heads, head_axes, 0, 0, tiled=True)
    if moved:
        heads = heads.reshape(head_groups, frame_local, FRAME_TOK, 3 * width)
        items = (heads, heads, heads)
    else:
        heads = heads.reshape(head_groups, 3, frame_local, FRAME_TOK, width)
        items = (heads[:, 0],) + tuple(
            lax.all_gather(heads[:, part], "core", axis=0, tiled=True) for part in (1, 2)
        )
    attended, flat, logs = attend(key_order, key_count, items, width)
    attended = attended.reshape(head_groups, token_count, width)
    attended = lax.all_to_all(attended, head_axes, 0, 0, tiled=True)
    attended, normed_low = lax.optimization_barrier((attended, normed_low))
    normed_clip = lax.all_gather(normed_low, head_axes, axis=0, tiled=True)
    attended_low, branch, hidden_one, mixed_low = project_norm(
        attended, second_weights, hidden_zero, mods
    )
    frame_count = jnp.sum((1 - clean_flags).astype(jnp.float32))
    loss_scale = noised * (2.0 / (FRAME_TOK * PATCH_FEAT)) / jnp.maximum(frame_count, 1.0)
    (
        inner,
        active_low,
        grad_hidden_two,
        grad_outer,
        grad_readout,
        grad_gate_two,
        squared,
    ) = feed_forward(
        loss_scale, mixed_low, second_weights, hidden_one, mods, first_weights, noise_tok
    )
    frame_loss = squared[:, 0, 0] * (1.0 / (FRAME_TOK * PATCH_FEAT)) * noised
    grad_inner_low, grad_hidden_one, grad_branch, grad_attended, grad_mods = feed_backward(
        grad_outer,
        second_weights,
        inner,
        hidden_one,
        grad_hidden_two,
        branch,
        mods,
        head_groups,
    )
    grad_attended = lax.all_to_all(grad_attended, head_axes, 0, 0, tiled=True)
    grad_attended = grad_attended.reshape(head_groups, frame_local, FRAME_TOK, width)
    early_adapt = jnp.concatenate(
        [grad_mods.reshape(frame_local, 3 * D), grad_gate_two.reshape(frame_local, D)], axis=1
    ).astype(low_type)
    early_adapt = gather_near(early_adapt, ("core", "batch"))
    grad_attended, early_adapt = lax.optimization_barrier((grad_attended, early_adapt))
    early_adapt = gather_near(early_adapt, ("row",))

    second_grads = weight_grads(
        (batch_count, row_count, core_count),
        active_low,
        grad_outer,
        attended_low,
        grad_branch,
        mixed_low,
        grad_inner_low,
    )
    second_own = lax.psum_scatter(
        second_grads.reshape((-1,) + second_grads.shape[2:]),
        ("batch", "core"),
        scatter_dimension=0,
    )
    second_own = lax.psum_scatter(second_own, "row", scatter_dimension=0).astype(jnp.float32)

    grads = attend_back(
        query_order,
        query_count,
        items,
        grad_attended,
        flat,
        logs,
        query_times,
        key_times,
        spaces,
    )
    if moved:
        grad_heads = grads[0].reshape(head_groups, token_count, 3 * width)
    else:
        grad_heads = [grads[0]] + [
            lax.psum_scatter(
                item.astype(jnp.float32), "core", scatter_dimension=0, tiled=True
            ).astype(low_type)
            for item in grads[1:]
        ]
        grad_heads = jnp.concatenate(grad_heads, axis=-1).reshape(
            head_groups, token_count, 3 * width
        )
    grad_triple = across(
        normed_clip.reshape(-1, D), grad_heads.reshape(head_groups * token_count, 3 * width)
    )
    grad_heads = lax.all_to_all(grad_heads, head_axes, 0, 0, tiled=True)
    if not moved:
        grad_heads = grad_heads.reshape(head_groups, token_count, 3, width).swapaxes(1, 2)
    grad_triple = grad_triple.reshape(batch_count, row_count, core_count, rows, 3 * width)
    if moved:
        grad_triple = grad_triple.transpose(1, 0, 2, 3, 4)
    else:
        grad_triple = grad_triple.transpose(0, 2, 1, 3, 4)
    rest_count = devices // head_groups
    triple_own = exchange_sum(
        grad_triple.reshape(rest_count, head_groups, rows, 3 * width),
        rest_axes,
        sent=low_type,
    )
    grad_heads, triple_own, early_adapt = lax.optimization_barrier(
        (grad_heads, triple_own, early_adapt)
    )
    grad_shift, grad_patch = triple_back(
        grad_heads, first_weights, hidden_zero, grad_hidden_one, mods, inputs, head_groups
    )
    late_adapt = gather_near(grad_shift.reshape(frame_local, 2 * D).astype(low_type))
    small = jnp.concatenate([grad_patch, grad_readout], axis=1)
    small = small.reshape(batch_count, row_count, core_count, -1, LANES)
    small = exchange_sum(small, "core", 2)
    small = exchange_sum(small, "batch")
    small_own = exchange_sum(small, "row").reshape(rows, 2 * PATCH_FEAT)

    triple_own = lax.all_to_all(triple_own, head_axes, 0, 0, tiled=True)
    triple_own = (
        triple_own.reshape(head_groups, rows, 3, width).transpose(1, 2, 0, 3).reshape(rows, 3 * D)
    )
    early_columns = 2 * D
    adapt_own = jnp.concatenate(
        [across(cond_near, late_adapt), across(cond_near, early_adapt)], axis=1
    )
    grad_cond = against(late_adapt, adaptive_low[:, :early_columns]) + against(
        early_adapt, adaptive_low[:, early_columns:]
    )
    (grad_pre,) = silu_back(grad_cond)
    table_own = lax.dot_general(
        hot_near,
        grad_pre,
        (((0,), (0,)), ((), ())),
        precision=lax.Precision.HIGHEST,
        preferred_element_type=jnp.float32,
    )
    expand_own = jnp.concatenate(
        [
            second_own[(FF // D + 1 + k) * rows : (FF // D + 2 + k) * rows]
            for k in range(FF // D)
        ],
        axis=1,
    )
    reduced = (
        jnp.transpose(small_own[:, :PATCH_FEAT]),
        table_own,
        adapt_own,
        triple_own,
        second_own[FF // D * rows : (FF // D + 1) * rows],
        expand_own,
        second_own[: FF // D * rows],
        small_own[:, PATCH_FEAT:],
    )
    squares = sum((jnp.sum(gradient * gradient) for gradient in reduced))
    level_hits = (my_levels[:, None] == jnp.arange(NB, dtype=jnp.int32)[None, :]).astype(
        jnp.float32
    )
    bucket_local = jnp.sum(level_hits * frame_loss[:, None], axis=0)
    sums = jnp.zeros((8, LANES), jnp.float32)
    sums = sums.at[0, :NB].set(bucket_local)
    sums = sums.at[1, 0].set(squares)
    sums = sums.at[2, 0].set(jnp.sum(frame_loss))
    sums = total_sum(sums)
    clip_norm = jnp.sqrt(sums[1, 0])
    factor = jnp.minimum(1.0, clip_bound / clip_norm)
    new = [
        adamw_update(
            masters[item], firsts[item], seconds[item], reduced[item], factor, learn_rates[item]
        )
        for item in range(8)
    ]
    return (sums[2, 0], frame_count, sums[0, :NB], clip_norm) + tuple(
        item for triple in new for item in triple
    )


def solution(mesh):
    in_specs = (
        P("batch", ("row", "core"), None),
        P("batch", ("row", "core"), None),
        P(),
        P(),
        P(),
        P(None, ALL),
        P(None, ALL),
        P(None, ALL),
        P(None, ALL),
        P(None, ALL),
        P(None, ALL),
        P(ALL, None),
        P(ALL, None),
        P(ALL, None),
        P(ALL, None),
        P(ALL, None),
        P(ALL, None),
        P(ALL, None),
        P(ALL, None),
        P(ALL, None),
        P(ALL, None),
        P(ALL, None),
        P(ALL, None),
        P(ALL, None),
        P(ALL, None),
        P(ALL, None),
        P(ALL, None),
        P(ALL, None),
        P(ALL, None),
    )
    out_specs = (
        P(),
        P(),
        P(),
        P(),
        P(None, ALL),
        P(None, ALL),
        P(None, ALL),
        P(None, ALL),
        P(None, ALL),
        P(None, ALL),
        P(ALL, None),
        P(ALL, None),
        P(ALL, None),
        P(ALL, None),
        P(ALL, None),
        P(ALL, None),
        P(ALL, None),
        P(ALL, None),
        P(ALL, None),
        P(ALL, None),
        P(ALL, None),
        P(ALL, None),
        P(ALL, None),
        P(ALL, None),
        P(ALL, None),
        P(ALL, None),
        P(ALL, None),
        P(ALL, None),
    )
    batch_size, blk_size = mesh.shape["batch"], mesh.shape["blk"]
    inner = Mesh(mesh.devices.reshape(batch_size, blk_size // 2, 2), ALL)
    return jax.shard_map(
        per_device, mesh=inner, in_specs=in_specs, out_specs=out_specs, check_vma=False
    )
```

```python
import functools
import math

import jax
import jax.numpy as jnp
from jax import lax
from jax.experimental import pallas as pl
from jax.experimental.pallas import tpu as pltpu
from jax.sharding import Mesh
from jax.sharding import PartitionSpec as P

D = 1024
HEADS = 16
HEAD_DIM = 64
FF = 4096
PATCH_FEAT = 16
FRAME_TOK = 256
SIDE = 16
NB = 32
STEP = 10
LANES = 128
ALL = ("batch", "row", "core")


learn_rates = (0.5, 2.0, 0.05, 0.05, 0.5, 0.05, 0.05, 0.05)
beta_first = 0.9
beta_second = 0.999
decay_rate = 0.01
adam_floor = 1e-08
clip_bound = 0.02
low_type = jnp.bfloat16


def product(left, right):
    return jnp.dot(left, right, preferred_element_type=jnp.float32)


def across(left, right):
    return lax.dot_general(
        left, right, (((0,), (0,)), ((), ())), preferred_element_type=jnp.float32
    )


def against(left, right):
    return lax.dot_general(
        left, right, (((1,), (1,)), ((), ())), preferred_element_type=jnp.float32
    )


def plan(levels, clean_flags):
    alpha_bar = jnp.cos(0.5 * math.pi * (levels.astype(jnp.float32) + 1.0) / (NB + 1.0)) ** 2
    noised = (1 - clean_flags).astype(jnp.float32)
    table_index = jnp.where(clean_flags == 1, 0, levels + 1)
    return (alpha_bar, noised, table_index)


def noised_input(clean_tok, noise_tok, alpha_bar, noised):
    frame_shape = (alpha_bar.shape[0], -1, clean_tok.shape[-1])
    clean_frames = clean_tok.reshape(frame_shape)
    noise_frames = noise_tok.reshape(frame_shape)
    mixed_tok = (
        jnp.sqrt(alpha_bar)[:, None, None] * clean_frames
        + jnp.sqrt(1.0 - alpha_bar)[:, None, None] * noise_frames
    )
    return jnp.where(noised[:, None, None] > 0.5, mixed_tok, clean_frames).reshape(clean_tok.shape)


def adamw_update(master, first_moment, second_moment, gradient, factor, step_rate):
    clipped = gradient * factor
    first_new = beta_first * first_moment + (1.0 - beta_first) * clipped
    second_new = beta_second * second_moment + (1.0 - beta_second) * clipped * clipped
    first_hat = first_new / (1.0 - beta_first**STEP)
    second_hat = second_new / (1.0 - beta_second**STEP)
    master_new = master - step_rate * (
        first_hat / (jnp.sqrt(second_hat) + adam_floor) + decay_rate * master
    )
    return (first_new, second_new, master_new)


def lane_places():
    lane = jnp.arange(LANES, dtype=jnp.int32) % HEAD_DIM
    half = HEAD_DIM // 2
    place = lane % half
    time_count = HEAD_DIM // 8
    space_count = 3 * HEAD_DIM // 16
    sign = jnp.where(lane < half, -1.0, 1.0)
    time_freq = 10000.0 ** (-(place.astype(jnp.float32)) / time_count)
    space_place = jnp.where(place < time_count + space_count, place - time_count, place - time_count - space_count)
    space_freq = 100.0 ** (-(space_place.astype(jnp.float32)) / space_count)
    is_time = place < time_count
    is_row = (place >= time_count) & (place < time_count + space_count)
    return sign, time_freq, space_freq, is_time, is_row


def time_tables(frames):
    sign, time_freq, _, is_time, _ = lane_places()
    angle = frames.astype(jnp.float32)[:, None] * time_freq[None]
    return (
        jnp.where(is_time, jnp.cos(angle), 0.0)[:, None],
        jnp.where(is_time, jnp.sin(angle) * sign, 0.0)[:, None],
    )


def space_tables():
    sign, _, space_freq, is_time, is_row = lane_places()
    token = jnp.arange(FRAME_TOK, dtype=jnp.int32)
    row_pos = (token // SIDE).astype(jnp.float32)[:, None]
    col_pos = (token % SIDE).astype(jnp.float32)[:, None]
    angle = jnp.where(is_row[None], row_pos, col_pos) * space_freq[None]
    return (
        jnp.where(is_time, 0.0, jnp.cos(angle)),
        jnp.where(is_time, 0.0, jnp.sin(angle) * sign),
    )


def partner(value):
    half = HEAD_DIM // 2
    width = value.shape[1]
    if width == LANES:
        lane = lax.broadcasted_iota(jnp.int32, value.shape, 1)
        ahead = pltpu.roll(value, width - half, 1)
        behind = pltpu.roll(value, half, 1)
        return jnp.where(lane % HEAD_DIM < half, ahead, behind)
    return jnp.concatenate([value[:, half:], value[:, :half]], axis=1)


def norm_parts(hidden):
    centred = hidden - jnp.mean(hidden, axis=-1, keepdims=True)
    variance = jnp.mean(centred * centred, axis=-1, keepdims=True)
    inverse = lax.rsqrt(variance + 1e-06)
    return centred * inverse, inverse


def norm_back(normed, inverse, grad):
    along = jnp.mean(grad * normed, axis=-1, keepdims=True)
    return inverse * (grad - jnp.mean(grad, axis=-1, keepdims=True) - normed * along)


def row_sum(value):
    return jnp.sum(value, axis=0, keepdims=True)


def triple_kernel(
    inputs_ref,
    extra_ref,
    mods_ref,
    weight_ref,
    time_cos,
    time_sin,
    space_cos,
    space_sin,
    hidden_ref,
    normed_ref,
    out_ref,
):
    column = pl.program_id(0)
    width = out_ref.shape[-1]
    frames = mods_ref.shape[0]

    @pl.when(column == 0)
    def _():
        patch = extra_ref[...][:, :PATCH_FEAT]
        for frame in range(frames):
            tokens = slice(frame * FRAME_TOK, (frame + 1) * FRAME_TOK)
            hidden = against(inputs_ref[tokens], patch)
            hidden_ref[tokens] = hidden
            normed, _ = norm_parts(hidden)
            normed_ref[tokens] = (
                normed * (1.0 + mods_ref[frame, 1:2]) + mods_ref[frame, 0:1]
            ).astype(low_type)

    acc = product(normed_ref[...], weight_ref[...])
    per_block = acc.shape[1] // LANES

    def store(piece, values):
        for part in range(LANES // width):
            at = piece * (LANES // width) + part
            done = values[:, part * width : (part + 1) * width].astype(low_type)
            if len(out_ref.shape) == 3:
                out_ref[at] = done
            else:
                out_ref[at, 0] = done

    turned = column < 2 * D // acc.shape[1]

    @pl.when(turned)
    def _():
        for piece in range(per_block):
            done = []
            for frame in range(frames):
                value = acc[
                    frame * FRAME_TOK : (frame + 1) * FRAME_TOK,
                    piece * LANES : (piece + 1) * LANES,
                ]
                cosine = time_cos[frame] + space_cos[...]
                sine = time_sin[frame] + space_sin[...]
                done.append(value * cosine + partner(value) * sine)
            store(piece, jnp.concatenate(done, axis=0))

    @pl.when(jnp.logical_not(turned))
    def _():
        for piece in range(per_block):
            store(piece, acc[:, piece * LANES : (piece + 1) * LANES])


BLOCK = 256


def heads_layout(groups, tokens):
    width = D // groups
    per_block = BLOCK // width
    per_part = D // BLOCK
    if width == LANES:
        return (groups, tokens, 3 * width), pl.BlockSpec(
            (per_block, tokens, width), lambda j: (j % per_part, 0, j // per_part)
        )
    return (groups, 3, tokens, width), pl.BlockSpec(
        (per_block, 1, tokens, width), lambda j: (j % per_part, j // per_part, 0, 0)
    )


def triple_heads(inputs, mods, weight, times, spaces, groups):
    tokens = inputs.shape[0]
    shape, spec = heads_layout(groups, tokens)
    return pl.pallas_call(
        triple_kernel,
        grid=(3 * D // BLOCK,),
        in_specs=[
            whole(inputs.shape),
            pl.BlockSpec((D, LANES), lambda j: (0, 3 * D // LANES)),
            whole(mods.shape),
            pl.BlockSpec((D, BLOCK), lambda j: (0, j)),
            whole(times[0].shape),
            whole(times[1].shape),
            whole(spaces[0].shape),
            whole(spaces[1].shape),
        ],
        out_specs=[whole((tokens, D)), whole((tokens, D)), spec],
        out_shape=[
            jax.ShapeDtypeStruct((tokens, D), jnp.float32),
            jax.ShapeDtypeStruct((tokens, D), low_type),
            jax.ShapeDtypeStruct(shape, low_type),
        ],
        compiler_params=pltpu.CompilerParams(vmem_limit_bytes=40 * 1024 * 1024),
        cost_estimate=about(12),
        name="triple_heads",
    )(inputs, weight, mods, weight, *times, *spaces)


def triple_back_kernel(
    grads_ref,
    weight_ref,
    hidden_ref,
    grad_one_ref,
    mods_ref,
    inputs_ref,
    grad_mods_ref,
    grad_patch_ref,
    sum_ref,
):
    step = pl.program_id(0)
    frames = mods_ref.shape[0]
    pieces = range(grads_ref.shape[0])
    if len(grads_ref.shape) == 3:
        grads = jnp.concatenate([grads_ref[piece] for piece in pieces], axis=1)
    else:
        grads = jnp.concatenate([grads_ref[piece, 0] for piece in pieces], axis=1)
    part = against(grads, weight_ref[...])

    @pl.when(step == 0)
    def _():
        sum_ref[...] = part

    @pl.when(step > 0)
    def _():
        sum_ref[...] += part

    @pl.when(step == pl.num_programs(0) - 1)
    def _():
        grad_patch = jnp.zeros((D, PATCH_FEAT), jnp.float32)
        for frame in range(frames):
            tokens = slice(frame * FRAME_TOK, (frame + 1) * FRAME_TOK)
            normed, inverse = norm_parts(hidden_ref[tokens])
            grad_normed = sum_ref[tokens]
            grad_mods_ref[frame, 0:1] = row_sum(grad_normed)
            grad_mods_ref[frame, 1:2] = row_sum(grad_normed * normed)
            grad_hidden = grad_one_ref[tokens] + norm_back(
                normed, inverse, grad_normed * (1.0 + mods_ref[frame, 1:2])
            )
            grad_patch += across(grad_hidden.astype(low_type), inputs_ref[tokens])
        grad_patch_ref[...] = grad_patch


def triple_back(grads, weight, hidden, grad_one, mods, inputs, groups):
    tokens = inputs.shape[0]
    frames = mods.shape[0]
    return pl.pallas_call(
        triple_back_kernel,
        grid=(3 * D // BLOCK,),
        in_specs=[
            heads_layout(groups, tokens)[1],
            pl.BlockSpec((D, BLOCK), lambda j: (0, j)),
            whole(hidden.shape),
            whole(hidden.shape),
            whole(mods.shape),
            whole(inputs.shape),
        ],
        out_specs=[whole((frames, 2, D)), whole((D, PATCH_FEAT))],
        out_shape=[
            jax.ShapeDtypeStruct((frames, 2, D), jnp.float32),
            jax.ShapeDtypeStruct((D, PATCH_FEAT), jnp.float32),
        ],
        scratch_shapes=[pltpu.VMEM((tokens, D), jnp.float32)],
        compiler_params=pltpu.CompilerParams(vmem_limit_bytes=40 * 1024 * 1024),
        cost_estimate=about(12),
        name="triple_back",
    )(grads, weight, hidden, grad_one, mods, inputs)


def head_stack(value):
    count = value.shape[1] // HEAD_DIM
    if count == 1:
        return value
    lane = lax.broadcasted_iota(jnp.int32, value.shape, 1)
    zero = jnp.zeros_like(value)
    return jnp.concatenate(
        [jnp.where(lane // HEAD_DIM == head, value, zero) for head in range(count)], axis=0
    )


UNROLL = 4


def unrolled(count, body, carry):
    def several(base, now):
        for offset in range(UNROLL):
            now = body(base * UNROLL + offset, now)
        return now

    whole_part = count // UNROLL
    carry = lax.fori_loop(0, whole_part, several, carry)
    return lax.fori_loop(whole_part * UNROLL, count, body, carry)


def attend_kernel(
    order_ref,
    count_ref,
    query_ref,
    key_ref,
    value_ref,
    out_ref,
    flat_ref,
    log_ref,
    turned_ref,
    scores_ref,
):
    step = pl.program_id(0)
    chunks, per_chunk = key_ref.shape[0], key_ref.shape[1]
    width = key_ref.shape[-1]
    heads = width // HEAD_DIM
    span = heads * FRAME_TOK

    @pl.when(step == 0)
    def _():
        def turn(chunk, carry):
            for part in range(per_chunk):
                turned_ref[chunk, part] = jnp.transpose(value_ref[chunk, part])
            return carry

        lax.fori_loop(0, chunks, turn, 0)

    queries = jnp.transpose(head_stack(query_ref[...] * jnp.asarray(HEAD_DIM**-0.5, low_type)))
    count = count_ref[step]

    def by_eight(value):
        return value.reshape(FRAME_TOK // 8, 8, span)

    def score(place, top):
        frame = order_ref[place]
        scores = product(key_ref[frame // per_chunk, frame % per_chunk], queries)
        scores_ref[place] = scores
        return jnp.maximum(top, jnp.max(by_eight(scores), axis=0))

    top = unrolled(count, score, jnp.full((8, span), -1e30, jnp.float32))
    top = jnp.max(top, axis=0, keepdims=True)

    def weigh(place, carry):
        total, sums = carry
        frame = order_ref[place]
        chances = jnp.exp(scores_ref[place] - top)
        total = total + jnp.sum(by_eight(chances), axis=0)
        chances = chances.astype(low_type)
        new_sums = []
        for head in range(heads):
            values = turned_ref[
                frame // per_chunk,
                frame % per_chunk,
                head * HEAD_DIM : (head + 1) * HEAD_DIM,
                :,
            ]
            columns = slice(head * FRAME_TOK, (head + 1) * FRAME_TOK)
            new_sums.append(sums[head] + product(values, chances[:, columns]))
        return total, tuple(new_sums)

    initial = (
        jnp.zeros((8, span), jnp.float32),
        tuple(jnp.zeros((HEAD_DIM, FRAME_TOK), jnp.float32) for _ in range(heads)),
    )
    total, sums = unrolled(count, weigh, initial)
    total = jnp.sum(total, axis=0, keepdims=True)
    log_ref[...] = top + jnp.log(total)
    inverse = 1.0 / total
    result = jnp.concatenate(
        [
            sums[head] * inverse[:, head * FRAME_TOK : (head + 1) * FRAME_TOK]
            for head in range(heads)
        ],
        axis=0,
    )
    flat_ref[...] = result
    out_ref[...] = jnp.transpose(result).astype(low_type)


def about(microseconds):
    return pl.CostEstimate(
        flops=microseconds * 1_100_000_000, bytes_accessed=1 << 20, transcendentals=0
    )


def whole(shape):
    return pl.BlockSpec(shape, lambda *_: (0,) * len(shape))


def lanes_of(items, width):
    joint = items[0].shape[-1] != width
    return [place if joint else 0 for place in range(3)]


def attend(order, count, items, width):
    chunks, per_chunk = items[0].shape[:2]
    key_chunks = items[1].shape[0]
    frames = chunks * per_chunk
    span = width // HEAD_DIM * FRAME_TOK
    lane = lanes_of(items, width)
    return pl.pallas_call(
        attend_kernel,
        grid_spec=pltpu.PrefetchScalarGridSpec(
            num_scalar_prefetch=2,
            grid=(frames,),
            in_specs=[
                pl.BlockSpec(
                    (None, None, FRAME_TOK, width),
                    lambda i, *_: (i // per_chunk, i % per_chunk, 0, lane[0]),
                ),
                pl.BlockSpec(
                    (key_chunks, per_chunk, FRAME_TOK, width), lambda i, *_: (0, 0, 0, lane[1])
                ),
                pl.BlockSpec(
                    (key_chunks, per_chunk, FRAME_TOK, width), lambda i, *_: (0, 0, 0, lane[2])
                ),
            ],
            out_specs=[
                pl.BlockSpec(
                    (None, None, FRAME_TOK, width),
                    lambda i, *_: (i // per_chunk, i % per_chunk, 0, 0),
                ),
                pl.BlockSpec((None, width, FRAME_TOK), lambda i, *_: (i, 0, 0)),
                pl.BlockSpec((None, 1, span), lambda i, *_: (i, 0, 0)),
            ],
            scratch_shapes=[
                pltpu.VMEM((key_chunks, per_chunk, width, FRAME_TOK), low_type),
                pltpu.VMEM((key_chunks * per_chunk, FRAME_TOK, span), jnp.float32),
            ],
        ),
        out_shape=[
            jax.ShapeDtypeStruct((chunks, per_chunk, FRAME_TOK, width), low_type),
            jax.ShapeDtypeStruct((frames, width, FRAME_TOK), jnp.float32),
            jax.ShapeDtypeStruct((frames, 1, span), jnp.float32),
        ],
        compiler_params=pltpu.CompilerParams(vmem_limit_bytes=48 * 1024 * 1024),
        cost_estimate=about(45),
        name="attend",
    )(order, count, *items)


def attend_back_kernel(
    order_ref,
    count_ref,
    query_ref,
    key_ref,
    value_ref,
    grad_ref,
    flat_ref,
    log_ref,
    query_cos,
    query_sin,
    key_cos,
    key_sin,
    space_cos,
    space_sin,
    *rest,
):
    outs, (stacked_query, stacked_grad, row_dot, sums_ref) = rest[:-4], rest[-4:]
    step = pl.program_id(0)
    frames, width, _ = flat_ref.shape
    per_chunk = query_ref.shape[1]
    heads = width // HEAD_DIM
    scale = HEAD_DIM**-0.5

    @pl.when(step == 0)
    def _():
        def ready(frame, carry):
            chunk, part = frame // per_chunk, frame % per_chunk
            query = query_ref[chunk, part] * jnp.asarray(scale, low_type)
            stacked_query[frame] = head_stack(query)
            grad = grad_ref[chunk, part]
            stacked_grad[frame] = head_stack(grad)
            both = jnp.transpose(grad.astype(jnp.float32)) * flat_ref[frame]
            row_dot[frame] = jnp.concatenate(
                [
                    jnp.sum(both[head * HEAD_DIM : (head + 1) * HEAD_DIM], axis=0, keepdims=True)
                    for head in range(heads)
                ],
                axis=1,
            )
            sums_ref[frame] = jnp.zeros((width, FRAME_TOK), jnp.float32)
            return carry

        lax.fori_loop(0, frames, ready, 0)

    keys = key_ref[...]
    values = value_ref[...]
    turned_keys = jnp.transpose(keys)

    def several(base, count, carry):
        grad_keys, grad_values = carry
        frames_now = [order_ref[base + i] for i in range(count)]
        updates = []
        scores = [against(keys, stacked_query[frame]) for frame in frames_now]
        grad_chances = [against(values, stacked_grad[frame]) for frame in frames_now]
        for frame, score, grad_chance in zip(frames_now, scores, grad_chances):
            chances = jnp.exp(score - log_ref[frame])
            grad_scores = (chances * (grad_chance - row_dot[frame])).astype(low_type)
            grad_values = grad_values + product(chances.astype(low_type), stacked_grad[frame])
            grad_keys = grad_keys + product(grad_scores, stacked_query[frame])
            for head in range(heads):
                rows = slice(head * HEAD_DIM, (head + 1) * HEAD_DIM)
                updates.append(
                    product(
                        turned_keys[rows],
                        grad_scores[:, head * FRAME_TOK : (head + 1) * FRAME_TOK],
                    )
                )
        for i, frame in enumerate(frames_now):
            for head in range(heads):
                rows = slice(head * HEAD_DIM, (head + 1) * HEAD_DIM)
                sums_ref[frame, rows, :] += updates[i * heads + head]
        return grad_keys, grad_values

    zero = jnp.zeros((FRAME_TOK, width), jnp.float32)
    total = count_ref[step]
    carry = lax.fori_loop(
        0, total // UNROLL, lambda i, c: several(i * UNROLL, UNROLL, c), (zero, zero)
    )
    grad_keys, grad_values = lax.fori_loop(
        total // UNROLL * UNROLL, total, lambda i, c: several(i, 1, c), carry
    )
    space_c, space_s = space_cos[:, :width], space_sin[:, :width]

    def store(part, frame, value):
        place = (frame // per_chunk, frame % per_chunk)
        if len(outs) == 1:
            outs[0][place + (slice(None), slice(part * width, (part + 1) * width))] = value
        else:
            outs[part][place] = value

    store(2, step, grad_values.astype(low_type))
    store(
        1,
        step,
        (
            grad_keys * (key_cos[:, :width] + space_c)
            - partner(grad_keys) * (key_sin[:, :width] + space_s)
        ).astype(low_type),
    )

    @pl.when(step == pl.num_programs(0) - 1)
    def _():
        def finish(frame, carry):
            value = jnp.transpose(sums_ref[frame]) * scale
            store(
                0,
                frame,
                (
                    value * (query_cos[frame][:, :width] + space_c)
                    - partner(value) * (query_sin[frame][:, :width] + space_s)
                ).astype(low_type),
            )
            return carry

        lax.fori_loop(0, frames, finish, 0)


def attend_back(order, count, items, grads, flat, logs, query_times, key_times, spaces):
    per_chunk, width = grads.shape[1], grads.shape[3]
    frames = flat.shape[0]
    key_frames = items[1].shape[0] * per_chunk
    span = width // HEAD_DIM * FRAME_TOK
    lane = lanes_of(items, width)

    def key_spec(place):
        return pl.BlockSpec(
            (None, None, FRAME_TOK, width), lambda i, *_: (i // per_chunk, i % per_chunk, 0, place)
        )

    key_time = pl.BlockSpec((None, 1, LANES), lambda i, *_: (i, 0, 0))
    if lane[1]:
        shapes = [items[0].shape]
    else:
        shapes = [item.shape for item in items]
    return pl.pallas_call(
        attend_back_kernel,
        grid_spec=pltpu.PrefetchScalarGridSpec(
            num_scalar_prefetch=2,
            grid=(key_frames,),
            in_specs=[
                whole(grads.shape),
                key_spec(lane[1]),
                key_spec(lane[2]),
                whole(grads.shape),
                whole(flat.shape),
                whole(logs.shape),
                whole(query_times[0].shape),
                whole(query_times[1].shape),
                key_time,
                key_time,
                whole(spaces[0].shape),
                whole(spaces[1].shape),
            ],
            out_specs=[whole(shape) for shape in shapes],
            scratch_shapes=[
                pltpu.VMEM((frames, span, width), low_type),
                pltpu.VMEM((frames, span, width), low_type),
                pltpu.VMEM((frames, 1, span), jnp.float32),
                pltpu.VMEM((frames, width, FRAME_TOK), jnp.float32),
            ],
        ),
        out_shape=[jax.ShapeDtypeStruct(shape, low_type) for shape in shapes],
        compiler_params=pltpu.CompilerParams(vmem_limit_bytes=56 * 1024 * 1024),
        cost_estimate=about(65),
        name="attend_back",
    )(order, count, *items, grads, flat, logs, *query_times, *key_times, *spaces)


def flat_weight(ref):
    return ref[...].reshape(-1, ref.shape[-1])


def project_kernel(
    heads_ref, weight_ref, hidden_ref, mods_ref, attended_ref, branch_ref, next_ref, mixed_ref
):
    attended = jnp.concatenate([heads_ref[group] for group in range(heads_ref.shape[0])], axis=1)
    attended_ref[...] = attended
    branch = product(attended, flat_weight(weight_ref))
    branch_ref[...] = branch
    hidden = hidden_ref[...] + mods_ref[2:3] * branch
    next_ref[...] = hidden
    normed, _ = norm_parts(hidden)
    mixed_ref[...] = (normed * (1.0 + mods_ref[4:5]) + mods_ref[3:4]).astype(low_type)


def project_norm(heads, weights, hidden, mods):
    groups, tokens, width = heads.shape
    devices, height, _ = weights.shape
    rows = D // devices
    by_frame = pl.BlockSpec((FRAME_TOK, D), lambda i: (i, 0))
    wide = jax.ShapeDtypeStruct((tokens, D), jnp.float32)
    low = jax.ShapeDtypeStruct((tokens, D), low_type)
    return pl.pallas_call(
        project_kernel,
        grid=(tokens // FRAME_TOK,),
        in_specs=[
            pl.BlockSpec((groups, FRAME_TOK, width), lambda i: (0, i, 0)),
            pl.BlockSpec((devices, rows, D), lambda i: (0, FF // D, 0)),
            by_frame,
            pl.BlockSpec((None, 6, D), lambda i: (i, 0, 0)),
        ],
        out_specs=[by_frame] * 4,
        out_shape=[low, wide, wide, low],
        compiler_params=pltpu.CompilerParams(vmem_limit_bytes=60 * 1024 * 1024),
        cost_estimate=about(4),
        name="project_norm",
    )(heads, weights, hidden, mods)


GELU_OUT = math.sqrt(2.0 / math.pi)
GELU_CUBE = 0.044715


def forward_kernel(
    scale_ref,
    mixed_ref,
    expand_ref,
    reduce_ref,
    hidden_ref,
    mods_ref,
    readout_ref,
    noise_ref,
    inner_ref,
    active_ref,
    grad_hidden_ref,
    grad_outer_ref,
    grad_readout_ref,
    grad_gate_ref,
    loss_ref,
    outer_ref,
):
    step = pl.program_id(0)
    frames = mods_ref.shape[0]
    inner = product(mixed_ref[...], flat_weight(expand_ref))
    inner_ref[...] = inner
    bend = jnp.tanh(GELU_OUT * (inner + GELU_CUBE * (inner * inner * inner)))
    active = (0.5 * inner * (1.0 + bend)).astype(low_type)
    active_ref[...] = active
    part = product(active, flat_weight(reduce_ref))

    @pl.when(step == 0)
    def _():
        outer_ref[...] = part

    @pl.when(step > 0)
    def _():
        outer_ref[...] += part

    @pl.when(step == pl.num_programs(0) - 1)
    def _():
        readout = readout_ref[...][:, PATCH_FEAT : 2 * PATCH_FEAT]
        grad_readout = jnp.zeros((D, PATCH_FEAT), jnp.float32)
        for frame in range(frames):
            tokens = slice(frame * FRAME_TOK, (frame + 1) * FRAME_TOK)
            outer = outer_ref[tokens]
            gate = mods_ref[frame, 5:6]
            final, inverse = norm_parts(hidden_ref[tokens] + gate * outer)
            final_low = final.astype(low_type)
            residue = product(final_low, readout) - noise_ref[tokens]
            loss_ref[frame] = jnp.zeros((1, LANES), jnp.float32) + jnp.sum(residue * residue)
            grad_pred = (residue * scale_ref[frame]).astype(low_type)
            grad_readout += across(final_low, grad_pred)
            grad_hidden = norm_back(final, inverse, against(grad_pred, readout))
            grad_hidden_ref[tokens] = grad_hidden
            grad_outer_ref[tokens] = (gate * grad_hidden).astype(low_type)
            grad_gate_ref[frame] = row_sum(grad_hidden * outer)
        grad_readout_ref[...] = grad_readout


def feed_forward(loss_scale, mixed, weights, hidden, mods, first_weights, noise):
    tokens = mixed.shape[0]
    devices, height, _ = weights.shape
    rows = D // devices
    frames = mods.shape[0]
    pieces = FF // D
    wide = jax.ShapeDtypeStruct((tokens, D), jnp.float32)
    by_piece = pl.BlockSpec((tokens, D), lambda k, *_: (0, k))
    return pl.pallas_call(
        forward_kernel,
        grid_spec=pltpu.PrefetchScalarGridSpec(
            num_scalar_prefetch=1,
            grid=(pieces,),
            in_specs=[
                whole((tokens, D)),
                pl.BlockSpec((devices, rows, D), lambda k, *_: (0, pieces + 1 + k, 0)),
                pl.BlockSpec((devices // pieces, pieces * rows, D), lambda k, *_: (k, 0, 0)),
                whole((tokens, D)),
                whole(mods.shape),
                pl.BlockSpec((D, LANES), lambda k, *_: (0, 3 * D // LANES)),
                whole((tokens, PATCH_FEAT)),
            ],
            out_specs=[
                by_piece,
                by_piece,
                whole((tokens, D)),
                whole((tokens, D)),
                whole((D, PATCH_FEAT)),
                whole((frames, 1, D)),
                whole((frames, 1, LANES)),
            ],
            scratch_shapes=[pltpu.VMEM((tokens, D), jnp.float32)],
        ),
        out_shape=[
            jax.ShapeDtypeStruct((tokens, FF), jnp.float32),
            jax.ShapeDtypeStruct((tokens, FF), low_type),
            wide,
            jax.ShapeDtypeStruct((tokens, D), low_type),
            jax.ShapeDtypeStruct((D, PATCH_FEAT), jnp.float32),
            jax.ShapeDtypeStruct((frames, 1, D), jnp.float32),
            jax.ShapeDtypeStruct((frames, 1, LANES), jnp.float32),
        ],
        compiler_params=pltpu.CompilerParams(vmem_limit_bytes=60 * 1024 * 1024),
        cost_estimate=about(20),
        name="feed_forward",
    )(loss_scale, mixed, weights, weights, hidden, mods, first_weights, noise)


def backward_kernel(
    grad_outer_ref,
    reduce_ref,
    expand_ref,
    inner_ref,
    hidden_ref,
    grad_hidden_ref,
    branch_ref,
    mods_ref,
    project_ref,
    grad_inner_ref,
    grad_one_ref,
    grad_branch_ref,
    heads_ref,
    grad_mods_ref,
    grad_mixed_ref,
):
    step = pl.program_id(0)
    frames = mods_ref.shape[0]
    groups, _, width = heads_ref.shape
    inner = inner_ref[...]
    square = inner * inner
    bend = jnp.tanh(GELU_OUT * (inner + GELU_CUBE * (square * inner)))
    slope = 0.5 * (1.0 + bend) + 0.5 * inner * (1.0 - bend * bend) * (
        GELU_OUT * (1.0 + 3.0 * GELU_CUBE * square)
    )
    grad_active = against(grad_outer_ref[...], flat_weight(reduce_ref))
    grad_inner = (grad_active * slope).astype(low_type)
    grad_inner_ref[...] = grad_inner
    part = against(grad_inner, flat_weight(expand_ref))

    @pl.when(step == 0)
    def _():
        grad_mixed_ref[...] = part

    @pl.when(step > 0)
    def _():
        grad_mixed_ref[...] += part

    @pl.when(step == pl.num_programs(0) - 1)
    def _():
        project = flat_weight(project_ref)
        for frame in range(frames):
            tokens = slice(frame * FRAME_TOK, (frame + 1) * FRAME_TOK)
            normed, inverse = norm_parts(hidden_ref[tokens])
            grad_mixed = grad_mixed_ref[tokens]
            grad_mods_ref[frame, 1:2] = row_sum(grad_mixed)
            grad_mods_ref[frame, 2:3] = row_sum(grad_mixed * normed)
            grad_one = grad_hidden_ref[tokens] + norm_back(
                normed, inverse, grad_mixed * (1.0 + mods_ref[frame, 4:5])
            )
            grad_one_ref[tokens] = grad_one
            grad_mods_ref[frame, 0:1] = row_sum(grad_one * branch_ref[tokens])
            grad_branch = (mods_ref[frame, 2:3] * grad_one).astype(low_type)
            grad_branch_ref[tokens] = grad_branch
            grad_attended = against(grad_branch, project).astype(low_type)
            for group in range(groups):
                heads_ref[group, tokens] = grad_attended[:, group * width : (group + 1) * width]


def feed_backward(grad_outer, weights, inner, hidden, grad_hidden, branch, mods, groups):
    tokens = hidden.shape[0]
    devices, height, _ = weights.shape
    rows = D // devices
    frames = mods.shape[0]
    pieces = FF // D
    by_piece = pl.BlockSpec((tokens, D), lambda k: (0, k))
    return pl.pallas_call(
        backward_kernel,
        grid=(pieces,),
        in_specs=[
            whole((tokens, D)),
            pl.BlockSpec((devices // pieces, pieces * rows, D), lambda k: (k, 0, 0)),
            pl.BlockSpec((devices, rows, D), lambda k: (0, pieces + 1 + k, 0)),
            by_piece,
            whole((tokens, D)),
            whole((tokens, D)),
            whole((tokens, D)),
            whole(mods.shape),
            pl.BlockSpec((devices, rows, D), lambda k: (0, pieces, 0)),
        ],
        out_specs=[
            by_piece,
            whole((tokens, D)),
            whole((tokens, D)),
            whole((groups, tokens, D // groups)),
            whole((frames, 3, D)),
        ],
        out_shape=[
            jax.ShapeDtypeStruct((tokens, FF), low_type),
            jax.ShapeDtypeStruct((tokens, D), jnp.float32),
            jax.ShapeDtypeStruct((tokens, D), low_type),
            jax.ShapeDtypeStruct((groups, tokens, D // groups), low_type),
            jax.ShapeDtypeStruct((frames, 3, D), jnp.float32),
        ],
        scratch_shapes=[pltpu.VMEM((tokens, D), jnp.float32)],
        compiler_params=pltpu.CompilerParams(vmem_limit_bytes=60 * 1024 * 1024),
        cost_estimate=about(22),
        name="feed_backward",
    )(grad_outer, weights, weights, inner, hidden, grad_hidden, branch, mods, weights)


def grads_kernel(
    active_ref, grad_outer_ref, attended_ref, grad_branch_ref, mixed_ref, grad_inner_ref, out_ref
):
    cores, lines, height, _ = out_ref.shape
    pieces = FF // D
    rows = height // (2 * pieces + 1)

    def store(start, count, value):
        value = value.astype(low_type)
        for line in range(lines):
            for core in range(cores):
                at = (line * cores + core) * count
                out_ref[core, line, start : start + count] = value[at : at + count]

    store(0, pieces * rows, across(active_ref[...], grad_outer_ref[...]))
    store(pieces * rows, rows, across(attended_ref[...], grad_branch_ref[...]))
    for piece in range(pieces):
        store(
            (pieces + 1 + piece) * rows,
            rows,
            across(mixed_ref[...], grad_inner_ref[:, piece * D : (piece + 1) * D]),
        )


def weight_grads(sizes, active, grad_outer, attended, grad_branch, mixed, grad_inner):
    batch, row, core = sizes
    tokens = mixed.shape[0]
    rows = D // (batch * row * core)
    height = rows * (2 * (FF // D) + 1)
    part = pl.BlockSpec((tokens, D // batch), lambda i: (0, i))
    return pl.pallas_call(
        grads_kernel,
        grid=(batch,),
        in_specs=[
            pl.BlockSpec((tokens, FF // batch), lambda i: (0, i)),
            whole((tokens, D)),
            part,
            whole((tokens, D)),
            part,
            whole((tokens, FF)),
        ],
        out_specs=pl.BlockSpec((None, core, row, height, D), lambda i: (i, 0, 0, 0, 0)),
        out_shape=jax.ShapeDtypeStruct((batch, core, row, height, D), low_type),
        compiler_params=pltpu.CompilerParams(vmem_limit_bytes=56 * 1024 * 1024),
        cost_estimate=about(28),
        name="weight_grads",
    )(active, grad_outer, attended, grad_branch, mixed, grad_inner)


def update_kernel(rates, factor_ref, *refs):
    for item, rate in enumerate(rates):
        master, first, second, gradient = (refs[4 * item + part][...] for part in range(4))
        new = adamw_update(master, first, second, gradient, factor_ref[0], rate)
        for part in range(3):
            refs[4 * len(rates) + 3 * item + part][...] = new[part]


def update(factor, states, rates):
    flat = [array for state in states for array in state]
    steps = 4
    specs = [
        pl.BlockSpec((array.shape[0], array.shape[1] // steps), lambda i, *_: (0, i))
        for array in flat
    ]
    outs = [4 * item + part for item in range(len(states)) for part in (1, 2, 0)]
    new = pl.pallas_call(
        functools.partial(update_kernel, rates),
        grid_spec=pltpu.PrefetchScalarGridSpec(
            num_scalar_prefetch=1,
            grid=(steps,),
            in_specs=specs,
            out_specs=[specs[out] for out in outs],
        ),
        out_shape=[jax.ShapeDtypeStruct(flat[out].shape, jnp.float32) for out in outs],
        compiler_params=pltpu.CompilerParams(vmem_limit_bytes=60 * 1024 * 1024),
        cost_estimate=about(7),
        name="update",
    )(factor.reshape(1), *flat)
    return [new[3 * item : 3 * item + 3] for item in range(len(states))]


def swapped(value, axis, offset):
    return lax.ppermute(value, axis, [(i, i ^ offset) for i in range(lax.axis_size(axis))])


def gather_near(value, axes=("core", "batch", "row")):
    for axis in axes:
        others = [swapped(value, axis, offset) for offset in range(1, lax.axis_size(axis))]
        value = jnp.concatenate([value] + others, axis=0)
    return value


def near_owner(index):
    batch, row, core = (lax.axis_size(axis) for axis in ALL)
    places = (
        (index // core % batch) ^ lax.axis_index("batch"),
        (index // (core * batch)) ^ lax.axis_index("row"),
        (index % core) ^ lax.axis_index("core"),
    )
    return (places[0] * row + places[1]) * core + places[2]


def exchange_sum(value, axes, at=0, sent=jnp.float32):
    count = value.shape[at]
    mine = lax.axis_index(axes)
    total = lax.dynamic_index_in_dim(value, mine, at, keepdims=False)
    parts = [
        lax.ppermute(
            lax.dynamic_index_in_dim(value, mine ^ offset, at, keepdims=False).astype(sent),
            axes,
            [(i, i ^ offset) for i in range(count)],
        )
        for offset in range(1, count)
    ]
    for part in parts:
        total = total + part.astype(jnp.float32)
    return total


def total_sum(value):
    for axis in ("core", "batch", "row"):
        parts = [value] + [
            swapped(value, axis, offset) for offset in range(1, lax.axis_size(axis))
        ]
        while len(parts) > 1:
            parts = [parts[i] + parts[i + 1] for i in range(0, len(parts), 2)]
        value = parts[0]
    return value


def per_device(
    clean_latents,
    noise_sample,
    noise_levels,
    clean_flags,
    span_frame,
    patch_master,
    patch_first,
    patch_second,
    level_master,
    level_first,
    level_second,
    adaptive_master,
    adaptive_first,
    adaptive_second,
    triple_master,
    triple_first,
    triple_second,
    project_master,
    project_first,
    project_second,
    expand_master,
    expand_first,
    expand_second,
    reduce_master,
    reduce_first,
    reduce_second,
    readout_master,
    readout_first,
    readout_second,
):
    masters = (
        patch_master,
        level_master,
        adaptive_master,
        triple_master,
        project_master,
        expand_master,
        reduce_master,
        readout_master,
    )
    firsts = (
        patch_first,
        level_first,
        adaptive_first,
        triple_first,
        project_first,
        expand_first,
        reduce_first,
        readout_first,
    )
    seconds = (
        patch_second,
        level_second,
        adaptive_second,
        triple_second,
        project_second,
        expand_second,
        reduce_second,
        readout_second,
    )
    batch_count, row_count, core_count = (lax.axis_size(axis) for axis in ALL)
    batch_index, row_index, core_index = (lax.axis_index(axis) for axis in ALL)
    devices = batch_count * row_count * core_count
    rows = D // devices
    token_count = clean_latents.shape[1]
    frame_local = token_count // FRAME_TOK

    moved = batch_count == row_count and HEADS % (batch_count * core_count) == 0
    if moved:
        clip_index, chunk_index = row_index, batch_index * core_count + core_index
        head_axes, head_groups = ("batch", "core"), batch_count * core_count
        rest_axes = ("row",)
    else:
        clip_index, chunk_index = batch_index, row_index * core_count + core_index
        head_axes, head_groups = ("row",), row_count
        rest_axes = ("batch", "core")

    both = jnp.concatenate([clean_latents[0], noise_sample[0]], axis=1)
    if moved:
        turn = [
            (
                (a * row_count + b) * core_count + c,
                (b * row_count + a) * core_count + c,
            )
            for a in range(batch_count)
            for b in range(row_count)
            for c in range(core_count)
        ]
        both = lax.ppermute(both, ALL, turn)
    clean_tok, noise_tok = both[:, :PATCH_FEAT], both[:, PATCH_FEAT:]

    first_weights = jnp.concatenate(
        [
            triple_master.astype(low_type),
            jnp.transpose(patch_master).astype(low_type),
            readout_master.astype(low_type),
            jnp.zeros((rows, LANES - 2 * PATCH_FEAT), low_type),
        ],
        axis=1,
    )
    first_weights = lax.all_gather(first_weights, ALL, axis=0, tiled=True)
    second_weights = jnp.concatenate(
        [reduce_master.astype(low_type), project_master.astype(low_type)]
        + [expand_master[:, k * D : (k + 1) * D].astype(low_type) for k in range(FF // D)],
        axis=0,
    )
    second_weights = lax.all_gather(second_weights, ALL, axis=0)

    levels_all = noise_levels.reshape(-1)
    flags_all = clean_flags.reshape(-1)
    _, _, index_all = plan(levels_all, flags_all)
    if moved:
        order_all = lambda v: (
            v.reshape((row_count, batch_count, core_count, frame_local) + v.shape[1:])
            .swapaxes(0, 1)
            .reshape(v.shape)
        )
    else:
        order_all = lambda v: v
    index_all = order_all(index_all)
    every = jnp.arange(devices, dtype=jnp.int32)
    index_near = jnp.sum(
        jnp.where(
            (near_owner(every)[:, None] == every[None, :])[..., None],
            index_all.reshape(1, devices, frame_local),
            0,
        ),
        axis=1,
    ).reshape(-1)
    table_low = level_master.astype(low_type).astype(jnp.float32)

    def table_rows(index):
        hot = (index[:, None] == jnp.arange(NB + 1, dtype=jnp.int32)[None, :]).astype(jnp.float32)
        return hot, jnp.dot(hot, table_low, precision=lax.Precision.HIGHEST)

    _, pre_own = table_rows(index_all)
    hot_near, pre_near = table_rows(index_near)
    cond_near, silu_back = jax.vjp(jax.nn.silu, pre_near)
    cond_near = cond_near.astype(low_type)
    cond_own = jax.nn.silu(pre_own).astype(low_type)
    adaptive_low = adaptive_master.astype(low_type)
    adapt = product(cond_own, adaptive_low).reshape(devices, frame_local, 6 * D)
    mods = jnp.sum(lax.all_to_all(adapt, ALL, 0, 0, tiled=True), axis=0)
    mods = mods.reshape(frame_local, 6, D)

    my_levels = lax.dynamic_slice_in_dim(
        lax.dynamic_index_in_dim(noise_levels, clip_index, 0, keepdims=False),
        chunk_index * frame_local,
        frame_local,
    )
    my_flags = lax.dynamic_slice_in_dim(
        lax.dynamic_index_in_dim(clean_flags, clip_index, 0, keepdims=False),
        chunk_index * frame_local,
        frame_local,
    )
    my_frames = lax.dynamic_slice_in_dim(span_frame, chunk_index * frame_local, frame_local)
    if moved:
        query_frames = key_frames = span_frame
    else:
        by_chunk = span_frame.reshape(row_count, core_count, frame_local)
        query_frames = lax.dynamic_index_in_dim(by_chunk, core_index, 1, keepdims=False).reshape(-1)
        key_frames = by_chunk.swapaxes(0, 1).reshape(-1)
    query_total, key_total = query_frames.shape[0], key_frames.shape[0]
    earlier = jnp.sum(key_frames[None, :] < key_frames[:, None], axis=1)
    key_order = jnp.sum(
        jnp.where(earlier[:, None] == jnp.arange(key_total)[None, :], jnp.arange(key_total)[:, None], 0),
        axis=0,
    ).astype(jnp.int32)
    key_count = jnp.sum(key_frames[None, :] <= query_frames[:, None], axis=1).astype(jnp.int32)
    later = jnp.sum(query_frames[None, :] > query_frames[:, None], axis=1)
    query_order = jnp.sum(
        jnp.where(later[:, None] == jnp.arange(query_total)[None, :], jnp.arange(query_total)[:, None], 0),
        axis=0,
    ).astype(jnp.int32)
    query_count = jnp.sum(query_frames[None, :] >= key_frames[:, None], axis=1).astype(jnp.int32)
    my_times, query_times, key_times = (
        time_tables(my_frames),
        time_tables(query_frames),
        time_tables(key_frames),
    )
    spaces = space_tables()

    alpha_bar, noised, _ = plan(my_levels, my_flags)
    inputs = noised_input(clean_tok, noise_tok, alpha_bar, noised).astype(low_type)
    width = D // head_groups
    hidden_zero, normed_low, heads = triple_heads(
        inputs, mods, first_weights, my_times, spaces, head_groups
    )
    heads = lax.all_to_all(heads, head_axes, 0, 0, tiled=True)
    if moved:
        heads = heads.reshape(head_groups, frame_local, FRAME_TOK, 3 * width)
        items = (heads, heads, heads)
    else:
        heads = heads.reshape(head_groups, 3, frame_local, FRAME_TOK, width)
        items = (heads[:, 0],) + tuple(
            lax.all_gather(heads[:, part], "core", axis=0, tiled=True) for part in (1, 2)
        )
    attended, flat, logs = attend(key_order, key_count, items, width)
    attended = attended.reshape(head_groups, token_count, width)
    attended = lax.all_to_all(attended, head_axes, 0, 0, tiled=True)
    attended, normed_low = lax.optimization_barrier((attended, normed_low))
    normed_clip = lax.all_gather(normed_low, head_axes, axis=0, tiled=True)
    attended_low, branch, hidden_one, mixed_low = project_norm(
        attended, second_weights, hidden_zero, mods
    )
    frame_count = jnp.sum((1 - clean_flags).astype(jnp.float32))
    loss_scale = noised * (2.0 / (FRAME_TOK * PATCH_FEAT)) / jnp.maximum(frame_count, 1.0)
    (
        inner,
        active_low,
        grad_hidden_two,
        grad_outer,
        grad_readout,
        grad_gate_two,
        squared,
    ) = feed_forward(
        loss_scale, mixed_low, second_weights, hidden_one, mods, first_weights, noise_tok
    )
    frame_loss = squared[:, 0, 0] * (1.0 / (FRAME_TOK * PATCH_FEAT)) * noised
    grad_inner_low, grad_hidden_one, grad_branch, grad_attended, grad_mods = feed_backward(
        grad_outer,
        second_weights,
        inner,
        hidden_one,
        grad_hidden_two,
        branch,
        mods,
        head_groups,
    )
    grad_attended = lax.all_to_all(grad_attended, head_axes, 0, 0, tiled=True)
    grad_attended = grad_attended.reshape(head_groups, frame_local, FRAME_TOK, width)
    early_adapt = jnp.concatenate(
        [grad_mods.reshape(frame_local, 3 * D), grad_gate_two.reshape(frame_local, D)], axis=1
    ).astype(low_type)
    early_adapt = gather_near(early_adapt, ("core", "batch"))
    grad_attended, early_adapt = lax.optimization_barrier((grad_attended, early_adapt))
    early_adapt = gather_near(early_adapt, ("row",))

    second_grads = weight_grads(
        (batch_count, row_count, core_count),
        active_low,
        grad_outer,
        attended_low,
        grad_branch,
        mixed_low,
        grad_inner_low,
    )
    second_own = lax.psum_scatter(
        second_grads.reshape((-1,) + second_grads.shape[2:]),
        ("batch", "core"),
        scatter_dimension=0,
    )

    grads = attend_back(
        query_order,
        query_count,
        items,
        grad_attended,
        flat,
        logs,
        query_times,
        key_times,
        spaces,
    )
    if moved:
        grad_heads = grads[0].reshape(head_groups, token_count, 3 * width)
    else:
        grad_heads = [grads[0]] + [
            lax.psum_scatter(
                item.astype(jnp.float32), "core", scatter_dimension=0, tiled=True
            ).astype(low_type)
            for item in grads[1:]
        ]
        grad_heads = jnp.concatenate(grad_heads, axis=-1).reshape(
            head_groups, token_count, 3 * width
        )
    grad_triple = across(
        normed_clip.reshape(-1, D), grad_heads.reshape(head_groups * token_count, 3 * width)
    )
    grad_heads = lax.all_to_all(grad_heads, head_axes, 0, 0, tiled=True)
    if not moved:
        grad_heads = grad_heads.reshape(head_groups, token_count, 3, width).swapaxes(1, 2)
    grad_triple = grad_triple.reshape(batch_count, row_count, core_count, rows, 3 * width)
    if moved:
        grad_triple = grad_triple.transpose(1, 0, 2, 3, 4)
    else:
        grad_triple = grad_triple.transpose(0, 2, 1, 3, 4)
    rest_count = devices // head_groups
    triple_own = exchange_sum(
        grad_triple.reshape(rest_count, head_groups, rows, 3 * width),
        rest_axes,
        sent=low_type,
    )
    grad_heads, triple_own, early_adapt = lax.optimization_barrier(
        (grad_heads, triple_own, early_adapt)
    )
    grad_shift, grad_patch = triple_back(
        grad_heads, first_weights, hidden_zero, grad_hidden_one, mods, inputs, head_groups
    )
    second_own, grad_shift = lax.optimization_barrier((second_own, grad_shift))
    second_own = lax.psum_scatter(second_own, "row", scatter_dimension=0).astype(jnp.float32)
    late_adapt = gather_near(grad_shift.reshape(frame_local, 2 * D).astype(low_type))
    small = jnp.concatenate([grad_patch, grad_readout], axis=1)
    small = small.reshape(batch_count, row_count, core_count, -1, LANES)
    small = exchange_sum(small, "core", 2)
    small = exchange_sum(small, "batch")
    small_own = exchange_sum(small, "row").reshape(rows, 2 * PATCH_FEAT)

    triple_own = lax.all_to_all(triple_own, head_axes, 0, 0, tiled=True)
    triple_own = (
        triple_own.reshape(head_groups, rows, 3, width).transpose(1, 2, 0, 3).reshape(rows, 3 * D)
    )
    early_columns = 2 * D
    adapt_own = jnp.concatenate(
        [across(cond_near, late_adapt), across(cond_near, early_adapt)], axis=1
    )
    grad_cond = against(late_adapt, adaptive_low[:, :early_columns]) + against(
        early_adapt, adaptive_low[:, early_columns:]
    )
    (grad_pre,) = silu_back(grad_cond)
    table_own = lax.dot_general(
        hot_near,
        grad_pre,
        (((0,), (0,)), ((), ())),
        precision=lax.Precision.HIGHEST,
        preferred_element_type=jnp.float32,
    )
    expand_own = jnp.concatenate(
        [
            second_own[(FF // D + 1 + k) * rows : (FF // D + 2 + k) * rows]
            for k in range(FF // D)
        ],
        axis=1,
    )
    reduced = (
        jnp.transpose(small_own[:, :PATCH_FEAT]),
        table_own,
        adapt_own,
        triple_own,
        second_own[FF // D * rows : (FF // D + 1) * rows],
        expand_own,
        second_own[: FF // D * rows],
        small_own[:, PATCH_FEAT:],
    )
    squares = sum(
        jnp.sum(gradient * gradient)
        for gradient in (small_own, table_own, adapt_own, triple_own, second_own)
    )
    lane = jnp.arange(LANES, dtype=jnp.int32)
    bucket_lanes = jnp.sum(
        jnp.where(my_levels[:, None] == lane[None], frame_loss[:, None], 0.0), axis=0
    )
    sums = jnp.stack(
        [bucket_lanes, jnp.full((LANES,), squares), jnp.full((LANES,), jnp.sum(frame_loss))]
    )
    sums = total_sum(sums)
    clip_norm = jnp.sqrt(sums[1, 0])
    factor = jnp.minimum(1.0, clip_bound / clip_norm)
    states = [
        (masters[item], firsts[item], seconds[item], reduced[item]) for item in range(len(reduced))
    ]
    large = (2, 3, 4, 5, 6)
    updated = update(
        factor, [states[item] for item in large], tuple(learn_rates[item] for item in large)
    )
    new = [
        updated[large.index(item)]
        if item in large
        else adamw_update(*states[item], factor, learn_rates[item])
        for item in range(len(states))
    ]
    return (sums[2, 0], frame_count, sums[0, :NB], clip_norm) + tuple(
        item for triple in new for item in triple
    )


def solution(mesh):
    in_specs = (
        P("batch", ("row", "core"), None),
        P("batch", ("row", "core"), None),
        P(),
        P(),
        P(),
        P(None, ALL),
        P(None, ALL),
        P(None, ALL),
        P(None, ALL),
        P(None, ALL),
        P(None, ALL),
        P(ALL, None),
        P(ALL, None),
        P(ALL, None),
        P(ALL, None),
        P(ALL, None),
        P(ALL, None),
        P(ALL, None),
        P(ALL, None),
        P(ALL, None),
        P(ALL, None),
        P(ALL, None),
        P(ALL, None),
        P(ALL, None),
        P(ALL, None),
        P(ALL, None),
        P(ALL, None),
        P(ALL, None),
        P(ALL, None),
    )
    out_specs = (
        P(),
        P(),
        P(),
        P(),
        P(None, ALL),
        P(None, ALL),
        P(None, ALL),
        P(None, ALL),
        P(None, ALL),
        P(None, ALL),
        P(ALL, None),
        P(ALL, None),
        P(ALL, None),
        P(ALL, None),
        P(ALL, None),
        P(ALL, None),
        P(ALL, None),
        P(ALL, None),
        P(ALL, None),
        P(ALL, None),
        P(ALL, None),
        P(ALL, None),
        P(ALL, None),
        P(ALL, None),
        P(ALL, None),
        P(ALL, None),
        P(ALL, None),
        P(ALL, None),
    )
    batch_size, blk_size = mesh.shape["batch"], mesh.shape["blk"]
    inner = Mesh(mesh.devices.reshape(batch_size, blk_size // 2, 2), ALL)
    return jax.shard_map(
        per_device, mesh=inner, in_specs=in_specs, out_specs=out_specs, check_vma=False
    )
```

```python
import functools
import math

import jax
import jax.numpy as jnp
from jax import lax
from jax.experimental import pallas as pl
from jax.experimental.pallas import tpu as pltpu
from jax.sharding import Mesh
from jax.sharding import PartitionSpec as P

D = 1024
HEADS = 16
HEAD_DIM = 64
FF = 4096
PATCH_FEAT = 16
FRAME_TOK = 256
SIDE = 16
NB = 32
STEP = 10
LANES = 128
ALL = ("batch", "row", "core")


learn_rates = (0.5, 2.0, 0.05, 0.05, 0.5, 0.05, 0.05, 0.05)
beta_first = 0.9
beta_second = 0.999
decay_rate = 0.01
adam_floor = 1e-08
clip_bound = 0.02
low_type = jnp.bfloat16


def product(left, right):
    return jnp.dot(left, right, preferred_element_type=jnp.float32)


def across(left, right):
    return lax.dot_general(
        left, right, (((0,), (0,)), ((), ())), preferred_element_type=jnp.float32
    )


def against(left, right):
    return lax.dot_general(
        left, right, (((1,), (1,)), ((), ())), preferred_element_type=jnp.float32
    )


def plan(levels, clean_flags):
    alpha_bar = jnp.cos(0.5 * math.pi * (levels.astype(jnp.float32) + 1.0) / (NB + 1.0)) ** 2
    noised = (1 - clean_flags).astype(jnp.float32)
    table_index = jnp.where(clean_flags == 1, 0, levels + 1)
    return (alpha_bar, noised, table_index)


def noised_input(clean_tok, noise_tok, alpha_bar, noised):
    frame_shape = (alpha_bar.shape[0], -1, clean_tok.shape[-1])
    clean_frames = clean_tok.reshape(frame_shape)
    noise_frames = noise_tok.reshape(frame_shape)
    mixed_tok = (
        jnp.sqrt(alpha_bar)[:, None, None] * clean_frames
        + jnp.sqrt(1.0 - alpha_bar)[:, None, None] * noise_frames
    )
    return jnp.where(noised[:, None, None] > 0.5, mixed_tok, clean_frames).reshape(clean_tok.shape)


def adamw_update(master, first_moment, second_moment, gradient, factor, step_rate):
    clipped = gradient * factor
    first_new = beta_first * first_moment + (1.0 - beta_first) * clipped
    second_new = beta_second * second_moment + (1.0 - beta_second) * clipped * clipped
    first_hat = first_new / (1.0 - beta_first**STEP)
    second_hat = second_new / (1.0 - beta_second**STEP)
    master_new = master - step_rate * (
        first_hat / (jnp.sqrt(second_hat) + adam_floor) + decay_rate * master
    )
    return (first_new, second_new, master_new)


def lane_places():
    lane = jnp.arange(LANES, dtype=jnp.int32) % HEAD_DIM
    half = HEAD_DIM // 2
    place = lane % half
    time_count = HEAD_DIM // 8
    space_count = 3 * HEAD_DIM // 16
    sign = jnp.where(lane < half, -1.0, 1.0)
    time_freq = 10000.0 ** (-(place.astype(jnp.float32)) / time_count)
    space_place = jnp.where(place < time_count + space_count, place - time_count, place - time_count - space_count)
    space_freq = 100.0 ** (-(space_place.astype(jnp.float32)) / space_count)
    is_time = place < time_count
    is_row = (place >= time_count) & (place < time_count + space_count)
    return sign, time_freq, space_freq, is_time, is_row


def time_tables(frames):
    sign, time_freq, _, is_time, _ = lane_places()
    angle = frames.astype(jnp.float32)[:, None] * time_freq[None]
    return (
        jnp.where(is_time, jnp.cos(angle), 0.0)[:, None],
        jnp.where(is_time, jnp.sin(angle) * sign, 0.0)[:, None],
    )


def space_tables():
    sign, _, space_freq, is_time, is_row = lane_places()
    token = jnp.arange(FRAME_TOK, dtype=jnp.int32)
    row_pos = (token // SIDE).astype(jnp.float32)[:, None]
    col_pos = (token % SIDE).astype(jnp.float32)[:, None]
    angle = jnp.where(is_row[None], row_pos, col_pos) * space_freq[None]
    return (
        jnp.where(is_time, 0.0, jnp.cos(angle)),
        jnp.where(is_time, 0.0, jnp.sin(angle) * sign),
    )


def partner(value):
    half = HEAD_DIM // 2
    width = value.shape[1]
    if width == LANES:
        lane = lax.broadcasted_iota(jnp.int32, value.shape, 1)
        ahead = pltpu.roll(value, width - half, 1)
        behind = pltpu.roll(value, half, 1)
        return jnp.where(lane % HEAD_DIM < half, ahead, behind)
    return jnp.concatenate([value[:, half:], value[:, :half]], axis=1)


def norm_parts(hidden):
    centred = hidden - jnp.mean(hidden, axis=-1, keepdims=True)
    variance = jnp.mean(centred * centred, axis=-1, keepdims=True)
    inverse = lax.rsqrt(variance + 1e-06)
    return centred * inverse, inverse


def norm_back(normed, inverse, grad):
    along = jnp.mean(grad * normed, axis=-1, keepdims=True)
    return inverse * (grad - jnp.mean(grad, axis=-1, keepdims=True) - normed * along)


def row_sum(value):
    return jnp.sum(value, axis=0, keepdims=True)


def triple_kernel(
    inputs_ref,
    extra_ref,
    mods_ref,
    weight_ref,
    time_cos,
    time_sin,
    space_cos,
    space_sin,
    hidden_ref,
    normed_ref,
    out_ref,
):
    column = pl.program_id(0)
    width = out_ref.shape[-1]
    frames = mods_ref.shape[0]

    @pl.when(column == 0)
    def _():
        patch = extra_ref[...][:, :PATCH_FEAT]
        for frame in range(frames):
            tokens = slice(frame * FRAME_TOK, (frame + 1) * FRAME_TOK)
            hidden = against(inputs_ref[tokens], patch)
            hidden_ref[tokens] = hidden
            normed, _ = norm_parts(hidden)
            normed_ref[tokens] = (
                normed * (1.0 + mods_ref[frame, 1:2]) + mods_ref[frame, 0:1]
            ).astype(low_type)

    acc = product(normed_ref[...], weight_ref[...])
    per_block = acc.shape[1] // LANES

    def store(piece, values):
        for part in range(LANES // width):
            at = piece * (LANES // width) + part
            done = values[:, part * width : (part + 1) * width].astype(low_type)
            if len(out_ref.shape) == 3:
                out_ref[at] = done
            else:
                out_ref[at, 0] = done

    turned = column < 2 * D // acc.shape[1]

    @pl.when(turned)
    def _():
        for piece in range(per_block):
            done = []
            for frame in range(frames):
                value = acc[
                    frame * FRAME_TOK : (frame + 1) * FRAME_TOK,
                    piece * LANES : (piece + 1) * LANES,
                ]
                cosine = time_cos[frame] + space_cos[...]
                sine = time_sin[frame] + space_sin[...]
                done.append(value * cosine + partner(value) * sine)
            store(piece, jnp.concatenate(done, axis=0))

    @pl.when(jnp.logical_not(turned))
    def _():
        for piece in range(per_block):
            store(piece, acc[:, piece * LANES : (piece + 1) * LANES])


BLOCK = 256


def heads_layout(groups, tokens):
    width = D // groups
    per_block = BLOCK // width
    per_part = D // BLOCK
    if width == LANES:
        return (groups, tokens, 3 * width), pl.BlockSpec(
            (per_block, tokens, width), lambda j: (j % per_part, 0, j // per_part)
        )
    return (groups, 3, tokens, width), pl.BlockSpec(
        (per_block, 1, tokens, width), lambda j: (j % per_part, j // per_part, 0, 0)
    )


def triple_heads(inputs, mods, weight, times, spaces, groups):
    tokens = inputs.shape[0]
    shape, spec = heads_layout(groups, tokens)
    return pl.pallas_call(
        triple_kernel,
        grid=(3 * D // BLOCK,),
        in_specs=[
            whole(inputs.shape),
            pl.BlockSpec((D, LANES), lambda j: (0, 3 * D // LANES)),
            whole(mods.shape),
            pl.BlockSpec((D, BLOCK), lambda j: (0, j)),
            whole(times[0].shape),
            whole(times[1].shape),
            whole(spaces[0].shape),
            whole(spaces[1].shape),
        ],
        out_specs=[whole((tokens, D)), whole((tokens, D)), spec],
        out_shape=[
            jax.ShapeDtypeStruct((tokens, D), jnp.float32),
            jax.ShapeDtypeStruct((tokens, D), low_type),
            jax.ShapeDtypeStruct(shape, low_type),
        ],
        compiler_params=pltpu.CompilerParams(vmem_limit_bytes=40 * 1024 * 1024),
        cost_estimate=about(12),
        name="triple_heads",
    )(inputs, weight, mods, weight, *times, *spaces)


def triple_back_kernel(
    grads_ref,
    weight_ref,
    hidden_ref,
    grad_one_ref,
    mods_ref,
    inputs_ref,
    grad_mods_ref,
    grad_patch_ref,
    sum_ref,
):
    step = pl.program_id(0)
    frames = mods_ref.shape[0]
    pieces = range(grads_ref.shape[0])
    if len(grads_ref.shape) == 3:
        grads = jnp.concatenate([grads_ref[piece] for piece in pieces], axis=1)
    else:
        grads = jnp.concatenate([grads_ref[piece, 0] for piece in pieces], axis=1)
    part = against(grads, weight_ref[...])

    @pl.when(step == 0)
    def _():
        sum_ref[...] = part

    @pl.when(step > 0)
    def _():
        sum_ref[...] += part

    @pl.when(step == pl.num_programs(0) - 1)
    def _():
        grad_patch = jnp.zeros((D, PATCH_FEAT), jnp.float32)
        for frame in range(frames):
            tokens = slice(frame * FRAME_TOK, (frame + 1) * FRAME_TOK)
            normed, inverse = norm_parts(hidden_ref[tokens])
            grad_normed = sum_ref[tokens]
            grad_mods_ref[frame, 0:1] = row_sum(grad_normed)
            grad_mods_ref[frame, 1:2] = row_sum(grad_normed * normed)
            grad_hidden = grad_one_ref[tokens] + norm_back(
                normed, inverse, grad_normed * (1.0 + mods_ref[frame, 1:2])
            )
            grad_patch += across(grad_hidden.astype(low_type), inputs_ref[tokens])
        grad_patch_ref[...] = grad_patch


def triple_back(grads, weight, hidden, grad_one, mods, inputs, groups):
    tokens = inputs.shape[0]
    frames = mods.shape[0]
    return pl.pallas_call(
        triple_back_kernel,
        grid=(3 * D // BLOCK,),
        in_specs=[
            heads_layout(groups, tokens)[1],
            pl.BlockSpec((D, BLOCK), lambda j: (0, j)),
            whole(hidden.shape),
            whole(hidden.shape),
            whole(mods.shape),
            whole(inputs.shape),
        ],
        out_specs=[whole((frames, 2, D)), whole((D, PATCH_FEAT))],
        out_shape=[
            jax.ShapeDtypeStruct((frames, 2, D), jnp.float32),
            jax.ShapeDtypeStruct((D, PATCH_FEAT), jnp.float32),
        ],
        scratch_shapes=[pltpu.VMEM((tokens, D), jnp.float32)],
        compiler_params=pltpu.CompilerParams(vmem_limit_bytes=40 * 1024 * 1024),
        cost_estimate=about(12),
        name="triple_back",
    )(grads, weight, hidden, grad_one, mods, inputs)


def head_stack(value):
    count = value.shape[1] // HEAD_DIM
    if count == 1:
        return value
    lane = lax.broadcasted_iota(jnp.int32, value.shape, 1)
    zero = jnp.zeros_like(value)
    return jnp.concatenate(
        [jnp.where(lane // HEAD_DIM == head, value, zero) for head in range(count)], axis=0
    )


UNROLL = 4


def unrolled(count, body, carry):
    def several(base, now):
        for offset in range(UNROLL):
            now = body(base * UNROLL + offset, now)
        return now

    whole_part = count // UNROLL
    carry = lax.fori_loop(0, whole_part, several, carry)
    return lax.fori_loop(whole_part * UNROLL, count, body, carry)


def attend_kernel(
    order_ref,
    count_ref,
    query_ref,
    key_ref,
    value_ref,
    out_ref,
    flat_ref,
    log_ref,
    turned_ref,
    scores_ref,
):
    step = pl.program_id(0)
    chunks, per_chunk = key_ref.shape[0], key_ref.shape[1]
    width = key_ref.shape[-1]
    heads = width // HEAD_DIM
    span = heads * FRAME_TOK

    @pl.when(step == 0)
    def _():
        def turn(chunk, carry):
            for part in range(per_chunk):
                turned_ref[chunk, part] = jnp.transpose(value_ref[chunk, part])
            return carry

        lax.fori_loop(0, chunks, turn, 0)

    queries = jnp.transpose(head_stack(query_ref[...] * jnp.asarray(HEAD_DIM**-0.5, low_type)))
    count = count_ref[step]

    def by_eight(value):
        return value.reshape(FRAME_TOK // 8, 8, span)

    def score(place, top):
        frame = order_ref[place]
        scores = product(key_ref[frame // per_chunk, frame % per_chunk], queries)
        scores_ref[place] = scores
        return jnp.maximum(top, jnp.max(by_eight(scores), axis=0))

    top = unrolled(count, score, jnp.full((8, span), -1e30, jnp.float32))
    top = jnp.max(top, axis=0, keepdims=True)

    def weigh(place, carry):
        total, sums = carry
        frame = order_ref[place]
        chances = jnp.exp(scores_ref[place] - top)
        total = total + jnp.sum(by_eight(chances), axis=0)
        chances = chances.astype(low_type)
        new_sums = []
        for head in range(heads):
            values = turned_ref[
                frame // per_chunk,
                frame % per_chunk,
                head * HEAD_DIM : (head + 1) * HEAD_DIM,
                :,
            ]
            columns = slice(head * FRAME_TOK, (head + 1) * FRAME_TOK)
            new_sums.append(sums[head] + product(values, chances[:, columns]))
        return total, tuple(new_sums)

    initial = (
        jnp.zeros((8, span), jnp.float32),
        tuple(jnp.zeros((HEAD_DIM, FRAME_TOK), jnp.float32) for _ in range(heads)),
    )
    total, sums = unrolled(count, weigh, initial)
    total = jnp.sum(total, axis=0, keepdims=True)
    log_ref[...] = top + jnp.log(total)
    inverse = 1.0 / total
    result = jnp.concatenate(
        [
            sums[head] * inverse[:, head * FRAME_TOK : (head + 1) * FRAME_TOK]
            for head in range(heads)
        ],
        axis=0,
    )
    flat_ref[...] = result
    out_ref[...] = jnp.transpose(result).astype(low_type)


def about(microseconds):
    return pl.CostEstimate(
        flops=microseconds * 1_100_000_000, bytes_accessed=1 << 20, transcendentals=0
    )


def whole(shape):
    return pl.BlockSpec(shape, lambda *_: (0,) * len(shape))


def lanes_of(items, width):
    joint = items[0].shape[-1] != width
    return [place if joint else 0 for place in range(3)]


def attend(order, count, items, width):
    chunks, per_chunk = items[0].shape[:2]
    key_chunks = items[1].shape[0]
    frames = chunks * per_chunk
    span = width // HEAD_DIM * FRAME_TOK
    lane = lanes_of(items, width)
    return pl.pallas_call(
        attend_kernel,
        grid_spec=pltpu.PrefetchScalarGridSpec(
            num_scalar_prefetch=2,
            grid=(frames,),
            in_specs=[
                pl.BlockSpec(
                    (None, None, FRAME_TOK, width),
                    lambda i, *_: (i // per_chunk, i % per_chunk, 0, lane[0]),
                ),
                pl.BlockSpec(
                    (key_chunks, per_chunk, FRAME_TOK, width), lambda i, *_: (0, 0, 0, lane[1])
                ),
                pl.BlockSpec(
                    (key_chunks, per_chunk, FRAME_TOK, width), lambda i, *_: (0, 0, 0, lane[2])
                ),
            ],
            out_specs=[
                pl.BlockSpec(
                    (None, None, FRAME_TOK, width),
                    lambda i, *_: (i // per_chunk, i % per_chunk, 0, 0),
                ),
                pl.BlockSpec((None, width, FRAME_TOK), lambda i, *_: (i, 0, 0)),
                pl.BlockSpec((None, 1, span), lambda i, *_: (i, 0, 0)),
            ],
            scratch_shapes=[
                pltpu.VMEM((key_chunks, per_chunk, width, FRAME_TOK), low_type),
                pltpu.VMEM((key_chunks * per_chunk, FRAME_TOK, span), jnp.float32),
            ],
        ),
        out_shape=[
            jax.ShapeDtypeStruct((chunks, per_chunk, FRAME_TOK, width), low_type),
            jax.ShapeDtypeStruct((frames, width, FRAME_TOK), jnp.float32),
            jax.ShapeDtypeStruct((frames, 1, span), jnp.float32),
        ],
        compiler_params=pltpu.CompilerParams(vmem_limit_bytes=48 * 1024 * 1024),
        cost_estimate=about(45),
        name="attend",
    )(order, count, *items)


def attend_back_kernel(
    order_ref,
    count_ref,
    query_ref,
    key_ref,
    value_ref,
    grad_ref,
    flat_ref,
    log_ref,
    query_cos,
    query_sin,
    key_cos,
    key_sin,
    space_cos,
    space_sin,
    *rest,
):
    outs, (stacked_query, stacked_grad, row_dot, sums_ref) = rest[:-4], rest[-4:]
    step = pl.program_id(0)
    frames, width, _ = flat_ref.shape
    per_chunk = query_ref.shape[1]
    heads = width // HEAD_DIM
    scale = HEAD_DIM**-0.5

    @pl.when(step == 0)
    def _():
        def ready(frame, carry):
            chunk, part = frame // per_chunk, frame % per_chunk
            query = query_ref[chunk, part] * jnp.asarray(scale, low_type)
            stacked_query[frame] = head_stack(query)
            grad = grad_ref[chunk, part]
            stacked_grad[frame] = head_stack(grad)
            both = jnp.transpose(grad.astype(jnp.float32)) * flat_ref[frame]
            row_dot[frame] = jnp.concatenate(
                [
                    jnp.sum(both[head * HEAD_DIM : (head + 1) * HEAD_DIM], axis=0, keepdims=True)
                    for head in range(heads)
                ],
                axis=1,
            )
            sums_ref[frame] = jnp.zeros((width, FRAME_TOK), jnp.float32)
            return carry

        lax.fori_loop(0, frames, ready, 0)

    keys = key_ref[...]
    values = value_ref[...]
    turned_keys = jnp.transpose(keys)

    def several(base, count, carry):
        grad_keys, grad_values = carry
        frames_now = [order_ref[base + i] for i in range(count)]
        updates = []
        scores = [against(keys, stacked_query[frame]) for frame in frames_now]
        grad_chances = [against(values, stacked_grad[frame]) for frame in frames_now]
        for frame, score, grad_chance in zip(frames_now, scores, grad_chances):
            chances = jnp.exp(score - log_ref[frame])
            grad_scores = (chances * (grad_chance - row_dot[frame])).astype(low_type)
            grad_values = grad_values + product(chances.astype(low_type), stacked_grad[frame])
            grad_keys = grad_keys + product(grad_scores, stacked_query[frame])
            for head in range(heads):
                rows = slice(head * HEAD_DIM, (head + 1) * HEAD_DIM)
                updates.append(
                    product(
                        turned_keys[rows],
                        grad_scores[:, head * FRAME_TOK : (head + 1) * FRAME_TOK],
                    )
                )
        for i, frame in enumerate(frames_now):
            for head in range(heads):
                rows = slice(head * HEAD_DIM, (head + 1) * HEAD_DIM)
                sums_ref[frame, rows, :] += updates[i * heads + head]
        return grad_keys, grad_values

    zero = jnp.zeros((FRAME_TOK, width), jnp.float32)
    total = count_ref[step]
    carry = lax.fori_loop(
        0, total // UNROLL, lambda i, c: several(i * UNROLL, UNROLL, c), (zero, zero)
    )
    grad_keys, grad_values = lax.fori_loop(
        total // UNROLL * UNROLL, total, lambda i, c: several(i, 1, c), carry
    )
    space_c, space_s = space_cos[:, :width], space_sin[:, :width]

    def store(part, frame, value):
        place = (frame // per_chunk, frame % per_chunk)
        if len(outs) == 1:
            outs[0][place + (slice(None), slice(part * width, (part + 1) * width))] = value
        else:
            outs[part][place] = value

    store(2, step, grad_values.astype(low_type))
    store(
        1,
        step,
        (
            grad_keys * (key_cos[:, :width] + space_c)
            - partner(grad_keys) * (key_sin[:, :width] + space_s)
        ).astype(low_type),
    )

    @pl.when(step == pl.num_programs(0) - 1)
    def _():
        def finish(frame, carry):
            value = jnp.transpose(sums_ref[frame]) * scale
            store(
                0,
                frame,
                (
                    value * (query_cos[frame][:, :width] + space_c)
                    - partner(value) * (query_sin[frame][:, :width] + space_s)
                ).astype(low_type),
            )
            return carry

        lax.fori_loop(0, frames, finish, 0)


def attend_back(order, count, items, grads, flat, logs, query_times, key_times, spaces):
    per_chunk, width = grads.shape[1], grads.shape[3]
    frames = flat.shape[0]
    key_frames = items[1].shape[0] * per_chunk
    span = width // HEAD_DIM * FRAME_TOK
    lane = lanes_of(items, width)

    def key_spec(place):
        return pl.BlockSpec(
            (None, None, FRAME_TOK, width), lambda i, *_: (i // per_chunk, i % per_chunk, 0, place)
        )

    key_time = pl.BlockSpec((None, 1, LANES), lambda i, *_: (i, 0, 0))
    if lane[1]:
        shapes = [items[0].shape]
    else:
        shapes = [item.shape for item in items]
    return pl.pallas_call(
        attend_back_kernel,
        grid_spec=pltpu.PrefetchScalarGridSpec(
            num_scalar_prefetch=2,
            grid=(key_frames,),
            in_specs=[
                whole(grads.shape),
                key_spec(lane[1]),
                key_spec(lane[2]),
                whole(grads.shape),
                whole(flat.shape),
                whole(logs.shape),
                whole(query_times[0].shape),
                whole(query_times[1].shape),
                key_time,
                key_time,
                whole(spaces[0].shape),
                whole(spaces[1].shape),
            ],
            out_specs=[whole(shape) for shape in shapes],
            scratch_shapes=[
                pltpu.VMEM((frames, span, width), low_type),
                pltpu.VMEM((frames, span, width), low_type),
                pltpu.VMEM((frames, 1, span), jnp.float32),
                pltpu.VMEM((frames, width, FRAME_TOK), jnp.float32),
            ],
        ),
        out_shape=[jax.ShapeDtypeStruct(shape, low_type) for shape in shapes],
        compiler_params=pltpu.CompilerParams(vmem_limit_bytes=56 * 1024 * 1024),
        cost_estimate=about(65),
        name="attend_back",
    )(order, count, *items, grads, flat, logs, *query_times, *key_times, *spaces)


def flat_weight(ref):
    return ref[...].reshape(-1, ref.shape[-1])


def project_kernel(
    heads_ref, weight_ref, hidden_ref, mods_ref, attended_ref, branch_ref, next_ref, mixed_ref
):
    attended = jnp.concatenate([heads_ref[group] for group in range(heads_ref.shape[0])], axis=1)
    attended_ref[...] = attended
    branch = product(attended, flat_weight(weight_ref))
    branch_ref[...] = branch
    hidden = hidden_ref[...] + mods_ref[2:3] * branch
    next_ref[...] = hidden
    normed, _ = norm_parts(hidden)
    mixed_ref[...] = (normed * (1.0 + mods_ref[4:5]) + mods_ref[3:4]).astype(low_type)


def project_norm(heads, weights, hidden, mods):
    groups, tokens, width = heads.shape
    devices, height, _ = weights.shape
    rows = D // devices
    by_frame = pl.BlockSpec((FRAME_TOK, D), lambda i: (i, 0))
    wide = jax.ShapeDtypeStruct((tokens, D), jnp.float32)
    low = jax.ShapeDtypeStruct((tokens, D), low_type)
    return pl.pallas_call(
        project_kernel,
        grid=(tokens // FRAME_TOK,),
        in_specs=[
            pl.BlockSpec((groups, FRAME_TOK, width), lambda i: (0, i, 0)),
            pl.BlockSpec((devices, rows, D), lambda i: (0, FF // D, 0)),
            by_frame,
            pl.BlockSpec((None, 6, D), lambda i: (i, 0, 0)),
        ],
        out_specs=[by_frame] * 4,
        out_shape=[low, wide, wide, low],
        compiler_params=pltpu.CompilerParams(vmem_limit_bytes=60 * 1024 * 1024),
        cost_estimate=about(4),
        name="project_norm",
    )(heads, weights, hidden, mods)


GELU_OUT = math.sqrt(2.0 / math.pi)
GELU_CUBE = 0.044715


def forward_kernel(
    scale_ref,
    mixed_ref,
    expand_ref,
    reduce_ref,
    hidden_ref,
    mods_ref,
    readout_ref,
    noise_ref,
    inner_ref,
    active_ref,
    grad_hidden_ref,
    grad_outer_ref,
    grad_readout_ref,
    grad_gate_ref,
    loss_ref,
    outer_ref,
):
    step = pl.program_id(0)
    frames = mods_ref.shape[0]
    inner = product(mixed_ref[...], flat_weight(expand_ref))
    inner_ref[...] = inner
    bend = jnp.tanh(GELU_OUT * (inner + GELU_CUBE * (inner * inner * inner)))
    active = (0.5 * inner * (1.0 + bend)).astype(low_type)
    active_ref[...] = active
    part = product(active, flat_weight(reduce_ref))

    @pl.when(step == 0)
    def _():
        outer_ref[...] = part

    @pl.when(step > 0)
    def _():
        outer_ref[...] += part

    @pl.when(step == pl.num_programs(0) - 1)
    def _():
        readout = readout_ref[...][:, PATCH_FEAT : 2 * PATCH_FEAT]
        grad_readout = jnp.zeros((D, PATCH_FEAT), jnp.float32)
        for frame in range(frames):
            tokens = slice(frame * FRAME_TOK, (frame + 1) * FRAME_TOK)
            outer = outer_ref[tokens]
            gate = mods_ref[frame, 5:6]
            final, inverse = norm_parts(hidden_ref[tokens] + gate * outer)
            final_low = final.astype(low_type)
            residue = product(final_low, readout) - noise_ref[tokens]
            loss_ref[frame] = jnp.zeros((1, LANES), jnp.float32) + jnp.sum(residue * residue)
            grad_pred = (residue * scale_ref[frame]).astype(low_type)
            grad_readout += across(final_low, grad_pred)
            grad_hidden = norm_back(final, inverse, against(grad_pred, readout))
            grad_hidden_ref[tokens] = grad_hidden
            grad_outer_ref[tokens] = (gate * grad_hidden).astype(low_type)
            grad_gate_ref[frame] = row_sum(grad_hidden * outer)
        grad_readout_ref[...] = grad_readout


def feed_forward(loss_scale, mixed, weights, hidden, mods, first_weights, noise):
    tokens = mixed.shape[0]
    devices, height, _ = weights.shape
    rows = D // devices
    frames = mods.shape[0]
    pieces = FF // D
    wide = jax.ShapeDtypeStruct((tokens, D), jnp.float32)
    by_piece = pl.BlockSpec((tokens, D), lambda k, *_: (0, k))
    return pl.pallas_call(
        forward_kernel,
        grid_spec=pltpu.PrefetchScalarGridSpec(
            num_scalar_prefetch=1,
            grid=(pieces,),
            in_specs=[
                whole((tokens, D)),
                pl.BlockSpec((devices, rows, D), lambda k, *_: (0, pieces + 1 + k, 0)),
                pl.BlockSpec((devices // pieces, pieces * rows, D), lambda k, *_: (k, 0, 0)),
                whole((tokens, D)),
                whole(mods.shape),
                pl.BlockSpec((D, LANES), lambda k, *_: (0, 3 * D // LANES)),
                whole((tokens, PATCH_FEAT)),
            ],
            out_specs=[
                by_piece,
                by_piece,
                whole((tokens, D)),
                whole((tokens, D)),
                whole((D, PATCH_FEAT)),
                whole((frames, 1, D)),
                whole((frames, 1, LANES)),
            ],
            scratch_shapes=[pltpu.VMEM((tokens, D), jnp.float32)],
        ),
        out_shape=[
            jax.ShapeDtypeStruct((tokens, FF), jnp.float32),
            jax.ShapeDtypeStruct((tokens, FF), low_type),
            wide,
            jax.ShapeDtypeStruct((tokens, D), low_type),
            jax.ShapeDtypeStruct((D, PATCH_FEAT), jnp.float32),
            jax.ShapeDtypeStruct((frames, 1, D), jnp.float32),
            jax.ShapeDtypeStruct((frames, 1, LANES), jnp.float32),
        ],
        compiler_params=pltpu.CompilerParams(vmem_limit_bytes=60 * 1024 * 1024),
        cost_estimate=about(20),
        name="feed_forward",
    )(loss_scale, mixed, weights, weights, hidden, mods, first_weights, noise)


def backward_kernel(
    grad_outer_ref,
    reduce_ref,
    expand_ref,
    inner_ref,
    hidden_ref,
    grad_hidden_ref,
    branch_ref,
    mods_ref,
    project_ref,
    grad_inner_ref,
    grad_one_ref,
    grad_branch_ref,
    heads_ref,
    grad_mods_ref,
    grad_mixed_ref,
):
    step = pl.program_id(0)
    frames = mods_ref.shape[0]
    groups, _, width = heads_ref.shape
    inner = inner_ref[...]
    square = inner * inner
    bend = jnp.tanh(GELU_OUT * (inner + GELU_CUBE * (square * inner)))
    slope = 0.5 * (1.0 + bend) + 0.5 * inner * (1.0 - bend * bend) * (
        GELU_OUT * (1.0 + 3.0 * GELU_CUBE * square)
    )
    grad_active = against(grad_outer_ref[...], flat_weight(reduce_ref))
    grad_inner = (grad_active * slope).astype(low_type)
    grad_inner_ref[...] = grad_inner
    part = against(grad_inner, flat_weight(expand_ref))

    @pl.when(step == 0)
    def _():
        grad_mixed_ref[...] = part

    @pl.when(step > 0)
    def _():
        grad_mixed_ref[...] += part

    @pl.when(step == pl.num_programs(0) - 1)
    def _():
        project = flat_weight(project_ref)
        for frame in range(frames):
            tokens = slice(frame * FRAME_TOK, (frame + 1) * FRAME_TOK)
            normed, inverse = norm_parts(hidden_ref[tokens])
            grad_mixed = grad_mixed_ref[tokens]
            grad_mods_ref[frame, 1:2] = row_sum(grad_mixed)
            grad_mods_ref[frame, 2:3] = row_sum(grad_mixed * normed)
            grad_one = grad_hidden_ref[tokens] + norm_back(
                normed, inverse, grad_mixed * (1.0 + mods_ref[frame, 4:5])
            )
            grad_one_ref[tokens] = grad_one
            grad_mods_ref[frame, 0:1] = row_sum(grad_one * branch_ref[tokens])
            grad_branch = (mods_ref[frame, 2:3] * grad_one).astype(low_type)
            grad_branch_ref[tokens] = grad_branch
            grad_attended = against(grad_branch, project).astype(low_type)
            for group in range(groups):
                heads_ref[group, tokens] = grad_attended[:, group * width : (group + 1) * width]


def feed_backward(grad_outer, weights, inner, hidden, grad_hidden, branch, mods, groups):
    tokens = hidden.shape[0]
    devices, height, _ = weights.shape
    rows = D // devices
    frames = mods.shape[0]
    pieces = FF // D
    by_piece = pl.BlockSpec((tokens, D), lambda k: (0, k))
    return pl.pallas_call(
        backward_kernel,
        grid=(pieces,),
        in_specs=[
            whole((tokens, D)),
            pl.BlockSpec((devices // pieces, pieces * rows, D), lambda k: (k, 0, 0)),
            pl.BlockSpec((devices, rows, D), lambda k: (0, pieces + 1 + k, 0)),
            by_piece,
            whole((tokens, D)),
            whole((tokens, D)),
            whole((tokens, D)),
            whole(mods.shape),
            pl.BlockSpec((devices, rows, D), lambda k: (0, pieces, 0)),
        ],
        out_specs=[
            by_piece,
            whole((tokens, D)),
            whole((tokens, D)),
            whole((groups, tokens, D // groups)),
            whole((frames, 3, D)),
        ],
        out_shape=[
            jax.ShapeDtypeStruct((tokens, FF), low_type),
            jax.ShapeDtypeStruct((tokens, D), jnp.float32),
            jax.ShapeDtypeStruct((tokens, D), low_type),
            jax.ShapeDtypeStruct((groups, tokens, D // groups), low_type),
            jax.ShapeDtypeStruct((frames, 3, D), jnp.float32),
        ],
        scratch_shapes=[pltpu.VMEM((tokens, D), jnp.float32)],
        compiler_params=pltpu.CompilerParams(vmem_limit_bytes=60 * 1024 * 1024),
        cost_estimate=about(22),
        name="feed_backward",
    )(grad_outer, weights, weights, inner, hidden, grad_hidden, branch, mods, weights)


def grads_kernel(
    active_ref, grad_outer_ref, attended_ref, grad_branch_ref, mixed_ref, grad_inner_ref, out_ref
):
    cores, lines, height, _ = out_ref.shape
    pieces = FF // D
    rows = height // (2 * pieces + 1)

    def store(start, count, value):
        value = value.astype(low_type)
        for line in range(lines):
            for core in range(cores):
                at = (line * cores + core) * count
                out_ref[core, line, start : start + count] = value[at : at + count]

    store(0, pieces * rows, across(active_ref[...], grad_outer_ref[...]))
    store(pieces * rows, rows, across(attended_ref[...], grad_branch_ref[...]))
    for piece in range(pieces):
        store(
            (pieces + 1 + piece) * rows,
            rows,
            across(mixed_ref[...], grad_inner_ref[:, piece * D : (piece + 1) * D]),
        )


def weight_grads(sizes, active, grad_outer, attended, grad_branch, mixed, grad_inner):
    batch, row, core = sizes
    tokens = mixed.shape[0]
    rows = D // (batch * row * core)
    height = rows * (2 * (FF // D) + 1)
    part = pl.BlockSpec((tokens, D // batch), lambda i: (0, i))
    return pl.pallas_call(
        grads_kernel,
        grid=(batch,),
        in_specs=[
            pl.BlockSpec((tokens, FF // batch), lambda i: (0, i)),
            whole((tokens, D)),
            part,
            whole((tokens, D)),
            part,
            whole((tokens, FF)),
        ],
        out_specs=pl.BlockSpec((None, core, row, height, D), lambda i: (i, 0, 0, 0, 0)),
        out_shape=jax.ShapeDtypeStruct((batch, core, row, height, D), low_type),
        compiler_params=pltpu.CompilerParams(vmem_limit_bytes=56 * 1024 * 1024),
        cost_estimate=about(28),
        name="weight_grads",
    )(active, grad_outer, attended, grad_branch, mixed, grad_inner)


def update_kernel(rates, squares_ref, *refs):
    factor = jnp.minimum(1.0, clip_bound / jnp.sqrt(squares_ref[...]))
    for item, rate in enumerate(rates):
        master, first, second, gradient = (refs[4 * item + part][...] for part in range(4))
        new = adamw_update(master, first, second, gradient, factor, rate)
        for part in range(3):
            refs[4 * len(rates) + 3 * item + part][...] = new[part]


def update(squares, states, rates):
    flat = [array for state in states for array in state]
    steps = 4
    specs = [
        pl.BlockSpec((array.shape[0], array.shape[1] // steps), lambda i: (0, i))
        for array in flat
    ]
    outs = [4 * item + part for item in range(len(states)) for part in (1, 2, 0)]
    new = pl.pallas_call(
        functools.partial(update_kernel, rates),
        grid=(steps,),
        in_specs=[whole((1, 1))] + specs,
        out_specs=[specs[out] for out in outs],
        out_shape=[jax.ShapeDtypeStruct(flat[out].shape, jnp.float32) for out in outs],
        compiler_params=pltpu.CompilerParams(vmem_limit_bytes=60 * 1024 * 1024),
        cost_estimate=about(7),
        name="update",
    )(squares, *flat)
    return [new[3 * item : 3 * item + 3] for item in range(len(states))]


def swapped(value, axis, offset):
    return lax.ppermute(value, axis, [(i, i ^ offset) for i in range(lax.axis_size(axis))])


def gather_near(value, axes=("core", "batch", "row")):
    for axis in axes:
        others = [swapped(value, axis, offset) for offset in range(1, lax.axis_size(axis))]
        value = jnp.concatenate([value] + others, axis=0)
    return value


def near_owner(index):
    batch, row, core = (lax.axis_size(axis) for axis in ALL)
    places = (
        (index // core % batch) ^ lax.axis_index("batch"),
        (index // (core * batch)) ^ lax.axis_index("row"),
        (index % core) ^ lax.axis_index("core"),
    )
    return (places[0] * row + places[1]) * core + places[2]


def exchange_sum(value, axes, at=0, sent=jnp.float32):
    count = value.shape[at]
    mine = lax.axis_index(axes)
    total = lax.dynamic_index_in_dim(value, mine, at, keepdims=False)
    parts = [
        lax.ppermute(
            lax.dynamic_index_in_dim(value, mine ^ offset, at, keepdims=False).astype(sent),
            axes,
            [(i, i ^ offset) for i in range(count)],
        )
        for offset in range(1, count)
    ]
    for part in parts:
        total = total + part.astype(jnp.float32)
    return total


def total_sum(value):
    for axis in ("core", "batch", "row"):
        parts = [value] + [
            swapped(value, axis, offset) for offset in range(1, lax.axis_size(axis))
        ]
        while len(parts) > 1:
            parts = [parts[i] + parts[i + 1] for i in range(0, len(parts), 2)]
        value = parts[0]
    return value


def per_device(
    clean_latents,
    noise_sample,
    noise_levels,
    clean_flags,
    span_frame,
    patch_master,
    patch_first,
    patch_second,
    level_master,
    level_first,
    level_second,
    adaptive_master,
    adaptive_first,
    adaptive_second,
    triple_master,
    triple_first,
    triple_second,
    project_master,
    project_first,
    project_second,
    expand_master,
    expand_first,
    expand_second,
    reduce_master,
    reduce_first,
    reduce_second,
    readout_master,
    readout_first,
    readout_second,
):
    masters = (
        patch_master,
        level_master,
        adaptive_master,
        triple_master,
        project_master,
        expand_master,
        reduce_master,
        readout_master,
    )
    firsts = (
        patch_first,
        level_first,
        adaptive_first,
        triple_first,
        project_first,
        expand_first,
        reduce_first,
        readout_first,
    )
    seconds = (
        patch_second,
        level_second,
        adaptive_second,
        triple_second,
        project_second,
        expand_second,
        reduce_second,
        readout_second,
    )
    batch_count, row_count, core_count = (lax.axis_size(axis) for axis in ALL)
    batch_index, row_index, core_index = (lax.axis_index(axis) for axis in ALL)
    devices = batch_count * row_count * core_count
    rows = D // devices
    token_count = clean_latents.shape[1]
    frame_local = token_count // FRAME_TOK

    moved = batch_count == row_count and HEADS % (batch_count * core_count) == 0
    if moved:
        clip_index, chunk_index = row_index, batch_index * core_count + core_index
        head_axes, head_groups = ("batch", "core"), batch_count * core_count
        rest_axes = ("row",)
    else:
        clip_index, chunk_index = batch_index, row_index * core_count + core_index
        head_axes, head_groups = ("row",), row_count
        rest_axes = ("batch", "core")

    both = jnp.concatenate([clean_latents[0], noise_sample[0]], axis=1)
    if moved:
        turn = [
            (
                (a * row_count + b) * core_count + c,
                (b * row_count + a) * core_count + c,
            )
            for a in range(batch_count)
            for b in range(row_count)
            for c in range(core_count)
        ]
        both = lax.ppermute(both, ALL, turn)
    clean_tok, noise_tok = both[:, :PATCH_FEAT], both[:, PATCH_FEAT:]

    first_weights = jnp.concatenate(
        [
            triple_master.astype(low_type),
            jnp.transpose(patch_master).astype(low_type),
            readout_master.astype(low_type),
            jnp.zeros((rows, LANES - 2 * PATCH_FEAT), low_type),
        ],
        axis=1,
    )
    first_weights = lax.all_gather(first_weights, ALL, axis=0, tiled=True)
    second_weights = jnp.concatenate(
        [reduce_master.astype(low_type), project_master.astype(low_type)]
        + [expand_master[:, k * D : (k + 1) * D].astype(low_type) for k in range(FF // D)],
        axis=0,
    )
    second_weights = lax.all_gather(second_weights, ALL, axis=0)

    levels_all = noise_levels.reshape(-1)
    flags_all = clean_flags.reshape(-1)
    _, _, index_all = plan(levels_all, flags_all)
    if moved:
        order_all = lambda v: (
            v.reshape((row_count, batch_count, core_count, frame_local) + v.shape[1:])
            .swapaxes(0, 1)
            .reshape(v.shape)
        )
    else:
        order_all = lambda v: v
    index_all = order_all(index_all)
    every = jnp.arange(devices, dtype=jnp.int32)
    index_near = jnp.sum(
        jnp.where(
            (near_owner(every)[:, None] == every[None, :])[..., None],
            index_all.reshape(1, devices, frame_local),
            0,
        ),
        axis=1,
    ).reshape(-1)
    table_low = level_master.astype(low_type).astype(jnp.float32)

    def table_rows(index):
        hot = (index[:, None] == jnp.arange(NB + 1, dtype=jnp.int32)[None, :]).astype(jnp.float32)
        return hot, jnp.dot(hot, table_low, precision=lax.Precision.HIGHEST)

    _, pre_own = table_rows(index_all)
    hot_near, pre_near = table_rows(index_near)
    cond_near, silu_back = jax.vjp(jax.nn.silu, pre_near)
    cond_near = cond_near.astype(low_type)
    cond_own = jax.nn.silu(pre_own).astype(low_type)
    adaptive_low = adaptive_master.astype(low_type)
    adapt = product(cond_own, adaptive_low).reshape(devices, frame_local, 6 * D)
    mods = jnp.sum(lax.all_to_all(adapt, ALL, 0, 0, tiled=True), axis=0)
    mods = mods.reshape(frame_local, 6, D)

    my_levels = lax.dynamic_slice_in_dim(
        lax.dynamic_index_in_dim(noise_levels, clip_index, 0, keepdims=False),
        chunk_index * frame_local,
        frame_local,
    )
    my_flags = lax.dynamic_slice_in_dim(
        lax.dynamic_index_in_dim(clean_flags, clip_index, 0, keepdims=False),
        chunk_index * frame_local,
        frame_local,
    )
    my_frames = lax.dynamic_slice_in_dim(span_frame, chunk_index * frame_local, frame_local)
    if moved:
        query_frames = key_frames = span_frame
    else:
        by_chunk = span_frame.reshape(row_count, core_count, frame_local)
        query_frames = lax.dynamic_index_in_dim(by_chunk, core_index, 1, keepdims=False).reshape(-1)
        key_frames = by_chunk.swapaxes(0, 1).reshape(-1)
    query_total, key_total = query_frames.shape[0], key_frames.shape[0]
    earlier = jnp.sum(key_frames[None, :] < key_frames[:, None], axis=1)
    key_order = jnp.sum(
        jnp.where(earlier[:, None] == jnp.arange(key_total)[None, :], jnp.arange(key_total)[:, None], 0),
        axis=0,
    ).astype(jnp.int32)
    key_count = jnp.sum(key_frames[None, :] <= query_frames[:, None], axis=1).astype(jnp.int32)
    later = jnp.sum(query_frames[None, :] > query_frames[:, None], axis=1)
    query_order = jnp.sum(
        jnp.where(later[:, None] == jnp.arange(query_total)[None, :], jnp.arange(query_total)[:, None], 0),
        axis=0,
    ).astype(jnp.int32)
    query_count = jnp.sum(query_frames[None, :] >= key_frames[:, None], axis=1).astype(jnp.int32)
    my_times, query_times, key_times = (
        time_tables(my_frames),
        time_tables(query_frames),
        time_tables(key_frames),
    )
    spaces = space_tables()

    alpha_bar, noised, _ = plan(my_levels, my_flags)
    inputs = noised_input(clean_tok, noise_tok, alpha_bar, noised).astype(low_type)
    width = D // head_groups
    hidden_zero, normed_low, heads = triple_heads(
        inputs, mods, first_weights, my_times, spaces, head_groups
    )
    heads = lax.all_to_all(heads, head_axes, 0, 0, tiled=True)
    if moved:
        heads = heads.reshape(head_groups, frame_local, FRAME_TOK, 3 * width)
        items = (heads, heads, heads)
    else:
        heads = heads.reshape(head_groups, 3, frame_local, FRAME_TOK, width)
        items = (heads[:, 0],) + tuple(
            lax.all_gather(heads[:, part], "core", axis=0, tiled=True) for part in (1, 2)
        )
    attended, flat, logs = attend(key_order, key_count, items, width)
    attended = attended.reshape(head_groups, token_count, width)
    attended = lax.all_to_all(attended, head_axes, 0, 0, tiled=True)
    attended, normed_low = lax.optimization_barrier((attended, normed_low))
    normed_clip = lax.all_gather(normed_low, head_axes, axis=0, tiled=True)
    attended_low, branch, hidden_one, mixed_low = project_norm(
        attended, second_weights, hidden_zero, mods
    )
    frame_count = jnp.sum((1 - clean_flags).astype(jnp.float32))
    loss_scale = noised * (2.0 / (FRAME_TOK * PATCH_FEAT)) / jnp.maximum(frame_count, 1.0)
    (
        inner,
        active_low,
        grad_hidden_two,
        grad_outer,
        grad_readout,
        grad_gate_two,
        squared,
    ) = feed_forward(
        loss_scale, mixed_low, second_weights, hidden_one, mods, first_weights, noise_tok
    )
    frame_loss = squared[:, 0, 0] * (1.0 / (FRAME_TOK * PATCH_FEAT)) * noised
    grad_inner_low, grad_hidden_one, grad_branch, grad_attended, grad_mods = feed_backward(
        grad_outer,
        second_weights,
        inner,
        hidden_one,
        grad_hidden_two,
        branch,
        mods,
        head_groups,
    )
    grad_attended = lax.all_to_all(grad_attended, head_axes, 0, 0, tiled=True)
    grad_attended = grad_attended.reshape(head_groups, frame_local, FRAME_TOK, width)
    early_adapt = jnp.concatenate(
        [grad_mods.reshape(frame_local, 3 * D), grad_gate_two.reshape(frame_local, D)], axis=1
    ).astype(low_type)
    early_adapt = gather_near(early_adapt, ("core", "batch"))
    grad_attended, early_adapt = lax.optimization_barrier((grad_attended, early_adapt))
    early_adapt = gather_near(early_adapt, ("row",))

    second_grads = weight_grads(
        (batch_count, row_count, core_count),
        active_low,
        grad_outer,
        attended_low,
        grad_branch,
        mixed_low,
        grad_inner_low,
    )
    second_own = lax.psum_scatter(
        second_grads.reshape((-1,) + second_grads.shape[2:]),
        ("batch", "core"),
        scatter_dimension=0,
    )

    grads = attend_back(
        query_order,
        query_count,
        items,
        grad_attended,
        flat,
        logs,
        query_times,
        key_times,
        spaces,
    )
    if moved:
        grad_heads = grads[0].reshape(head_groups, token_count, 3 * width)
    else:
        grad_heads = [grads[0]] + [
            lax.psum_scatter(
                item.astype(jnp.float32), "core", scatter_dimension=0, tiled=True
            ).astype(low_type)
            for item in grads[1:]
        ]
        grad_heads = jnp.concatenate(grad_heads, axis=-1).reshape(
            head_groups, token_count, 3 * width
        )
    grad_triple = across(
        normed_clip.reshape(-1, D), grad_heads.reshape(head_groups * token_count, 3 * width)
    )
    grad_heads = lax.all_to_all(grad_heads, head_axes, 0, 0, tiled=True)
    if not moved:
        grad_heads = grad_heads.reshape(head_groups, token_count, 3, width).swapaxes(1, 2)
    grad_triple = grad_triple.reshape(batch_count, row_count, core_count, rows, 3 * width)
    if moved:
        grad_triple = grad_triple.transpose(1, 0, 2, 3, 4)
    else:
        grad_triple = grad_triple.transpose(0, 2, 1, 3, 4)
    rest_count = devices // head_groups
    triple_own = exchange_sum(
        grad_triple.reshape(rest_count, head_groups, rows, 3 * width),
        rest_axes,
        sent=low_type,
    )
    grad_heads, triple_own, early_adapt = lax.optimization_barrier(
        (grad_heads, triple_own, early_adapt)
    )
    grad_shift, grad_patch = triple_back(
        grad_heads, first_weights, hidden_zero, grad_hidden_one, mods, inputs, head_groups
    )
    second_own, grad_shift = lax.optimization_barrier((second_own, grad_shift))
    second_own = lax.psum_scatter(second_own, "row", scatter_dimension=0)
    late_adapt = gather_near(grad_shift.reshape(frame_local, 2 * D).astype(low_type))
    small = jnp.concatenate([grad_patch, grad_readout], axis=1)
    small = small.reshape(batch_count, row_count, core_count, -1, LANES)
    small = exchange_sum(small, "core", 2)
    small = exchange_sum(small, "batch")
    small_own = exchange_sum(small, "row").reshape(rows, 2 * PATCH_FEAT)

    triple_own = lax.all_to_all(triple_own, head_axes, 0, 0, tiled=True)
    triple_own = (
        triple_own.reshape(head_groups, rows, 3, width).transpose(1, 2, 0, 3).reshape(rows, 3 * D)
    )
    early_columns = 2 * D
    adapt_own = jnp.concatenate(
        [across(cond_near, late_adapt), across(cond_near, early_adapt)], axis=1
    )
    grad_cond = against(late_adapt, adaptive_low[:, :early_columns]) + against(
        early_adapt, adaptive_low[:, early_columns:]
    )
    (grad_pre,) = silu_back(grad_cond)
    table_own = lax.dot_general(
        hot_near,
        grad_pre,
        (((0,), (0,)), ((), ())),
        precision=lax.Precision.HIGHEST,
        preferred_element_type=jnp.float32,
    )
    squares = sum(
        jnp.sum(gradient * gradient) for gradient in (small_own, table_own, adapt_own, triple_own)
    )
    second_own, squares = lax.optimization_barrier((second_own, squares))
    second_own = second_own.astype(jnp.float32)
    expand_own = jnp.concatenate(
        [
            second_own[(FF // D + 1 + k) * rows : (FF // D + 2 + k) * rows]
            for k in range(FF // D)
        ],
        axis=1,
    )
    reduced = (
        jnp.transpose(small_own[:, :PATCH_FEAT]),
        table_own,
        adapt_own,
        triple_own,
        second_own[FF // D * rows : (FF // D + 1) * rows],
        expand_own,
        second_own[: FF // D * rows],
        small_own[:, PATCH_FEAT:],
    )
    squares = squares + jnp.sum(second_own * second_own)
    lane = jnp.arange(LANES, dtype=jnp.int32)
    bucket_lanes = jnp.sum(
        jnp.where(my_levels[:, None] == lane[None], frame_loss[:, None], 0.0), axis=0
    )
    sums = jnp.stack(
        [bucket_lanes, jnp.full((LANES,), squares), jnp.full((LANES,), jnp.sum(frame_loss))]
    )
    sums = total_sum(sums)
    clip_norm = jnp.sqrt(sums[1, 0])
    factor = jnp.minimum(1.0, clip_bound / clip_norm)
    states = [
        (masters[item], firsts[item], seconds[item], reduced[item]) for item in range(len(reduced))
    ]
    large = (2, 3, 4, 5, 6)
    updated = update(
        sums[1:2, :1], [states[item] for item in large], tuple(learn_rates[item] for item in large)
    )
    new = [
        updated[large.index(item)]
        if item in large
        else adamw_update(*states[item], factor, learn_rates[item])
        for item in range(len(states))
    ]
    return (sums[2, 0], frame_count, sums[0, :NB], clip_norm) + tuple(
        item for triple in new for item in triple
    )


def solution(mesh):
    in_specs = (
        P("batch", ("row", "core"), None),
        P("batch", ("row", "core"), None),
        P(),
        P(),
        P(),
        P(None, ALL),
        P(None, ALL),
        P(None, ALL),
        P(None, ALL),
        P(None, ALL),
        P(None, ALL),
        P(ALL, None),
        P(ALL, None),
        P(ALL, None),
        P(ALL, None),
        P(ALL, None),
        P(ALL, None),
        P(ALL, None),
        P(ALL, None),
        P(ALL, None),
        P(ALL, None),
        P(ALL, None),
        P(ALL, None),
        P(ALL, None),
        P(ALL, None),
        P(ALL, None),
        P(ALL, None),
        P(ALL, None),
        P(ALL, None),
    )
    out_specs = (
        P(),
        P(),
        P(),
        P(),
        P(None, ALL),
        P(None, ALL),
        P(None, ALL),
        P(None, ALL),
        P(None, ALL),
        P(None, ALL),
        P(ALL, None),
        P(ALL, None),
        P(ALL, None),
        P(ALL, None),
        P(ALL, None),
        P(ALL, None),
        P(ALL, None),
        P(ALL, None),
        P(ALL, None),
        P(ALL, None),
        P(ALL, None),
        P(ALL, None),
        P(ALL, None),
        P(ALL, None),
        P(ALL, None),
        P(ALL, None),
        P(ALL, None),
        P(ALL, None),
    )
    batch_size, blk_size = mesh.shape["batch"], mesh.shape["blk"]
    inner = Mesh(mesh.devices.reshape(batch_size, blk_size // 2, 2), ALL)
    return jax.shard_map(
        per_device, mesh=inner, in_specs=in_specs, out_specs=out_specs, check_vma=False
    )
```
